32 devices in a mesh: dp: 4 (over z), emb: 8 (over y, x, core).
Axes of the slice: x: 2, y: 2, z: 4, core: 2. Of those that a mesh axis runs over, the one named last changes fastest.
Arguments:
- pixels: bfloat16 [32768, 768], P(('dp', 'emb')), may hold values from -6 to 6
- counts: int32 [32, 2], P(('dp', 'emb')), may hold values from 0 to 511, as said below
- token_ids: int32 [32768], P(('dp', 'emb')), may hold values from 0 to 31999, as said below
- action_bins: int32 [32768], P(('dp', 'emb')), may hold values from 0 to 1023
- patch_pos: int32 [32768], P(('dp', 'emb')), may hold values from 0 to 255
- token_table: bfloat16 [33024, 768], P('emb'), may hold values from -6 to 6
- pos_table: bfloat16 [256, 768], replicated, may hold values from -4 to 4
- w_patch: bfloat16 [768, 768], replicated, may hold values from -0.21875 to 0.21875
- w_res_a: bfloat16 [768, 768], replicated, may hold values from -0.21875 to 0.21875
- w_res_b: bfloat16 [768, 768], replicated, may hold values from -0.21875 to 0.21875
- gain_one: bfloat16 [768], replicated, may hold values from 0.5 to 1.5
- bias_one: bfloat16 [768], replicated, may hold values from -2 to 2
- w_q: bfloat16 [768, 768], replicated, may hold values from -0.21875 to 0.21875
- w_k: bfloat16 [768, 768], replicated, may hold values from -0.21875 to 0.21875
- w_v: bfloat16 [768, 768], replicated, may hold values from -0.21875 to 0.21875
- w_o: bfloat16 [768, 768], replicated, may hold values from -1 to 1
- gain_two: bfloat16 [768], replicated, may hold values from 0.5 to 1.5
- bias_two: bfloat16 [768], replicated, may hold values from -2 to 2
- w_up: bfloat16 [768, 3072], replicated, may hold values from -0.21875 to 0.21875
- w_down: bfloat16 [3072, 768], replicated, may hold values from -0.109375 to 0.109375
- cotangent: bfloat16 [32768, 768], P(('dp', 'emb')), may hold values from -6 to 6
Outputs:
- output: bfloat16 [32768, 768], P(('dp', 'emb'))
- grad_pixels: float32 [32768, 768], P(('dp', 'emb'))
- grad_table: float32 [33024, 768], P('emb', 'dp')
- grad_pos_table: float32 [256, 768], P(('dp', 'emb'))
- grad_w_patch: float32 [768, 768], P(('dp', 'emb'))
- grad_w_res_a: float32 [768, 768], P(('dp', 'emb'))
- grad_w_res_b: float32 [768, 768], P(('dp', 'emb'))
- grad_gain_one: float32 [768], P(('dp', 'emb'))
- grad_bias_one: float32 [768], P(('dp', 'emb'))
- grad_w_q: float32 [768, 768], P(('dp', 'emb'))
- grad_w_k: float32 [768, 768], P(('dp', 'emb'))
- grad_w_v: float32 [768, 768], P(('dp', 'emb'))
- grad_w_o: float32 [768, 768], P(('dp', 'emb'))
- grad_gain_two: float32 [768], P(('dp', 'emb'))
- grad_bias_two: float32 [768], P(('dp', 'emb'))
- grad_w_up: float32 [768, 3072], P(('dp', 'emb'))
- grad_w_down: float32 [3072, 768], P(('dp', 'emb'))
The draws below stay inside these ranges and needn't reach their ends.
Inputs may be any that keep to these rules, and one draw needn't show every extreme that they name: Sequence s opens with counts[s, 0] image patches and closes with counts[s, 1] actions, 1 to 192 of them; text fills the rest. Some sequence has no patches, some has 511, some has 192 actions. `token_ids`: text ids are under 32000. Of one sequence's text and action tokens (an action's row is 32000 + its bin), at most 192 have rows in one aligned block of 4128 table rows, and in each sequence some block has exactly 192.
All inputs are finite; a program needn't handle non-finite values.
Results may differ from the reference program's by a relative error of at most 0.02.
Values may be sent and summed in bfloat16 or wider, within the bound.
A program may use at most 576 MiB of HBM per device.

```python
import math
import jax
import jax.numpy as jnp
from jax import lax

D = 768
HEADS = 24
HEAD_DIM = 32
FF = 3072
PIX = 768
TEXT_VOCAB = 32000
NBINS = 1024
PATCH_POS = 256
TOK_DEV = 1024
VOCAB = 33024
SEQS = 32
TOKENS = 32768
ROWS_EMB = 4128
CAP = 192


def sequence_counts(key):
    split_keys = jax.random.split(jax.random.fold_in(key, 101), 3)
    images = jax.random.randint(split_keys[0], (SEQS,), 0, TOK_DEV // 2)
    actions = jax.random.randint(split_keys[1], (SEQS,), 1, CAP + 1)
    chosen = jax.random.permutation(split_keys[2], SEQS)
    images = images.at[chosen[0]].set(0).at[chosen[1]].set(TOK_DEV // 2 - 1)
    actions = actions.at[chosen[2]].set(CAP)
    return (images, actions)


def draw_counts(key, part):
    images, actions = sequence_counts(key)
    return jnp.stack([images, actions], 1).astype(jnp.int32)


def arrange_owners(favoured, actions, images, noise):
    owners_total = VOCAB // ROWS_EMB
    pool_size = owners_total * CAP
    slot_index = jnp.arange(pool_size)
    labels = slot_index // CAP
    blocked = (labels == owners_total - 1) & (slot_index < (owners_total - 1) * CAP + actions)
    score = jnp.where(labels == favoured, slot_index, jnp.where(blocked, pool_size + 65536 * pool_size + slot_index, pool_size + noise * pool_size + slot_index))
    order = jnp.argsort(score)
    sorted_labels = labels[order]
    text_rank = jnp.clip(jnp.arange(TOK_DEV) - images, 0, TOK_DEV - 1)
    return sorted_labels[text_rank]


def draw_token_ids(key, part):
    images, actions = sequence_counts(key)
    key = jax.random.fold_in(key, 2)
    split_keys = jax.random.split(key, 3)
    owners_total = VOCAB // ROWS_EMB
    favoured = jax.random.randint(split_keys[0], (SEQS,), 0, owners_total - 1)
    noise = jax.random.randint(split_keys[1], (SEQS, owners_total * CAP), 0, 65536)
    owners = jax.vmap(arrange_owners)(favoured, actions, images, noise)
    limits = jnp.minimum(ROWS_EMB, TEXT_VOCAB - owners * ROWS_EMB)
    offsets = jax.random.randint(split_keys[2], (SEQS, TOK_DEV), 0, 1 << 30) % limits
    row_values = owners * ROWS_EMB + offsets
    row_values = row_values.at[0, TOK_DEV - 1].set(TEXT_VOCAB - 1).at[1, TOK_DEV - 1].set(0)
    return row_values.reshape(TOKENS).astype(jnp.int32)


def place_ends(values, stream_key, least, largest):
    longest = values.shape.index(max(values.shape))
    spots = []
    for shift in (0, 1):
        where = [jax.random.randint(jax.random.fold_in(stream_key, axis), (), 0, length) for axis, length in enumerate(values.shape)]
        where[longest] = (where[longest] + shift) % values.shape[longest]
        spots.append(tuple(where))
    return values.at[spots[0]].set(least).at[spots[1]].set(largest)


def level_of(rng, extent, pieces, least, top_value):
    loudness = 1.0
    for position, shards_of in pieces:
        draws = jax.random.uniform(jax.random.fold_in(jax.random.fold_in(rng, 6), position), (shards_of,), jnp.float32, least / len(pieces), top_value / len(pieces))
        loudness = loudness * jnp.repeat(jnp.exp(draws), extent[position] // shards_of).reshape((-1,) + (1,) * (len(extent) - 1 - position))
    return loudness


def normal_values(stream_key, extent, width, reach, pieces=(), dtype=jnp.bfloat16):
    array = jax.random.normal(stream_key, extent, jnp.float32) * width
    if len(pieces) > 0:
        array = level_of(stream_key, extent, pieces, -0.22, 0.18) * array
    return jnp.clip(array, min=-reach, max=reach).astype(dtype)


def setup_inputs(seed: int = 0) -> dict:
    arg_keys = jax.random.split(jax.random.key(seed), 22)
    pixels = normal_values(arg_keys[0], (TOKENS, PIX), 1.0, 6.0, ((0, 32),))
    counts = draw_counts(jax.random.fold_in(arg_keys[21], 71), 0)
    token_ids = draw_token_ids(jax.random.fold_in(arg_keys[21], 71), 0)
    action_bins = place_ends(jax.random.randint(arg_keys[3], (TOKENS,), 0, NBINS), jax.random.fold_in(arg_keys[3], 1), 0, NBINS - 1).astype(jnp.int32)
    patch_pos = place_ends(jax.random.randint(arg_keys[4], (TOKENS,), 0, PATCH_POS), jax.random.fold_in(arg_keys[4], 1), 0, PATCH_POS - 1).astype(jnp.int32)
    token_table = normal_values(arg_keys[5], (VOCAB, D), 1.0, 6.0, ((0, 8),))
    pos_table = normal_values(arg_keys[6], (PATCH_POS, D), 0.5, 4.0)
    w_patch = normal_values(arg_keys[7], (PIX, D), PIX ** -0.5, 0.21875)
    w_res_a = normal_values(arg_keys[8], (D, D), D ** -0.5, 0.21875)
    w_res_b = normal_values(arg_keys[9], (D, D), D ** -0.5, 0.21875)
    gain_one = jnp.clip(1.0 + 0.1 * jax.random.normal(arg_keys[10], (D,), jnp.float32), 0.5, 1.5).astype(jnp.bfloat16)
    bias_one = normal_values(arg_keys[11], (D,), 0.3, 2.0)
    w_q = normal_values(arg_keys[12], (D, D), D ** -0.5, 0.21875)
    w_k = normal_values(arg_keys[13], (D, D), D ** -0.5, 0.21875)
    w_v = normal_values(arg_keys[14], (D, D), D ** -0.5, 0.21875)
    w_o = normal_values(arg_keys[15], (D, D), HEAD_DIM ** -0.5, 1.0)
    gain_two = jnp.clip(1.0 + 0.1 * jax.random.normal(arg_keys[16], (D,), jnp.float32), 0.5, 1.5).astype(jnp.bfloat16)
    bias_two = normal_values(arg_keys[17], (D,), 0.3, 2.0)
    w_up = normal_values(arg_keys[18], (D, FF), D ** -0.5, 0.21875)
    w_down = normal_values(arg_keys[19], (FF, D), FF ** -0.5, 0.109375)
    cotangent = normal_values(arg_keys[20], (TOKENS, D), 1.0, 6.0, ((0, 32),))
    return dict(pixels=pixels, counts=counts, token_ids=token_ids, action_bins=action_bins, patch_pos=patch_pos, token_table=token_table, pos_table=pos_table, w_patch=w_patch, w_res_a=w_res_a, w_res_b=w_res_b, gain_one=gain_one, bias_one=bias_one, w_q=w_q, w_k=w_k, w_v=w_v, w_o=w_o, gain_two=gain_two, bias_two=bias_two, w_up=w_up, w_down=w_down, cotangent=cotangent)


exact_precision = lax.Precision.HIGHEST

@jax.custom_vjp
def low(v):
    return lax.optimization_barrier(v.astype(jnp.bfloat16)).astype(jnp.float32)

@jax.custom_vjp
def low_back(v):
    return v

def low_keep(v):
    return (low(v), None)

def low_pass(kept, grad):
    return (grad,)

def back_keep(v):
    return (v, None)

def back_low(kept, grad):
    return (low(grad),)
low.defvjp(low_keep, low_pass)
low_back.defvjp(back_keep, back_low)

def normalize(values):
    average = lax.optimization_barrier(jnp.mean(values, -1, keepdims=True))
    centred = values - average
    variance = lax.optimization_barrier(jnp.mean(centred * centred, -1, keepdims=True))
    return centred * lax.rsqrt(variance + 1e-05)

def product(left, right):
    return jnp.dot(left, right, precision=exact_precision)

def one_sequence(weights, pixel_rows, row_ids, patch_ids, image_rows, table_full):
    pos_table, w_patch, w_res_a, w_res_b, gain_one, bias_one, w_q, w_k, w_v, w_o, gain_two, bias_two, w_up, w_down = weights
    length = pixel_rows.shape[0]
    patch_first = low_back(product(pixel_rows, w_patch))
    res_inner = low_back(product(low(patch_first), w_res_a))
    res_mixed = low_back(product(low(jax.nn.gelu(res_inner)), w_res_b))
    image_embed = patch_first + res_mixed + pos_table[patch_ids]
    table_embed = low_back(table_full[row_ids])
    embedded = jnp.where(image_rows[:, None], image_embed, table_embed)
    normed_one = low(normalize(embedded) * gain_one + bias_one)
    queries = low(low_back(product(normed_one, w_q))).reshape(length, HEADS, HEAD_DIM)
    key_heads = low(low_back(product(normed_one, w_k))).reshape(length, HEADS, HEAD_DIM)
    value_heads = low(low_back(product(normed_one, w_v))).reshape(length, HEADS, HEAD_DIM)
    scores = low_back(jnp.einsum('qhd,khd->hqk', queries, key_heads, precision=exact_precision) * HEAD_DIM ** (-0.5))
    positions = jnp.arange(length)
    allowed = positions[None, :] <= positions[:, None]
    scores = jnp.where(allowed[None], scores, -1e+30)
    softmax_low = low(jax.nn.softmax(scores, axis=-1))
    attended = jnp.einsum('hqk,khd->qhd', softmax_low, value_heads, precision=exact_precision)
    attended = low(low_back(attended.reshape(length, HEADS * HEAD_DIM)))
    middle = embedded + low_back(product(attended, w_o))
    normed_two = low(normalize(middle) * gain_two + bias_two)
    up_low = low(jax.nn.gelu(low_back(product(normed_two, w_up))))
    return middle + low_back(product(up_low, w_down))

def reference(pixels, counts, token_ids, action_bins, patch_pos, token_table, pos_table, w_patch, w_res_a, w_res_b, gain_one, bias_one, w_q, w_k, w_v, w_o, gain_two, bias_two, w_up, w_down, cotangent):
    positions = jnp.arange(TOK_DEV)
    image_rows = positions[None, :] < counts[:, 0:1]
    action_rows = positions[None, :] >= TOK_DEV - counts[:, 1:2]
    row_ids = jnp.where(action_rows, TEXT_VOCAB + action_bins.reshape(SEQS, TOK_DEV), token_ids.reshape(SEQS, TOK_DEV)).astype(jnp.int32)
    patch_ids = patch_pos.reshape(SEQS, TOK_DEV).astype(jnp.int32)
    weights = tuple((w.astype(jnp.float32) for w in (pos_table, w_patch, w_res_a, w_res_b, gain_one, bias_one, w_q, w_k, w_v, w_o, gain_two, bias_two, w_up, w_down)))
    pixel_all = pixels.astype(jnp.float32)
    table_full = token_table.astype(jnp.float32)
    group_size = math.gcd(SEQS, max(1, 4096 // TOK_DEV))
    groups = SEQS // group_size

    def forward(weight_set, pixel_set, table_set):

        def group_step(carry, inputs):
            pixel_group, row_group, patch_group, image_group = inputs
            runner = jax.vmap(one_sequence, in_axes=(None, 0, 0, 0, 0, None))
            return (carry, runner(weight_set, pixel_group, row_group, patch_group, image_group, table_set))
        inputs = (pixel_set.reshape(groups, group_size, TOK_DEV, PIX), row_ids.reshape(groups, group_size, TOK_DEV), patch_ids.reshape(groups, group_size, TOK_DEV), image_rows.reshape(groups, group_size, TOK_DEV))
        _, outputs = lax.scan(jax.checkpoint(group_step), None, inputs)
        return outputs.reshape(TOKENS, D)
    result, pullback = jax.vjp(forward, weights, pixel_all, table_full)
    grad_weights, grad_pixels, grad_table = pullback(cotangent.astype(jnp.float32))
    return (result.astype(jnp.bfloat16), grad_pixels, grad_table, grad_weights[0], grad_weights[1], grad_weights[2], grad_weights[3], grad_weights[4], grad_weights[5], grad_weights[6], grad_weights[7], grad_weights[8], grad_weights[9], grad_weights[10], grad_weights[11], grad_weights[12], grad_weights[13])
```

```python
import functools

import jax
import jax.numpy as jnp
from jax import lax
from jax.experimental import pallas as pl
from jax.experimental.pallas import tpu as pltpu
from jax.sharding import PartitionSpec as P

HEAD_DIM = 32
TEXT_VOCAB = 32000
BLOCK = 256
HEADS_STEP = 2
BOTH = ("dp", "emb")
LOG2_E = 1.4426950408889634


def normalize(values):
    average = jnp.mean(values, -1, keepdims=True)
    centred = values - average
    variance = jnp.mean(centred * centred, -1, keepdims=True)
    return centred * lax.rsqrt(variance + 1e-05)


def norm_affine(values, gain, offset):
    return normalize(values) * gain + offset


def contract(left, right, left_dim, right_dim):
    return lax.dot_general(
        left, right, (((left_dim,), (right_dim,)), ((), ())), preferred_element_type=jnp.float32
    )


def product(left, right):
    return contract(left, right, 1, 0)


def product_left(left, right):
    return contract(left, right, 0, 0)


def product_right(left, right):
    return contract(left, right, 1, 1)


def forward_kernel(heads, q_ref, k_ref, v_ref, o_ref, p_ref, r_ref):
    length = q_ref.shape[1]
    scaling = HEAD_DIM ** (-0.5) * LOG2_E
    key_place = lax.broadcasted_iota(jnp.int32, (BLOCK, BLOCK), 0)
    query_place = lax.broadcasted_iota(jnp.int32, (BLOCK, BLOCK), 1)
    allowed = key_place <= query_place
    for head in range(heads):
        rows = slice(head * HEAD_DIM, (head + 1) * HEAD_DIM)
        keys = k_ref[rows, :]
        values = v_ref[rows, :]
        for step in range(length // BLOCK):
            start, end = step * BLOCK, (step + 1) * BLOCK
            scores = contract(keys[:, :end], q_ref[rows, start:end], 0, 0) * scaling
            corner = jnp.where(allowed, scores[start:], -1e30)
            highest = jnp.max(corner, 0, keepdims=True)
            if step:
                highest = jnp.maximum(highest, jnp.max(scores[:start], 0, keepdims=True))
            weights = jnp.exp2(corner - highest)
            total = jnp.sum(weights, 0, keepdims=True)
            weights = weights.astype(jnp.bfloat16)
            if step:
                above = jnp.exp2(scores[:start] - highest)
                total = total + jnp.sum(above, 0, keepdims=True)
                weights = jnp.concatenate([above.astype(jnp.bfloat16), weights], 0)
            inverse = 1.0 / total
            base = BLOCK * (step * (step + 1) // 2)
            p_ref[head, base : base + end, :] = weights
            r_ref[head, :, start:end] = inverse
            o_ref[rows, start:end] = (
                contract(values[:, :end], weights, 1, 0) * inverse
            ).astype(jnp.bfloat16)


def packed_rows(length):
    steps = length // BLOCK
    return BLOCK * (steps * (steps + 1) // 2)


def attention_forward(queries, key_heads, values):
    width, length = queries.shape
    heads = width // HEAD_DIM
    packed = packed_rows(length)
    rows = pl.BlockSpec((HEADS_STEP * HEAD_DIM, length), lambda g: (g, 0))
    return pl.pallas_call(
        functools.partial(forward_kernel, HEADS_STEP),
        grid=(heads // HEADS_STEP,),
        in_specs=[rows] * 3,
        out_specs=[
            rows,
            pl.BlockSpec((HEADS_STEP, packed, BLOCK), lambda g: (g, 0, 0)),
            pl.BlockSpec((HEADS_STEP, 1, length), lambda g: (g, 0, 0)),
        ],
        out_shape=[
            jax.ShapeDtypeStruct((width, length), jnp.bfloat16),
            jax.ShapeDtypeStruct((heads, packed, BLOCK), jnp.bfloat16),
            jax.ShapeDtypeStruct((heads, 1, length), jnp.float32),
        ],
        compiler_params=pltpu.CompilerParams(vmem_limit_bytes=32 << 20),
        cost_estimate=pl.CostEstimate(
            flops=50_000_000_000, bytes_accessed=heads * packed * BLOCK * 2, transcendentals=0
        ),
        name="attention_forward",
    )(queries, key_heads, values)


def backward_kernel(heads, q_ref, k_ref, v_ref, o_ref, g_ref, p_ref, r_ref, d_ref, s_ref):
    length = q_ref.shape[1]
    steps = length // BLOCK
    scaling = HEAD_DIM ** (-0.5)
    for head in range(heads):
        rows = slice(head * HEAD_DIM, (head + 1) * HEAD_DIM)
        grads = (g_ref[rows, :].astype(jnp.float32) * r_ref[head]).astype(jnp.bfloat16)
        inner = jnp.sum(
            grads.astype(jnp.float32) * o_ref[rows, :].astype(jnp.float32), 0, keepdims=True
        )
        queries = q_ref[rows, :]
        keys = k_ref[rows, :]
        values = v_ref[rows, :]
        for step in range(steps):
            start, end = step * BLOCK, (step + 1) * BLOCK
            base = BLOCK * (step * (step + 1) // 2)
            grad_probs = contract(values[:, :end], grads[:, start:end], 0, 0)
            grad_scores = p_ref[head, base : base + end, :] * (
                grad_probs - inner[:, start:end]
            ).astype(jnp.bfloat16)
            s_ref[head, base : base + end, :] = grad_scores
            d_ref[0, rows, start:end] = (
                contract(keys[:, :end], grad_scores, 1, 0) * scaling
            ).astype(jnp.bfloat16)
        for column in range(steps):
            grad_keys = jnp.zeros((HEAD_DIM, BLOCK), jnp.float32)
            grad_values = jnp.zeros((HEAD_DIM, BLOCK), jnp.float32)
            for step in range(column, steps):
                base = BLOCK * (step * (step + 1) // 2 + column)
                span = slice(step * BLOCK, (step + 1) * BLOCK)
                grad_values = grad_values + contract(
                    grads[:, span], p_ref[head, base : base + BLOCK, :], 1, 1
                )
                grad_keys = grad_keys + contract(
                    queries[:, span], s_ref[head, base : base + BLOCK, :], 1, 1
                )
            span = slice(column * BLOCK, (column + 1) * BLOCK)
            d_ref[1, rows, span] = (grad_keys * scaling).astype(jnp.bfloat16)
            d_ref[2, rows, span] = grad_values.astype(jnp.bfloat16)


def attention_backward(queries, key_heads, values, attended, grads, probs, inverse):
    width, length = queries.shape
    heads = width // HEAD_DIM
    packed = packed_rows(length)
    rows = pl.BlockSpec((HEADS_STEP * HEAD_DIM, length), lambda g: (g, 0))
    return pl.pallas_call(
        functools.partial(backward_kernel, HEADS_STEP),
        grid=(heads // HEADS_STEP,),
        in_specs=[rows] * 5
        + [
            pl.BlockSpec((HEADS_STEP, packed, BLOCK), lambda g: (g, 0, 0)),
            pl.BlockSpec((HEADS_STEP, 1, length), lambda g: (g, 0, 0)),
        ],
        out_specs=pl.BlockSpec((3, HEADS_STEP * HEAD_DIM, length), lambda g: (0, g, 0)),
        out_shape=jax.ShapeDtypeStruct((3, width, length), jnp.bfloat16),
        scratch_shapes=[pltpu.VMEM((HEADS_STEP, packed, BLOCK), jnp.bfloat16)],
        compiler_params=pltpu.CompilerParams(vmem_limit_bytes=32 << 20),
        cost_estimate=pl.CostEstimate(
            flops=55_000_000_000, bytes_accessed=heads * packed * BLOCK * 2, transcendentals=0
        ),
        name="attention_backward",
    )(queries, key_heads, values, attended, grads, probs, inverse)


def chunk_shape(capacity, columns):
    if columns % 128 == 64 and capacity % 32 == 0:
        return (capacity * columns // 128, 128)
    return (capacity, columns)


def pack_kernel(parts, grad_ref, slot_ref, out_ref):
    length, width = grad_ref.shape
    columns = width // parts
    rows, lanes = out_ref.shape[2:]
    capacity = rows * lanes // columns
    slots = pl.program_id(0) * capacity + lax.broadcasted_iota(
        jnp.int32, (capacity, length), 0
    )
    hot = jnp.where(slots == slot_ref[...], 1.0, 0.0).astype(jnp.bfloat16)
    packed = product(hot, grad_ref[...])
    for part in range(parts):
        start = part * columns
        if lanes == columns:
            out_ref[part, 0] = packed[:, start : start + columns].astype(jnp.bfloat16)
            continue
        full = columns // 128 * 128
        tail = start + full
        for tile in range(full // 128):
            place = start + tile * 128
            if start % 128 == 0:
                piece = packed[:, place : place + 128]
            else:
                left = lax.broadcasted_iota(jnp.int32, (capacity, 128), 1) < 64
                piece = jnp.where(
                    left,
                    pltpu.roll(packed[:, place - 64 : place + 64], 64, 1),
                    pltpu.roll(packed[:, place + 64 : place + 192], 64, 1),
                )
            out_ref[part, 0, tile * capacity : (tile + 1) * capacity, :] = piece.astype(
                jnp.bfloat16
            )
        tile = tail // 128 * 128
        upper = packed[: capacity // 2, tile : tile + 128]
        lower = packed[capacity // 2 :, tile : tile + 128]
        left = lax.broadcasted_iota(jnp.int32, upper.shape, 1) < 64
        if tail % 128 == 0:
            mixed = jnp.where(left, upper, pltpu.roll(lower, 64, 1))
        else:
            mixed = jnp.where(left, pltpu.roll(upper, 64, 1), lower)
        out_ref[part, 0, full // 128 * capacity :, :] = mixed.astype(jnp.bfloat16)


def pack_rows(grad_rows, slot_index, parts, owners, capacity):
    length, width = grad_rows.shape
    rows, lanes = chunk_shape(capacity, width // parts)
    return pl.pallas_call(
        functools.partial(pack_kernel, parts),
        grid=(owners,),
        in_specs=[
            pl.BlockSpec((length, width), lambda o: (0, 0)),
            pl.BlockSpec((1, length), lambda o: (0, 0)),
        ],
        out_specs=pl.BlockSpec((parts, 1, rows, lanes), lambda o: (0, o, 0, 0)),
        out_shape=jax.ShapeDtypeStruct((parts, owners, rows, lanes), jnp.bfloat16),
        compiler_params=pltpu.CompilerParams(vmem_limit_bytes=32 << 20),
        name="pack_rows",
    )(grad_rows, slot_index)


def table_kernel(swapped, chunk_ref, ids_ref, out_ref, hold_ref):
    sources, rows, lanes = chunk_ref.shape
    block, columns = out_ref.shape
    slots = ids_ref.shape[1]
    capacity = slots // sources

    @pl.when(pl.program_id(0) == 0)
    def unpack():
        if lanes == columns:
            for source in range(sources):
                hold_ref[source * capacity : (source + 1) * capacity, :] = chunk_ref[source]
            return

        def one(source, carry):
            base = pl.multiple_of(source * capacity, capacity)
            full = columns // 128
            for tile in range(full):
                hold_ref[pl.ds(base, capacity), tile * 128 : (tile + 1) * 128] = chunk_ref[
                    source, tile * capacity : (tile + 1) * capacity, :
                ]
            mixed = chunk_ref[source, full * capacity :, :].astype(jnp.float32)
            turned = pltpu.roll(mixed, 64, 1).astype(jnp.bfloat16)
            half = capacity // 2
            hold_ref[pl.ds(base, half), full * 128 :] = mixed.astype(jnp.bfloat16)[:, :64]
            hold_ref[pl.ds(base + half, half), full * 128 :] = turned[:, :64]
            return carry

        lax.fori_loop(0, sources, one, 0)

    places = pl.program_id(0) * block + lax.broadcasted_iota(jnp.int32, (block, 512), 0)
    total = jnp.zeros((block, columns), jnp.float32)
    for start in range(0, slots, 512):
        hot = jnp.where(places == ids_ref[:, start : start + 512], 1.0, 0.0)
        total = total + product(hot.astype(jnp.bfloat16), hold_ref[start : start + 512, :])
    out_ref[...] = total


def add_rows(chunks, ids, table_rows, columns):
    sources, rows, lanes = chunks.shape
    slots = ids.shape[1]
    block = table_rows // 6 if table_rows % 48 == 0 else table_rows
    return pl.pallas_call(
        functools.partial(table_kernel, False),
        grid=(table_rows // block,),
        in_specs=[
            pl.BlockSpec((sources, rows, lanes), lambda b: (0, 0, 0)),
            pl.BlockSpec((1, slots), lambda b: (0, 0)),
        ],
        out_specs=pl.BlockSpec((block, columns), lambda b: (b, 0)),
        out_shape=jax.ShapeDtypeStruct((table_rows, columns), jnp.float32),
        scratch_shapes=[pltpu.VMEM((slots, columns), jnp.bfloat16)],
        compiler_params=pltpu.CompilerParams(vmem_limit_bytes=40 << 20),
        name="add_rows",
    )(chunks, ids)


def swap_half(blocks, axis, bit):
    size = lax.axis_size("emb")
    mine = (lax.axis_index("emb") >> bit) & 1
    keep = lax.dynamic_index_in_dim(blocks, mine, axis, keepdims=False)
    send = lax.dynamic_index_in_dim(blocks, 1 - mine, axis, keepdims=False)
    got = lax.ppermute(send, "emb", [(i, i ^ (1 << bit)) for i in range(size)])
    return (keep.astype(jnp.float32) + got.astype(jnp.float32)).astype(jnp.bfloat16)


def swap_all(blocks, order, held):
    for bit in order:
        blocks = swap_half(blocks, 1 + held.index(bit), bit)
        held = [other for other in held if other != bit]
    return blocks


def scatter_sum(array):
    owners = lax.axis_size("emb")
    groups = lax.axis_size("dp")
    bits = owners.bit_length() - 1
    rows, columns = array.shape
    share = rows // (owners * groups)
    blocks = array.reshape((groups,) + (2,) * bits + (share, columns))
    held = list(range(bits))[::-1]
    blocks = swap_half(blocks, 1 + held.index(0), 0)
    held.remove(0)
    cut = columns // 256 * 128
    upward = list(range(1, bits))
    parts = [
        swap_all(blocks[..., :cut], upward, held),
        swap_all(blocks[..., cut:], upward[::-1], held),
    ]
    parts = [lax.all_to_all(part, "dp", 0, 0, tiled=True) for part in parts]
    return jnp.concatenate([jnp.sum(part.astype(jnp.float32), 0) for part in parts], 1)


def columns_of(vectors):
    stacked = jnp.stack(vectors, 1).astype(jnp.bfloat16)
    return jnp.pad(stacked, ((0, 0), (0, 128 - len(vectors))))


def on_device(
    pixels,
    counts,
    token_ids,
    action_bins,
    patch_pos,
    token_table,
    pos_table,
    w_patch,
    w_res_a,
    w_res_b,
    gain_one,
    bias_one,
    w_q,
    w_k,
    w_v,
    w_o,
    gain_two,
    bias_two,
    w_up,
    w_down,
    cotangent,
):
    length = pixels.shape[0]
    model_width = w_q.shape[0]
    positions = jnp.arange(length)
    image_rows = positions < counts[0, 0]
    action_rows = positions >= length - counts[0, 1]
    table_rows = jnp.logical_not(image_rows)
    row_ids = jnp.where(action_rows, TEXT_VOCAB + action_bins, token_ids)
    rows_owned = token_table.shape[0]
    owners_total = lax.axis_size("emb")
    capacity = 3 * length // (2 * owners_total)
    owner_index = row_ids // rows_owned
    local_row = row_ids - owner_index * rows_owned
    owner_hot = (
        (owner_index[:, None] == jnp.arange(owners_total)[None, :]) & table_rows[:, None]
    ).astype(jnp.int32)
    earlier = jnp.cumsum(owner_hot, 0) - owner_hot
    rank_within = jnp.sum(earlier * owner_hot, 1)
    slot_index = jnp.where(
        table_rows, owner_index * capacity + rank_within, owners_total * capacity
    )
    request = (
        jnp.full((owners_total * capacity + 1,), -1, jnp.int32)
        .at[slot_index]
        .set(jnp.where(table_rows, local_row, -1))
    )
    received = lax.all_to_all(
        request[:-1].reshape(owners_total, capacity), "emb", split_axis=0, concat_axis=0, tiled=True
    )
    valid_slots = received >= 0
    local_ids = jnp.maximum(received, 0)
    fetched = jnp.where(valid_slots[..., None], token_table[local_ids], jnp.zeros((), jnp.bfloat16))
    returned = lax.all_to_all(fetched, "emb", split_axis=0, concat_axis=0, tiled=True)
    slot_safe = jnp.minimum(slot_index, owners_total * capacity - 1)
    table_embed = returned.reshape(owners_total * capacity, model_width)[slot_safe].astype(
        jnp.float32
    )
    patch_first = product(pixels, w_patch)
    first_low = patch_first.astype(jnp.bfloat16)
    res_inner = product(first_low, w_res_a)
    res_gelu, gelu_back_res = jax.vjp(jax.nn.gelu, res_inner)
    res_act = res_gelu.astype(jnp.bfloat16)
    res_mixed = product(res_act, w_res_b)
    position_hot = patch_pos[:, None] == jnp.arange(pos_table.shape[0])[None, :]
    position_embed = product(position_hot.astype(jnp.bfloat16), pos_table)
    image_embed = patch_first + res_mixed + position_embed
    embedded = jnp.where(image_rows[:, None], image_embed, table_embed)
    normed_one_f, norm_back_one = jax.vjp(
        norm_affine, embedded, gain_one.astype(jnp.float32), bias_one.astype(jnp.float32)
    )
    normed_one = normed_one_f.astype(jnp.bfloat16)
    queries = contract(w_q, normed_one, 0, 1).astype(jnp.bfloat16)
    key_heads = contract(w_k, normed_one, 0, 1).astype(jnp.bfloat16)
    value_heads = contract(w_v, normed_one, 0, 1).astype(jnp.bfloat16)
    attended, probs, inverse = attention_forward(queries, key_heads, value_heads)
    middle = embedded + product_left(attended, w_o)
    normed_two_f, norm_back_two = jax.vjp(
        norm_affine, middle, gain_two.astype(jnp.float32), bias_two.astype(jnp.float32)
    )
    normed_two = normed_two_f.astype(jnp.bfloat16)
    up_pre = product(normed_two, w_up)
    up_act, gelu_back_up = jax.vjp(jax.nn.gelu, up_pre)
    up_low = up_act.astype(jnp.bfloat16)
    output = (middle + product(up_low, w_down)).astype(jnp.bfloat16)
    grad_w_down = product_left(up_low, cotangent).astype(jnp.bfloat16)
    share_w_down = scatter_sum(grad_w_down)
    (grad_up_pre,) = gelu_back_up(product_right(cotangent, w_down))
    grad_up = grad_up_pre.astype(jnp.bfloat16)
    grad_w_up = product_left(normed_two, grad_up).astype(jnp.bfloat16)
    grad_normed_two = product_right(grad_up, w_up)
    grad_middle_norm, grad_gain_two, grad_bias_two = norm_back_two(grad_normed_two)
    grad_middle = cotangent.astype(jnp.float32) + grad_middle_norm
    grad_branch = grad_middle.astype(jnp.bfloat16)
    grad_w_o = product(attended, grad_branch).astype(jnp.bfloat16)
    share_up = scatter_sum(
        jnp.concatenate([grad_w_up, grad_w_o, columns_of([grad_gain_two, grad_bias_two])], 1)
    )
    grad_attended = product_right(w_o, grad_branch).astype(jnp.bfloat16)
    grad_heads = attention_backward(
        queries, key_heads, value_heads, attended, grad_attended, probs, inverse
    ).reshape(3 * model_width, length)
    grad_w_heads = contract(normed_one, grad_heads, 0, 1).astype(jnp.bfloat16)
    grad_normed_one = product_left(grad_heads, jnp.concatenate([w_q.T, w_k.T, w_v.T], 0))
    grad_embed_norm, grad_gain_one, grad_bias_one = norm_back_one(grad_normed_one)
    share_heads = scatter_sum(
        jnp.concatenate([grad_w_heads, columns_of([grad_gain_one, grad_bias_one])], 1)
    )
    grad_embedded = grad_middle + grad_embed_norm
    grad_low = grad_embedded.astype(jnp.bfloat16)
    groups = lax.axis_size("dp")
    columns = model_width // groups
    all_ids = lax.all_gather(received, "dp", axis=0, tiled=False).reshape(1, -1)
    chunks = pack_rows(grad_low, slot_index.reshape(1, length), groups, owners_total, capacity)
    chunks = lax.all_to_all(
        chunks.reshape((groups * owners_total,) + chunks.shape[2:]), BOTH, 0, 0, tiled=True
    )
    grad_table = add_rows(chunks, all_ids, rows_owned, columns)
    grad_image = jnp.where(image_rows[:, None], grad_embedded, 0.0)
    grad_mixed = grad_image.astype(jnp.bfloat16)
    grad_pos_table = product_left(position_hot.astype(jnp.bfloat16), grad_mixed)
    grad_w_res_b = product_left(res_act, grad_mixed).astype(jnp.bfloat16)
    (grad_inner_f,) = gelu_back_res(product_right(grad_mixed, w_res_b))
    grad_inner = grad_inner_f.astype(jnp.bfloat16)
    grad_w_res_a = product_left(first_low, grad_inner).astype(jnp.bfloat16)
    grad_first = (grad_image + product_right(grad_inner, w_res_a)).astype(jnp.bfloat16)
    grad_w_patch = product_left(pixels, grad_first).astype(jnp.bfloat16)
    grad_pixels = product_right(grad_first, w_patch)
    devices = groups * owners_total
    pos_rows = pos_table.shape[0]
    share = model_width // devices
    pos_columns = pos_rows * model_width // model_width
    spread = grad_pos_table.astype(jnp.bfloat16).reshape(model_width, pos_columns)
    share_res = scatter_sum(
        jnp.concatenate([grad_w_patch, grad_w_res_a, grad_w_res_b, spread], 1)
    )
    wide = w_up.shape[1]

    def cut(array, place):
        return array[:, place * model_width : (place + 1) * model_width]

    return (
        output,
        grad_pixels,
        grad_table,
        share_res[:, 3 * model_width :].reshape(pos_rows // devices, model_width),
        cut(share_res, 0),
        cut(share_res, 1),
        cut(share_res, 2),
        share_heads[:, 3 * model_width],
        share_heads[:, 3 * model_width + 1],
        cut(share_heads, 0),
        cut(share_heads, 1),
        cut(share_heads, 2),
        share_up[:, wide : wide + model_width],
        share_up[:, wide + model_width],
        share_up[:, wide + model_width + 1],
        share_up[:, :wide],
        share_w_down,
    )


def solution(mesh):
    in_specs = (
        P(("dp", "emb"), None),
        P(("dp", "emb"), None),
        P(("dp", "emb")),
        P(("dp", "emb")),
        P(("dp", "emb")),
        P("emb", None),
        P(),
        P(),
        P(),
        P(),
        P(),
        P(),
        P(),
        P(),
        P(),
        P(),
        P(),
        P(),
        P(),
        P(),
        P(("dp", "emb"), None),
    )
    out_specs = (
        P(("dp", "emb"), None),
        P(("dp", "emb"), None),
        P("emb", "dp"),
        P(("dp", "emb"), None),
        P(("dp", "emb"), None),
        P(("dp", "emb"), None),
        P(("dp", "emb"), None),
        P(("dp", "emb")),
        P(("dp", "emb")),
        P(("dp", "emb"), None),
        P(("dp", "emb"), None),
        P(("dp", "emb"), None),
        P(("dp", "emb"), None),
        P(("dp", "emb")),
        P(("dp", "emb")),
        P(("dp", "emb"), None),
        P(("dp", "emb"), None),
    )
    return jax.shard_map(
        on_device, mesh=mesh, in_specs=in_specs, out_specs=out_specs, check_vma=False
    )
```

```python
import functools

import jax
import jax.numpy as jnp
from jax import lax
from jax.experimental import pallas as pl
from jax.experimental.pallas import tpu as pltpu
from jax.sharding import PartitionSpec as P

HEAD_DIM = 32
TEXT_VOCAB = 32000
BLOCK = 256
HEADS_STEP = 2
MESH = pl.DeviceIdType.MESH
LOG2_E = 1.4426950408889634


def normalize(values):
    average = jnp.mean(values, -1, keepdims=True)
    centred = values - average
    variance = jnp.mean(centred * centred, -1, keepdims=True)
    return centred * lax.rsqrt(variance + 1e-05)


def norm_affine(values, gain, offset):
    return normalize(values) * gain + offset


def contract(left, right, left_dim, right_dim):
    return lax.dot_general(
        left, right, (((left_dim,), (right_dim,)), ((), ())), preferred_element_type=jnp.float32
    )


def product(left, right):
    return contract(left, right, 1, 0)


def product_left(left, right):
    return contract(left, right, 0, 0)


def product_right(left, right):
    return contract(left, right, 1, 1)


def forward_kernel(heads, q_ref, k_ref, v_ref, o_ref, p_ref, r_ref):
    length = q_ref.shape[1]
    scaling = HEAD_DIM ** (-0.5) * LOG2_E
    key_place = lax.broadcasted_iota(jnp.int32, (BLOCK, BLOCK), 0)
    query_place = lax.broadcasted_iota(jnp.int32, (BLOCK, BLOCK), 1)
    allowed = key_place <= query_place
    for head in range(heads):
        rows = slice(head * HEAD_DIM, (head + 1) * HEAD_DIM)
        keys = k_ref[rows, :]
        values = v_ref[rows, :]
        for step in range(length // BLOCK):
            start, end = step * BLOCK, (step + 1) * BLOCK
            scores = contract(keys[:, :end], q_ref[rows, start:end], 0, 0) * scaling
            corner = jnp.where(allowed, scores[start:], -1e30)
            highest = jnp.max(corner, 0, keepdims=True)
            if step:
                highest = jnp.maximum(highest, jnp.max(scores[:start], 0, keepdims=True))
            weights = jnp.exp2(corner - highest)
            total = jnp.sum(weights, 0, keepdims=True)
            weights = weights.astype(jnp.bfloat16)
            if step:
                above = jnp.exp2(scores[:start] - highest)
                total = total + jnp.sum(above, 0, keepdims=True)
                weights = jnp.concatenate([above.astype(jnp.bfloat16), weights], 0)
            inverse = 1.0 / total
            base = BLOCK * (step * (step + 1) // 2)
            p_ref[head, base : base + end, :] = weights
            r_ref[head, :, start:end] = inverse
            o_ref[rows, start:end] = (
                contract(values[:, :end], weights, 1, 0) * inverse
            ).astype(jnp.bfloat16)


def packed_rows(length):
    steps = length // BLOCK
    return BLOCK * (steps * (steps + 1) // 2)


def attention_forward(queries, key_heads, values):
    width, length = queries.shape
    heads = width // HEAD_DIM
    packed = packed_rows(length)
    rows = pl.BlockSpec((HEADS_STEP * HEAD_DIM, length), lambda g: (g, 0))
    return pl.pallas_call(
        functools.partial(forward_kernel, HEADS_STEP),
        grid=(heads // HEADS_STEP,),
        in_specs=[rows] * 3,
        out_specs=[
            rows,
            pl.BlockSpec((HEADS_STEP, packed, BLOCK), lambda g: (g, 0, 0)),
            pl.BlockSpec((HEADS_STEP, 1, length), lambda g: (g, 0, 0)),
        ],
        out_shape=[
            jax.ShapeDtypeStruct((width, length), jnp.bfloat16),
            jax.ShapeDtypeStruct((heads, packed, BLOCK), jnp.bfloat16),
            jax.ShapeDtypeStruct((heads, 1, length), jnp.float32),
        ],
        compiler_params=pltpu.CompilerParams(vmem_limit_bytes=32 << 20),
        cost_estimate=pl.CostEstimate(
            flops=50_000_000_000, bytes_accessed=heads * packed * BLOCK * 2, transcendentals=0
        ),
        name="attention_forward",
    )(queries, key_heads, values)


def backward_kernel(heads, count, q_ref, k_ref, v_ref, o_ref, g_ref, p_ref, r_ref, *refs):
    packs, d_ref, outs = refs[:count], refs[count], refs[count + 1 : 2 * count + 1]
    s_ref = refs[2 * count + 1]
    shares = shares_of(packs, outs, refs[2 * count + 2 :])
    bits = shares[0].bits
    first, second = shares
    number = pl.program_id(0)
    last = pl.num_programs(0) - 1

    @pl.when(number == 0)
    def begin():
        greet(False)
        first.start()
        second.start()

    @pl.when(number == 2)
    def begin_first():
        first.take(0)

    @pl.when(number == 5)
    def begin_second():
        first.take(1)
        second.take(0)

    @pl.when(number == 8)
    def go_on():
        for stage in range(2, bits):
            first.take(stage)

    length = q_ref.shape[1]
    steps = length // BLOCK
    scaling = HEAD_DIM ** (-0.5)
    for head in range(heads):
        rows = slice(head * HEAD_DIM, (head + 1) * HEAD_DIM)
        grads = (g_ref[rows, :].astype(jnp.float32) * r_ref[head]).astype(jnp.bfloat16)
        inner = jnp.sum(
            grads.astype(jnp.float32) * o_ref[rows, :].astype(jnp.float32), 0, keepdims=True
        )
        queries = q_ref[rows, :]
        keys = k_ref[rows, :]
        values = v_ref[rows, :]
        for step in range(steps):
            start, end = step * BLOCK, (step + 1) * BLOCK
            base = BLOCK * (step * (step + 1) // 2)
            grad_probs = contract(values[:, :end], grads[:, start:end], 0, 0)
            grad_scores = p_ref[head, base : base + end, :] * (
                grad_probs - inner[:, start:end]
            ).astype(jnp.bfloat16)
            s_ref[head, base : base + end, :] = grad_scores
            d_ref[0, rows, start:end] = (
                contract(keys[:, :end], grad_scores, 1, 0) * scaling
            ).astype(jnp.bfloat16)
        for column in range(steps):
            grad_keys = jnp.zeros((HEAD_DIM, BLOCK), jnp.float32)
            grad_values = jnp.zeros((HEAD_DIM, BLOCK), jnp.float32)
            for step in range(column, steps):
                base = BLOCK * (step * (step + 1) // 2 + column)
                span = slice(step * BLOCK, (step + 1) * BLOCK)
                grad_values = grad_values + contract(
                    grads[:, span], p_ref[head, base : base + BLOCK, :], 1, 1
                )
                grad_keys = grad_keys + contract(
                    queries[:, span], s_ref[head, base : base + BLOCK, :], 1, 1
                )
            span = slice(column * BLOCK, (column + 1) * BLOCK)
            d_ref[1, rows, span] = (grad_keys * scaling).astype(jnp.bfloat16)
            d_ref[2, rows, span] = grad_values.astype(jnp.bfloat16)

    @pl.when(number == last)
    def end():
        for stage in range(1, bits):
            second.take(stage)
        first.finish()
        second.finish()


def attention_backward(queries, key_heads, values, attended, grads, probs, inverse, packs):
    width, length = queries.shape
    heads = width // HEAD_DIM
    packed = packed_rows(length)
    rows = pl.BlockSpec((HEADS_STEP * HEAD_DIM, length), lambda g: (g, 0))
    scratch = [pltpu.VMEM((HEADS_STEP, packed, BLOCK), jnp.bfloat16)]
    for pack in packs:
        scratch = scratch + shares_scratch(pack.shape)
    return pl.pallas_call(
        functools.partial(backward_kernel, HEADS_STEP, len(packs)),
        grid=(heads // HEADS_STEP,),
        in_specs=[rows] * 5
        + [
            pl.BlockSpec((HEADS_STEP, packed, BLOCK), lambda g: (g, 0, 0)),
            pl.BlockSpec((HEADS_STEP, 1, length), lambda g: (g, 0, 0)),
        ]
        + [pl.BlockSpec(memory_space=pl.ANY)] * len(packs),
        out_specs=[pl.BlockSpec((3, HEADS_STEP * HEAD_DIM, length), lambda g: (0, g, 0))]
        + [pl.BlockSpec(pack.shape[-2:], lambda g: (0, 0)) for pack in packs],
        out_shape=[jax.ShapeDtypeStruct((3, width, length), jnp.bfloat16)]
        + [jax.ShapeDtypeStruct(pack.shape[-2:], jnp.float32) for pack in packs],
        scratch_shapes=scratch,
        compiler_params=pltpu.CompilerParams(
            collective_id=2, has_side_effects=True, vmem_limit_bytes=56 << 20
        ),
        name="attention_backward",
    )(queries, key_heads, values, attended, grads, probs, inverse, *packs)


def bit_of(index, bit):
    return lax.rem(lax.div(index, 1 << bit), 2)


def flipped(index, bit):
    return index + (1 - 2 * bit_of(index, bit)) * (1 << bit)


def spans_of(rows):
    first = (rows + 31) // 32 * 16
    return ((0, first), (first, rows - first))


class Shares:
    def __init__(self, pack, out, refs):
        self.pack, self.out = pack, out
        self.groups = pack.shape[0]
        self.bits = len(pack.shape) - 3
        self.spans = spans_of(pack.shape[-2])
        refs = list(refs)
        self.own, self.zero = refs[:2]
        count = self.bits - 1
        self.later = [refs[2 + half * count : 2 + (half + 1) * count] for half in range(2)]
        refs = refs[2 + 2 * count :]
        self.ring = refs[:2]
        self.local_sem, self.swap_send, self.swap_got, self.ring_send, self.ring_got = refs[2:]
        self.emb = lax.axis_index("emb")
        self.group = lax.axis_index("dp")
        self.every = (slice(None),) * self.bits

    def order(self, half):
        rest = list(range(1, self.bits))
        return [0] + (rest if half == 0 else rest[::-1])

    def span(self, half):
        return pl.ds(*self.spans[half])

    def place(self, half, stage, mine):
        order = self.order(half)
        index = []
        for bit in range(self.bits - 1, 0, -1):
            value = bit_of(self.emb, bit)
            if order.index(bit) < stage:
                index.append(value)
            elif order.index(bit) == stage:
                index.append(value if mine else 1 - value)
            else:
                index.append(slice(None))
        return tuple(index)

    def swap(self, half, stage):
        if stage == 0:
            other = 1 - bit_of(self.emb, 0)
            source = self.pack.at[self.every + (other, self.span(half))]
            target = self.zero.at[self.every + (self.span(half),)]
        else:
            place = self.place(half, stage, False)
            source = self.own.at[(slice(None),) + place + (self.span(half),)]
            target = self.later[half][stage - 1]
        return pltpu.make_async_remote_copy(
            src_ref=source,
            dst_ref=target,
            send_sem=self.swap_send.at[half, stage],
            recv_sem=self.swap_got.at[half, stage],
            device_id={"emb": flipped(self.emb, self.order(half)[stage])},
            device_id_type=MESH,
        )

    def bring(self, half):
        mine = bit_of(self.emb, 0)
        return pltpu.make_async_copy(
            self.pack.at[self.every + (mine, self.span(half))],
            self.own.at[self.every + (self.span(half),)],
            self.local_sem.at[half],
        )

    def hop(self, half, step):
        other = lax.rem(self.group + step, self.groups)
        place = (other,) + self.place(half, self.bits, True) + (self.span(half),)
        return pltpu.make_async_remote_copy(
            src_ref=self.own.at[place],
            dst_ref=self.ring[half].at[step - 1],
            send_sem=self.ring_send.at[half, step - 1],
            recv_sem=self.ring_got.at[half, step - 1],
            device_id={"dp": other},
            device_id_type=MESH,
        )

    def start(self):
        for half in range(2):
            self.swap(half, 0).start()
            self.bring(half).start()

    def take(self, stage):
        for half in range(2):
            self.take_half(half, stage)

    def take_half(self, half, stage):
        if stage == 0:
            self.bring(half).wait()
        self.swap(half, stage).wait()
        place = self.place(half, stage, True)
        free = [n for n, index in enumerate(place) if isinstance(index, slice)]

        def one(number, carry):
            group = lax.rem(number, self.groups)
            rest = lax.div(number, self.groups)
            index = list(place)
            there = []
            for n in free:
                index[n] = lax.rem(rest, 2)
                there.append(index[n])
                rest = lax.div(rest, 2)
            target = (group,) + tuple(index) + (self.span(half), slice(None))
            if stage == 0:
                arrived = self.zero[target]
            else:
                arrived = self.later[half][stage - 1][(group,) + tuple(there)]
            total = self.own[target].astype(jnp.float32) + arrived.astype(jnp.float32)
            self.own[target] = total.astype(jnp.bfloat16)
            return carry

        lax.fori_loop(0, self.groups * 2 ** len(free), one, 0)
        if stage + 1 < self.bits:
            self.swap(half, stage + 1).start()
        else:
            for step in range(1, self.groups):
                self.hop(half, step).start()

    def finish(self):
        for half in range(2):
            place = (self.group,) + self.place(half, self.bits, True)
            total = self.own[place + (self.span(half), slice(None))].astype(jnp.float32)
            for step in range(1, self.groups):
                self.hop(half, step).wait()
                total = total + self.ring[half][step - 1].astype(jnp.float32)
            self.out[self.span(half), :] = total


def shares_scratch(shape):
    groups, bits, columns = shape[0], len(shape) - 3, shape[-1]
    whole = pltpu.VMEM((groups,) + (2,) * (bits - 1) + shape[-2:], jnp.bfloat16)
    later = [
        pltpu.VMEM((groups,) + (2,) * (bits - 1 - stage) + (span[1], columns), jnp.bfloat16)
        for span in spans_of(shape[-2])
        for stage in range(1, bits)
    ]
    ring = [
        pltpu.VMEM((groups - 1, span[1], columns), jnp.bfloat16) for span in spans_of(shape[-2])
    ]
    semaphores = [(2,), (2, bits), (2, bits), (2, groups - 1), (2, groups - 1)]
    return [whole, whole, *later, *ring] + [pltpu.SemaphoreType.DMA(size) for size in semaphores]


def shares_of(packs, outs, refs):
    bits = len(packs[0].shape) - 3
    each = 2 + 2 * (bits - 1) + 2 + 5
    return [
        Shares(pack, out, refs[n * each : (n + 1) * each])
        for n, (pack, out) in enumerate(zip(packs, outs))
    ]


def greet(everyone):
    emb, group = lax.axis_index("emb"), lax.axis_index("dp")
    owners, groups = lax.axis_size("emb"), lax.axis_size("dp")
    barrier = pltpu.get_barrier_semaphore()
    if everyone:
        others = [lax.rem(emb + step, owners) for step in range(1, owners)]
    else:
        others = [flipped(emb, bit) for bit in range(owners.bit_length() - 1)]
    for other in others:
        pl.semaphore_signal(barrier, inc=1, device_id={"emb": other}, device_id_type=MESH)
    for step in range(1, groups):
        other = lax.rem(group + step, groups)
        pl.semaphore_signal(barrier, inc=1, device_id={"dp": other}, device_id_type=MESH)
    pl.semaphore_wait(barrier, len(others) + groups - 1)


def blocks_of(array):
    owners, groups = lax.axis_size("emb"), lax.axis_size("dp")
    bits = owners.bit_length() - 1
    return array.reshape((groups,) + (2,) * bits + array.shape[1:])


def rows_of(array):
    devices = lax.axis_size("emb") * lax.axis_size("dp")
    return array.astype(jnp.bfloat16).reshape(devices, array.shape[0] // devices, array.shape[1])


def stacked(pieces):
    rows = sum(piece.shape[1] for piece in pieces)
    devices, _, columns = pieces[0].shape
    spare = -rows % 16
    if rows + spare < 32:
        spare = 32 - rows
    if spare:
        pieces = pieces + [jnp.zeros((devices, spare, columns), jnp.bfloat16)]
    return blocks_of(jnp.concatenate(pieces, 1))


def vector_rows(vectors, rows):
    devices = lax.axis_size("emb") * lax.axis_size("dp")
    wide = vectors[0].shape[0]
    piece = jnp.stack(vectors).astype(jnp.bfloat16).reshape(len(vectors), devices, -1)
    piece = jnp.swapaxes(piece, 0, 1).reshape(devices, 1, -1)
    return jnp.pad(piece, ((0, 0), (0, rows - 1), (0, wide - piece.shape[2])))


def table_scratch(groups, owners, columns, length, capacity):
    wide = groups * capacity
    return [
        pltpu.VMEM((groups, columns, length), jnp.bfloat16),
        pltpu.VMEM((owners, columns, wide), jnp.bfloat16),
        pltpu.VMEM((owners - 1, columns, wide), jnp.bfloat16),
        pltpu.SemaphoreType.DMA((1,)),
        pltpu.SemaphoreType.DMA((groups - 1,)),
        pltpu.SemaphoreType.DMA((groups - 1,)),
        pltpu.SemaphoreType.DMA((owners - 1,)),
        pltpu.SemaphoreType.DMA((owners - 1,)),
    ]


class Table:
    def __init__(self, grads, slots, ids, out, refs):
        self.grads, self.slots, self.ids, self.out = grads, slots, ids, out
        self.turned, self.packed, self.landed = refs[:3]
        self.local_sem, self.ring_send, self.ring_got, self.send, self.got = refs[3:]
        self.groups, self.columns, self.length = self.turned.shape
        self.owners, _, self.wide = self.packed.shape
        self.capacity = self.wide // self.groups
        self.emb = lax.axis_index("emb")
        self.group = lax.axis_index("dp")

    def bring(self):
        return pltpu.make_async_copy(
            self.grads.at[self.group], self.turned.at[0], self.local_sem.at[0]
        )

    def hop(self, step):
        other = lax.rem(self.group + step, self.groups)
        return pltpu.make_async_remote_copy(
            src_ref=self.grads.at[other],
            dst_ref=self.turned.at[step],
            send_sem=self.ring_send.at[step - 1],
            recv_sem=self.ring_got.at[step - 1],
            device_id={"dp": other},
            device_id_type=MESH,
        )

    def give(self, step):
        other = lax.rem(self.emb + step, self.owners)
        return pltpu.make_async_remote_copy(
            src_ref=self.packed.at[other],
            dst_ref=self.landed.at[step - 1],
            send_sem=self.send.at[step - 1],
            recv_sem=self.got.at[step - 1],
            device_id={"emb": other},
            device_id_type=MESH,
        )

    def start(self):
        self.bring().start()
        for step in range(1, self.groups):
            self.hop(step).start()

    def arrive(self):
        self.bring().wait()
        for step in range(1, self.groups):
            self.hop(step).wait()

    def sort(self, step):
        owner = lax.rem(self.emb + step, self.owners)
        lanes = lax.broadcasted_iota(jnp.int32, (self.length, 128), 1)
        tiles = []
        for tile in range(self.wide // 128):
            total = jnp.zeros((self.columns, 128), jnp.float32)
            for group in range(self.groups):
                low, high = group * self.capacity, (group + 1) * self.capacity
                if high <= tile * 128 or low >= (tile + 1) * 128:
                    continue
                source = lax.rem(self.group - group + self.groups, self.groups)
                slot = lanes + (tile * 128 - low)
                inside = (slot >= 0) & (slot < self.capacity)
                wanted = jnp.where(inside, slot + owner * self.capacity, -2)
                hot = jnp.where(wanted == self.slots[source], 1.0, 0.0).astype(jnp.bfloat16)
                total = total + product(self.turned[group], hot)
            tiles.append(total.astype(jnp.bfloat16))
        self.packed[owner] = jnp.concatenate(tiles, 1)
        return owner

    def add(self, step, first):
        source = lax.rem(self.emb - step + self.owners, self.owners)
        rows, columns = self.out.shape
        count = 6 if rows % 48 == 0 else 1
        block = rows // count
        chunk = self.packed[self.emb] if step == 0 else self.landed[step - 1]

        def one(number, carry):
            base = pl.multiple_of(number * block, 8)
            places = base + lax.broadcasted_iota(jnp.int32, (block, self.wide), 0)
            hot = jnp.where(places == self.ids[source], 1.0, 0.0).astype(jnp.bfloat16)
            part = product_right(hot, chunk)
            if not first:
                part = part + self.out[pl.ds(base, block), :]
            self.out[pl.ds(base, block), :] = part
            return carry

        lax.fori_loop(0, count, one, 0)


def tail_kernel(count, grads_ref, slots_ref, ids_ref, *refs):
    packs, table_out, outs = refs[:count], refs[count], refs[count + 1 : 2 * count + 1]
    refs = refs[2 * count + 1 :]
    table = Table(grads_ref, slots_ref, ids_ref, table_out, refs[:8])
    shares = shares_of(packs, outs, refs[8:])
    owners = table.owners
    greet(True)
    table.start()
    for share in shares:
        share.start()
    shares[0].take(0)
    shares[1].take(0)
    for stage in range(1, shares[0].bits):
        for share in shares:
            share.take(stage)
    table.arrive()
    for step in range(1, owners):
        table.sort(step)
        table.give(step).start()
    table.sort(0)
    table.add(0, True)
    for share in shares:
        share.finish()
    for step in range(1, owners):
        table.give(step).wait()
        table.add(step, False)


def tail(grads, slots, ids, packs, table_rows, capacity):
    groups, columns, length = grads.shape
    owners = ids.shape[0]
    anywhere = pl.BlockSpec(memory_space=pl.ANY)
    vmem = pl.BlockSpec(memory_space=pltpu.VMEM)
    scratch = table_scratch(groups, owners, columns, length, capacity)
    for pack in packs:
        scratch = scratch + shares_scratch(pack.shape)
    return pl.pallas_call(
        functools.partial(tail_kernel, len(packs)),
        in_specs=[anywhere, vmem, vmem] + [anywhere] * len(packs),
        out_specs=[vmem] * (1 + len(packs)),
        out_shape=[jax.ShapeDtypeStruct((table_rows, columns), jnp.float32)]
        + [jax.ShapeDtypeStruct(pack.shape[-2:], jnp.float32) for pack in packs],
        scratch_shapes=scratch,
        compiler_params=pltpu.CompilerParams(
            collective_id=3, has_side_effects=True, vmem_limit_bytes=56 << 20
        ),
        name="tail",
    )(grads, slots, ids, *packs)


def on_device(
    pixels,
    counts,
    token_ids,
    action_bins,
    patch_pos,
    token_table,
    pos_table,
    w_patch,
    w_res_a,
    w_res_b,
    gain_one,
    bias_one,
    w_q,
    w_k,
    w_v,
    w_o,
    gain_two,
    bias_two,
    w_up,
    w_down,
    cotangent,
):
    length = pixels.shape[0]
    model_width = w_q.shape[0]
    positions = jnp.arange(length)
    image_rows = positions < counts[0, 0]
    action_rows = positions >= length - counts[0, 1]
    table_rows = jnp.logical_not(image_rows)
    row_ids = jnp.where(action_rows, TEXT_VOCAB + action_bins, token_ids)
    rows_owned = token_table.shape[0]
    owners_total = lax.axis_size("emb")
    capacity = 3 * length // (2 * owners_total)
    owner_index = row_ids // rows_owned
    local_row = row_ids - owner_index * rows_owned
    owner_hot = (
        (owner_index[:, None] == jnp.arange(owners_total)[None, :]) & table_rows[:, None]
    ).astype(jnp.int32)
    earlier = jnp.cumsum(owner_hot, 0) - owner_hot
    rank_within = jnp.sum(earlier * owner_hot, 1)
    slot_index = jnp.where(
        table_rows, owner_index * capacity + rank_within, owners_total * capacity
    )
    request = (
        jnp.full((owners_total * capacity + 1,), -1, jnp.int32)
        .at[slot_index]
        .set(jnp.where(table_rows, local_row, -1))
    )
    received = lax.all_to_all(
        request[:-1].reshape(owners_total, capacity), "emb", split_axis=0, concat_axis=0, tiled=True
    )
    valid_slots = received >= 0
    local_ids = jnp.maximum(received, 0)
    fetched = jnp.where(valid_slots[..., None], token_table[local_ids], jnp.zeros((), jnp.bfloat16))
    returned = lax.all_to_all(fetched, "emb", split_axis=0, concat_axis=0, tiled=True)
    slot_safe = jnp.minimum(slot_index, owners_total * capacity - 1)
    table_embed = returned.reshape(owners_total * capacity, model_width)[slot_safe].astype(
        jnp.float32
    )
    patch_first = product(pixels, w_patch)
    first_low = patch_first.astype(jnp.bfloat16)
    res_inner = product(first_low, w_res_a)
    res_gelu, gelu_back_res = jax.vjp(jax.nn.gelu, res_inner)
    res_act = res_gelu.astype(jnp.bfloat16)
    res_mixed = product(res_act, w_res_b)
    position_hot = patch_pos[:, None] == jnp.arange(pos_table.shape[0])[None, :]
    position_embed = product(position_hot.astype(jnp.bfloat16), pos_table)
    image_embed = patch_first + res_mixed + position_embed
    embedded = jnp.where(image_rows[:, None], image_embed, table_embed)
    normed_one_f, norm_back_one = jax.vjp(
        norm_affine, embedded, gain_one.astype(jnp.float32), bias_one.astype(jnp.float32)
    )
    normed_one = normed_one_f.astype(jnp.bfloat16)
    queries = contract(w_q, normed_one, 0, 1).astype(jnp.bfloat16)
    key_heads = contract(w_k, normed_one, 0, 1).astype(jnp.bfloat16)
    value_heads = contract(w_v, normed_one, 0, 1).astype(jnp.bfloat16)
    attended, probs, inverse = attention_forward(queries, key_heads, value_heads)
    middle = embedded + product_left(attended, w_o)
    normed_two_f, norm_back_two = jax.vjp(
        norm_affine, middle, gain_two.astype(jnp.float32), bias_two.astype(jnp.float32)
    )
    normed_two = normed_two_f.astype(jnp.bfloat16)
    up_pre = product(normed_two, w_up)
    up_act, gelu_back_up = jax.vjp(jax.nn.gelu, up_pre)
    up_low = up_act.astype(jnp.bfloat16)
    output = (middle + product(up_low, w_down)).astype(jnp.bfloat16)
    grad_w_down = product_left(up_low, cotangent)
    (grad_up_pre,) = gelu_back_up(product_right(cotangent, w_down))
    grad_up = grad_up_pre.astype(jnp.bfloat16)
    grad_w_up = product_left(normed_two, grad_up).astype(jnp.bfloat16)
    devices = lax.axis_size("dp") * owners_total
    share = model_width // devices
    folds = grad_w_up.shape[1] // model_width
    folded = grad_w_up.reshape(devices, share, folds, model_width)
    folded = jnp.swapaxes(folded, 1, 2).reshape(devices, folds * share, model_width)
    grad_normed_two = product_right(grad_up, w_up)
    grad_middle_norm, grad_gain_two, grad_bias_two = norm_back_two(grad_normed_two)
    grad_middle = cotangent.astype(jnp.float32) + grad_middle_norm
    grad_branch = grad_middle.astype(jnp.bfloat16)
    grad_w_o = product(attended, grad_branch)
    grad_attended = product_right(w_o, grad_branch).astype(jnp.bfloat16)
    gains_two = vector_rows([grad_gain_two, grad_bias_two], 8)
    grad_heads, share_down, share_up = attention_backward(
        queries,
        key_heads,
        value_heads,
        attended,
        grad_attended,
        probs,
        inverse,
        [stacked([rows_of(grad_w_down)]), stacked([folded, rows_of(grad_w_o), gains_two])],
    )
    grad_heads = grad_heads.reshape(3 * model_width, length)
    grad_normed_one = product_left(grad_heads, jnp.concatenate([w_q.T, w_k.T, w_v.T], 0))
    grad_embed_norm, grad_gain_one, grad_bias_one = norm_back_one(grad_normed_one)
    gains_one = vector_rows([grad_gain_one, grad_bias_one], 8)
    grad_w_heads = [
        rows_of(contract(normed_one, grad_heads[n * model_width : (n + 1) * model_width], 0, 1))
        for n in range(3)
    ]
    grad_embedded = grad_middle + grad_embed_norm
    grad_low = grad_embedded.astype(jnp.bfloat16)
    groups = lax.axis_size("dp")
    columns = model_width // groups
    all_ids = lax.all_gather(received, "dp", axis=0, tiled=False)
    all_ids = jnp.swapaxes(all_ids, 0, 1)
    turned = (groups - jnp.arange(groups) + lax.axis_index("dp")) % groups
    all_ids = all_ids[:, turned].reshape(owners_total, 1, groups * capacity)
    all_slots = lax.all_gather(slot_index, "dp", axis=0, tiled=False)[:, :, None]
    grads_turned = grad_low.T.reshape(groups, columns, length)
    grad_image = jnp.where(image_rows[:, None], grad_embedded, 0.0)
    grad_mixed = grad_image.astype(jnp.bfloat16)
    grad_pos_table = product_left(position_hot.astype(jnp.bfloat16), grad_mixed)
    grad_w_res_b = product_left(res_act, grad_mixed)
    (grad_inner_f,) = gelu_back_res(product_right(grad_mixed, w_res_b))
    grad_inner = grad_inner_f.astype(jnp.bfloat16)
    grad_w_res_a = product_left(first_low, grad_inner)
    grad_first = (grad_image + product_right(grad_inner, w_res_a)).astype(jnp.bfloat16)
    grad_w_patch = product_left(pixels, grad_first)
    grad_pixels = product_right(grad_first, w_patch)
    res_rows = [rows_of(g) for g in (grad_w_patch, grad_w_res_a, grad_w_res_b, grad_pos_table)]
    grad_table, share_heads, share_res = tail(
        grads_turned,
        all_slots,
        all_ids,
        [stacked(grad_w_heads + [gains_one]), stacked(res_rows)],
        rows_owned,
        capacity,
    )
    pos_share = pos_table.shape[0] // devices
    wide = folds * share

    def cut(array, place):
        return array[place * share : (place + 1) * share]

    share_w_up = jnp.swapaxes(share_up[:wide].reshape(folds, share, model_width), 0, 1)
    gains_two = share_up[wide + share, : 2 * share]
    gains_one = share_heads[3 * share, : 2 * share]
    return (
        output,
        grad_pixels,
        grad_table,
        share_res[3 * share : 3 * share + pos_share],
        cut(share_res, 0),
        cut(share_res, 1),
        cut(share_res, 2),
        gains_one[:share],
        gains_one[share:],
        cut(share_heads, 0),
        cut(share_heads, 1),
        cut(share_heads, 2),
        share_up[wide : wide + share],
        gains_two[:share],
        gains_two[share:],
        share_w_up.reshape(share, folds * model_width),
        share_down[: grad_w_down.shape[0] // devices],
    )


def solution(mesh):
    in_specs = (
        P(("dp", "emb"), None),
        P(("dp", "emb"), None),
        P(("dp", "emb")),
        P(("dp", "emb")),
        P(("dp", "emb")),
        P("emb", None),
        P(),
        P(),
        P(),
        P(),
        P(),
        P(),
        P(),
        P(),
        P(),
        P(),
        P(),
        P(),
        P(),
        P(),
        P(("dp", "emb"), None),
    )
    out_specs = (
        P(("dp", "emb"), None),
        P(("dp", "emb"), None),
        P("emb", "dp"),
        P(("dp", "emb"), None),
        P(("dp", "emb"), None),
        P(("dp", "emb"), None),
        P(("dp", "emb"), None),
        P(("dp", "emb")),
        P(("dp", "emb")),
        P(("dp", "emb"), None),
        P(("dp", "emb"), None),
        P(("dp", "emb"), None),
        P(("dp", "emb"), None),
        P(("dp", "emb")),
        P(("dp", "emb")),
        P(("dp", "emb"), None),
        P(("dp", "emb"), None),
    )
    return jax.shard_map(
        on_device, mesh=mesh, in_specs=in_specs, out_specs=out_specs, check_vma=False
    )
```

```python
import functools

import jax
import jax.numpy as jnp
from jax import lax
from jax.experimental import pallas as pl
from jax.experimental.pallas import tpu as pltpu
from jax.sharding import PartitionSpec as P

HEAD_DIM = 32
TEXT_VOCAB = 32000
BLOCK = 256
HEADS_STEP = 2
MESH = pl.DeviceIdType.MESH
LOG2_E = 1.4426950408889634


def normalize(values):
    average = jnp.mean(values, -1, keepdims=True)
    centred = values - average
    variance = jnp.mean(centred * centred, -1, keepdims=True)
    return centred * lax.rsqrt(variance + 1e-05)


def norm_affine(values, gain, offset):
    return normalize(values) * gain + offset


def contract(left, right, left_dim, right_dim):
    return lax.dot_general(
        left, right, (((left_dim,), (right_dim,)), ((), ())), preferred_element_type=jnp.float32
    )


def product(left, right):
    return contract(left, right, 1, 0)


def product_left(left, right):
    return contract(left, right, 0, 0)


def product_right(left, right):
    return contract(left, right, 1, 1)


def forward_kernel(heads, q_ref, k_ref, v_ref, o_ref, p_ref, r_ref):
    length = q_ref.shape[1]
    scaling = HEAD_DIM ** (-0.5) * LOG2_E
    key_place = lax.broadcasted_iota(jnp.int32, (BLOCK, BLOCK), 0)
    query_place = lax.broadcasted_iota(jnp.int32, (BLOCK, BLOCK), 1)
    allowed = key_place <= query_place
    for head in range(heads):
        rows = slice(head * HEAD_DIM, (head + 1) * HEAD_DIM)
        keys = k_ref[rows, :]
        values = v_ref[rows, :]
        for step in range(length // BLOCK):
            start, end = step * BLOCK, (step + 1) * BLOCK
            scores = contract(keys[:, :end], q_ref[rows, start:end], 0, 0) * scaling
            corner = jnp.where(allowed, scores[start:], -1e30)
            highest = jnp.max(corner, 0, keepdims=True)
            if step:
                highest = jnp.maximum(highest, jnp.max(scores[:start], 0, keepdims=True))
            weights = jnp.exp2(corner - highest)
            total = jnp.sum(weights, 0, keepdims=True)
            weights = weights.astype(jnp.bfloat16)
            if step:
                above = jnp.exp2(scores[:start] - highest)
                total = total + jnp.sum(above, 0, keepdims=True)
                weights = jnp.concatenate([above.astype(jnp.bfloat16), weights], 0)
            inverse = 1.0 / total
            base = BLOCK * (step * (step + 1) // 2)
            p_ref[head, base : base + end, :] = weights
            r_ref[head, :, start:end] = inverse
            o_ref[rows, start:end] = (
                contract(values[:, :end], weights, 1, 0) * inverse
            ).astype(jnp.bfloat16)


def packed_rows(length):
    steps = length // BLOCK
    return BLOCK * (steps * (steps + 1) // 2)


def attention_forward(queries, key_heads, values):
    width, length = queries.shape
    heads = width // HEAD_DIM
    packed = packed_rows(length)
    rows = pl.BlockSpec((HEADS_STEP * HEAD_DIM, length), lambda g: (g, 0))
    return pl.pallas_call(
        functools.partial(forward_kernel, HEADS_STEP),
        grid=(heads // HEADS_STEP,),
        in_specs=[rows] * 3,
        out_specs=[
            rows,
            pl.BlockSpec((HEADS_STEP, packed, BLOCK), lambda g: (g, 0, 0)),
            pl.BlockSpec((HEADS_STEP, 1, length), lambda g: (g, 0, 0)),
        ],
        out_shape=[
            jax.ShapeDtypeStruct((width, length), jnp.bfloat16),
            jax.ShapeDtypeStruct((heads, packed, BLOCK), jnp.bfloat16),
            jax.ShapeDtypeStruct((heads, 1, length), jnp.float32),
        ],
        compiler_params=pltpu.CompilerParams(vmem_limit_bytes=32 << 20),
        cost_estimate=pl.CostEstimate(
            flops=50_000_000_000, bytes_accessed=heads * packed * BLOCK * 2, transcendentals=0
        ),
        name="attention_forward",
    )(queries, key_heads, values)


def backward_kernel(heads, count, q_ref, k_ref, v_ref, o_ref, g_ref, p_ref, r_ref, *refs):
    packs, d_ref, outs = refs[:count], refs[count], refs[count + 1 : 2 * count + 1]
    s_ref = refs[2 * count + 1]
    shares = shares_of(packs, outs, refs[2 * count + 2 :])
    bits = shares[0].bits
    first, second = shares
    number = pl.program_id(0)
    last = pl.num_programs(0) - 1

    @pl.when(number == 0)
    def begin():
        greet(False)
        first.start()
        second.start()

    @pl.when(number == 2)
    def begin_first():
        first.take(0)

    @pl.when(number == 5)
    def begin_second():
        first.take(1)
        second.take(0)

    @pl.when(number == 8)
    def go_on():
        for stage in range(2, bits):
            first.take(stage)

    length = q_ref.shape[1]
    steps = length // BLOCK
    scaling = HEAD_DIM ** (-0.5)
    for head in range(heads):
        rows = slice(head * HEAD_DIM, (head + 1) * HEAD_DIM)
        grads = (g_ref[rows, :].astype(jnp.float32) * r_ref[head]).astype(jnp.bfloat16)
        inner = jnp.sum(
            grads.astype(jnp.float32) * o_ref[rows, :].astype(jnp.float32), 0, keepdims=True
        )
        queries = q_ref[rows, :]
        keys = k_ref[rows, :]
        values = v_ref[rows, :]
        for step in range(steps):
            start, end = step * BLOCK, (step + 1) * BLOCK
            base = BLOCK * (step * (step + 1) // 2)
            grad_probs = contract(values[:, :end], grads[:, start:end], 0, 0)
            grad_scores = p_ref[head, base : base + end, :] * (
                grad_probs - inner[:, start:end]
            ).astype(jnp.bfloat16)
            s_ref[head, base : base + end, :] = grad_scores
            d_ref[0, rows, start:end] = (
                contract(keys[:, :end], grad_scores, 1, 0) * scaling
            ).astype(jnp.bfloat16)
        for column in range(steps):
            grad_keys = jnp.zeros((HEAD_DIM, BLOCK), jnp.float32)
            grad_values = jnp.zeros((HEAD_DIM, BLOCK), jnp.float32)
            for step in range(column, steps):
                base = BLOCK * (step * (step + 1) // 2 + column)
                span = slice(step * BLOCK, (step + 1) * BLOCK)
                grad_values = grad_values + contract(
                    grads[:, span], p_ref[head, base : base + BLOCK, :], 1, 1
                )
                grad_keys = grad_keys + contract(
                    queries[:, span], s_ref[head, base : base + BLOCK, :], 1, 1
                )
            span = slice(column * BLOCK, (column + 1) * BLOCK)
            d_ref[1, rows, span] = (grad_keys * scaling).astype(jnp.bfloat16)
            d_ref[2, rows, span] = grad_values.astype(jnp.bfloat16)

    @pl.when(number == last)
    def end():
        for stage in range(1, bits):
            second.take(stage)
        first.finish()
        second.finish()


def attention_backward(queries, key_heads, values, attended, grads, probs, inverse, packs):
    width, length = queries.shape
    heads = width // HEAD_DIM
    packed = packed_rows(length)
    rows = pl.BlockSpec((HEADS_STEP * HEAD_DIM, length), lambda g: (g, 0))
    scratch = [pltpu.VMEM((HEADS_STEP, packed, BLOCK), jnp.bfloat16)]
    for pack in packs:
        scratch = scratch + shares_scratch(pack.shape)
    return pl.pallas_call(
        functools.partial(backward_kernel, HEADS_STEP, len(packs)),
        grid=(heads // HEADS_STEP,),
        in_specs=[rows] * 5
        + [
            pl.BlockSpec((HEADS_STEP, packed, BLOCK), lambda g: (g, 0, 0)),
            pl.BlockSpec((HEADS_STEP, 1, length), lambda g: (g, 0, 0)),
        ]
        + [pl.BlockSpec(memory_space=pl.ANY)] * len(packs),
        out_specs=[pl.BlockSpec((3, HEADS_STEP * HEAD_DIM, length), lambda g: (0, g, 0))]
        + [pl.BlockSpec(pack.shape[-2:], lambda g: (0, 0)) for pack in packs],
        out_shape=[jax.ShapeDtypeStruct((3, width, length), jnp.bfloat16)]
        + [jax.ShapeDtypeStruct(pack.shape[-2:], jnp.float32) for pack in packs],
        scratch_shapes=scratch,
        compiler_params=pltpu.CompilerParams(
            collective_id=2, has_side_effects=True, vmem_limit_bytes=56 << 20
        ),
        name="attention_backward",
    )(queries, key_heads, values, attended, grads, probs, inverse, *packs)


def bit_of(index, bit):
    return lax.rem(lax.div(index, 1 << bit), 2)


def flipped(index, bit):
    return index + (1 - 2 * bit_of(index, bit)) * (1 << bit)


def spans_of(rows):
    first = (rows + 31) // 32 * 16
    return ((0, first), (first, rows - first))


class Shares:
    def __init__(self, pack, out, refs):
        self.pack, self.out = pack, out
        self.groups = pack.shape[0]
        self.bits = len(pack.shape) - 3
        self.spans = spans_of(pack.shape[-2])
        refs = list(refs)
        self.own, self.zero = refs[:2]
        count = self.bits - 1
        self.later = [refs[2 + half * count : 2 + (half + 1) * count] for half in range(2)]
        refs = refs[2 + 2 * count :]
        self.ring = refs[:2]
        self.local_sem, self.swap_send, self.swap_got, self.ring_send, self.ring_got = refs[2:]
        self.emb = lax.axis_index("emb")
        self.group = lax.axis_index("dp")
        self.every = (slice(None),) * self.bits

    def order(self, half):
        rest = list(range(1, self.bits))
        return [0] + (rest if half == 0 else rest[::-1])

    def span(self, half):
        return pl.ds(*self.spans[half])

    def place(self, half, stage, mine):
        order = self.order(half)
        index = []
        for bit in range(self.bits - 1, 0, -1):
            value = bit_of(self.emb, bit)
            if order.index(bit) < stage:
                index.append(value)
            elif order.index(bit) == stage:
                index.append(value if mine else 1 - value)
            else:
                index.append(slice(None))
        return tuple(index)

    def swap(self, half, stage):
        if stage == 0:
            other = 1 - bit_of(self.emb, 0)
            source = self.pack.at[self.every + (other, self.span(half))]
            target = self.zero.at[self.every + (self.span(half),)]
        else:
            place = self.place(half, stage, False)
            source = self.own.at[(slice(None),) + place + (self.span(half),)]
            target = self.later[half][stage - 1]
        return pltpu.make_async_remote_copy(
            src_ref=source,
            dst_ref=target,
            send_sem=self.swap_send.at[half, stage],
            recv_sem=self.swap_got.at[half, stage],
            device_id={"emb": flipped(self.emb, self.order(half)[stage])},
            device_id_type=MESH,
        )

    def bring(self, half):
        mine = bit_of(self.emb, 0)
        return pltpu.make_async_copy(
            self.pack.at[self.every + (mine, self.span(half))],
            self.own.at[self.every + (self.span(half),)],
            self.local_sem.at[half],
        )

    def hop(self, half, step):
        other = lax.rem(self.group + step, self.groups)
        place = (other,) + self.place(half, self.bits, True) + (self.span(half),)
        return pltpu.make_async_remote_copy(
            src_ref=self.own.at[place],
            dst_ref=self.ring[half].at[step - 1],
            send_sem=self.ring_send.at[half, step - 1],
            recv_sem=self.ring_got.at[half, step - 1],
            device_id={"dp": other},
            device_id_type=MESH,
        )

    def start(self):
        for half in range(2):
            self.swap(half, 0).start()
            self.bring(half).start()

    def take(self, stage):
        for half in range(2):
            self.take_half(half, stage)

    def take_half(self, half, stage):
        if stage == 0:
            self.bring(half).wait()
        self.swap(half, stage).wait()
        place = self.place(half, stage, True)
        free = [n for n, index in enumerate(place) if isinstance(index, slice)]

        def one(number, carry):
            group = lax.rem(number, self.groups)
            rest = lax.div(number, self.groups)
            index = list(place)
            there = []
            for n in free:
                index[n] = lax.rem(rest, 2)
                there.append(index[n])
                rest = lax.div(rest, 2)
            target = (group,) + tuple(index) + (self.span(half), slice(None))
            if stage == 0:
                arrived = self.zero[target]
            else:
                arrived = self.later[half][stage - 1][(group,) + tuple(there)]
            total = self.own[target].astype(jnp.float32) + arrived.astype(jnp.float32)
            self.own[target] = total.astype(jnp.bfloat16)
            return carry

        lax.fori_loop(0, self.groups * 2 ** len(free), one, 0)
        if stage + 1 < self.bits:
            self.swap(half, stage + 1).start()
        else:
            for step in range(1, self.groups):
                self.hop(half, step).start()

    def finish(self):
        for half in range(2):
            place = (self.group,) + self.place(half, self.bits, True)
            total = self.own[place + (self.span(half), slice(None))].astype(jnp.float32)
            for step in range(1, self.groups):
                self.hop(half, step).wait()
                total = total + self.ring[half][step - 1].astype(jnp.float32)
            self.out[self.span(half), :] = total


def shares_scratch(shape):
    groups, bits, columns = shape[0], len(shape) - 3, shape[-1]
    whole = pltpu.VMEM((groups,) + (2,) * (bits - 1) + shape[-2:], jnp.bfloat16)
    later = [
        pltpu.VMEM((groups,) + (2,) * (bits - 1 - stage) + (span[1], columns), jnp.bfloat16)
        for span in spans_of(shape[-2])
        for stage in range(1, bits)
    ]
    ring = [
        pltpu.VMEM((groups - 1, span[1], columns), jnp.bfloat16) for span in spans_of(shape[-2])
    ]
    semaphores = [(2,), (2, bits), (2, bits), (2, groups - 1), (2, groups - 1)]
    return [whole, whole, *later, *ring] + [pltpu.SemaphoreType.DMA(size) for size in semaphores]


def shares_of(packs, outs, refs):
    bits = len(packs[0].shape) - 3
    each = 2 + 2 * (bits - 1) + 2 + 5
    return [
        Shares(pack, out, refs[n * each : (n + 1) * each])
        for n, (pack, out) in enumerate(zip(packs, outs))
    ]


def greet(everyone):
    emb, group = lax.axis_index("emb"), lax.axis_index("dp")
    owners, groups = lax.axis_size("emb"), lax.axis_size("dp")
    barrier = pltpu.get_barrier_semaphore()
    if everyone:
        others = [lax.rem(emb + step, owners) for step in range(1, owners)]
    else:
        others = [flipped(emb, bit) for bit in range(owners.bit_length() - 1)]
    for other in others:
        pl.semaphore_signal(barrier, inc=1, device_id={"emb": other}, device_id_type=MESH)
    for step in range(1, groups):
        other = lax.rem(group + step, groups)
        pl.semaphore_signal(barrier, inc=1, device_id={"dp": other}, device_id_type=MESH)
    pl.semaphore_wait(barrier, len(others) + groups - 1)


def blocks_of(array):
    owners, groups = lax.axis_size("emb"), lax.axis_size("dp")
    bits = owners.bit_length() - 1
    return array.reshape((groups,) + (2,) * bits + array.shape[1:])


def rows_of(array):
    devices = lax.axis_size("emb") * lax.axis_size("dp")
    return array.astype(jnp.bfloat16).reshape(devices, array.shape[0] // devices, array.shape[1])


def stacked(pieces):
    rows = sum(piece.shape[1] for piece in pieces)
    devices, _, columns = pieces[0].shape
    spare = -rows % 16
    if rows + spare < 32:
        spare = 32 - rows
    if spare:
        pieces = pieces + [jnp.zeros((devices, spare, columns), jnp.bfloat16)]
    return blocks_of(jnp.concatenate(pieces, 1))


def vector_rows(vectors, rows):
    devices = lax.axis_size("emb") * lax.axis_size("dp")
    wide = vectors[0].shape[0]
    piece = jnp.stack(vectors).astype(jnp.bfloat16).reshape(len(vectors), devices, -1)
    piece = jnp.swapaxes(piece, 0, 1).reshape(devices, 1, -1)
    return jnp.pad(piece, ((0, 0), (0, rows - 1), (0, wide - piece.shape[2])))


def table_scratch(groups, owners, columns, length, capacity):
    wide = groups * capacity
    return [
        pltpu.VMEM((groups, columns, length), jnp.bfloat16),
        pltpu.VMEM((owners, columns, wide), jnp.bfloat16),
        pltpu.VMEM((owners - 1, columns, wide), jnp.bfloat16),
        pltpu.SemaphoreType.DMA((1,)),
        pltpu.SemaphoreType.DMA((groups - 1,)),
        pltpu.SemaphoreType.DMA((groups - 1,)),
        pltpu.SemaphoreType.DMA((owners - 1,)),
        pltpu.SemaphoreType.DMA((owners - 1,)),
    ]


class Table:
    def __init__(self, grads, slots, ids, out, refs):
        self.grads, self.slots, self.ids, self.out = grads, slots, ids, out
        self.turned, self.packed, self.landed = refs[:3]
        self.local_sem, self.ring_send, self.ring_got, self.send, self.got = refs[3:]
        self.groups, self.columns, self.length = self.turned.shape
        self.owners, _, self.wide = self.packed.shape
        self.capacity = self.wide // self.groups
        self.emb = lax.axis_index("emb")
        self.group = lax.axis_index("dp")

    def bring(self):
        return pltpu.make_async_copy(
            self.grads.at[self.group], self.turned.at[0], self.local_sem.at[0]
        )

    def hop(self, step):
        other = lax.rem(self.group + step, self.groups)
        return pltpu.make_async_remote_copy(
            src_ref=self.grads.at[other],
            dst_ref=self.turned.at[step],
            send_sem=self.ring_send.at[step - 1],
            recv_sem=self.ring_got.at[step - 1],
            device_id={"dp": other},
            device_id_type=MESH,
        )

    def give(self, step):
        other = lax.rem(self.emb + step, self.owners)
        return pltpu.make_async_remote_copy(
            src_ref=self.packed.at[other],
            dst_ref=self.landed.at[step - 1],
            send_sem=self.send.at[step - 1],
            recv_sem=self.got.at[step - 1],
            device_id={"emb": other},
            device_id_type=MESH,
        )

    def start(self):
        self.bring().start()
        for step in range(1, self.groups):
            self.hop(step).start()

    def arrive(self):
        self.bring().wait()
        for step in range(1, self.groups):
            self.hop(step).wait()

    def sort(self, step):
        owner = lax.rem(self.emb + step, self.owners)
        rows = lax.broadcasted_iota(jnp.int32, (128, self.length), 0)
        tiles = []
        for tile in range(self.wide // 128):
            total = jnp.zeros((self.columns, 128), jnp.float32)
            for group in range(self.groups):
                low, high = group * self.capacity, (group + 1) * self.capacity
                if high <= tile * 128 or low >= (tile + 1) * 128:
                    continue
                slot = rows + (tile * 128 - low)
                inside = (slot >= 0) & (slot < self.capacity)
                wanted = jnp.where(inside, slot + owner * self.capacity, -2)
                hot = jnp.where(wanted == self.slots[group], 1.0, 0.0).astype(jnp.bfloat16)
                total = total + product_right(self.turned[group], hot)
            tiles.append(total.astype(jnp.bfloat16))
        self.packed[owner] = jnp.concatenate(tiles, 1)
        return owner

    def add(self, step, first):
        source = lax.rem(self.emb - step + self.owners, self.owners)
        rows, columns = self.out.shape
        count = 6 if rows % 48 == 0 else 1
        block = rows // count
        chunk = self.packed[self.emb] if step == 0 else self.landed[step - 1]

        def one(number, carry):
            base = pl.multiple_of(number * block, 8)
            places = base + lax.broadcasted_iota(jnp.int32, (block, self.wide), 0)
            hot = jnp.where(places == self.ids[source], 1.0, 0.0).astype(jnp.bfloat16)
            part = product_right(hot, chunk)
            if not first:
                part = part + self.out[pl.ds(base, block), :]
            self.out[pl.ds(base, block), :] = part
            return carry

        lax.fori_loop(0, count, one, 0)


def tail_kernel(count, grads_ref, slots_ref, ids_ref, *refs):
    packs, table_out, outs = refs[:count], refs[count], refs[count + 1 : 2 * count + 1]
    refs = refs[2 * count + 1 :]
    table = Table(grads_ref, slots_ref, ids_ref, table_out, refs[:8])
    shares = shares_of(packs, outs, refs[8:])
    owners = table.owners
    greet(True)
    table.start()
    for share in shares:
        share.start()
    shares[0].take(0)
    shares[1].take(0)
    for stage in range(1, shares[0].bits):
        for share in shares:
            share.take(stage)
    table.arrive()
    for step in range(1, owners):
        table.sort(step)
        table.give(step).start()
    table.sort(0)
    table.add(0, True)
    for share in shares:
        share.finish()
    for step in range(1, owners):
        table.give(step).wait()
        table.add(step, False)


def tail(grads, slots, ids, packs, table_rows, capacity):
    groups, columns, length = grads.shape
    owners = ids.shape[0]
    anywhere = pl.BlockSpec(memory_space=pl.ANY)
    vmem = pl.BlockSpec(memory_space=pltpu.VMEM)
    scratch = table_scratch(groups, owners, columns, length, capacity)
    for pack in packs:
        scratch = scratch + shares_scratch(pack.shape)
    return pl.pallas_call(
        functools.partial(tail_kernel, len(packs)),
        in_specs=[anywhere, vmem, vmem] + [anywhere] * len(packs),
        out_specs=[vmem] * (1 + len(packs)),
        out_shape=[jax.ShapeDtypeStruct((table_rows, columns), jnp.float32)]
        + [jax.ShapeDtypeStruct(pack.shape[-2:], jnp.float32) for pack in packs],
        scratch_shapes=scratch,
        compiler_params=pltpu.CompilerParams(
            collective_id=3, has_side_effects=True, vmem_limit_bytes=56 << 20
        ),
        name="tail",
    )(grads, slots, ids, *packs)


def column_of(row, rows):
    diagonal = lax.broadcasted_iota(jnp.int32, (128, 128), 0) == lax.broadcasted_iota(
        jnp.int32, (128, 128), 1
    )
    pieces = [
        jnp.sum(jnp.where(diagonal, row[:, start : start + 128], 0), 1, keepdims=True)
        for start in range(0, rows, 128)
    ]
    return jnp.concatenate(pieces, 0)


def gelu_pair(value):
    root = 0.7978845608028654
    square = value * value
    bend = jnp.tanh(root * (value + 0.044715 * (value * square)))
    half = 0.5 * (1.0 + bend)
    slope = half + 0.5 * value * (1.0 - bend * bend) * (root * (1.0 + 3 * 0.044715 * square))
    return value * half, slope


def front_kernel(
    counts_ref,
    codes_ref,
    place_ref,
    pixels_ref,
    table_ref,
    pos_ref,
    w_patch_ref,
    w_a_ref,
    w_b_ref,
    gain_ref,
    bias_ref,
    embedded_ref,
    normed_ref,
    first_ref,
    act_ref,
    slope_ref,
    ids_ref,
    slots_ref,
    codes_all,
    ranks,
    earlier,
    held,
    packed,
    landed,
    fetched,
    mixed,
    local_sem,
    ask_send,
    ask_got,
    send,
    got,
):
    owners, capacity, width = packed.shape
    length = codes_ref.shape[1]
    table_rows = held.shape[0]
    emb = lax.axis_index("emb")
    bring = pltpu.make_async_copy(table_ref, held, local_sem.at[0])
    bring.start()
    barrier = pltpu.get_barrier_semaphore()
    for step in range(1, owners):
        other = lax.rem(emb + step, owners)
        pl.semaphore_signal(barrier, inc=1, device_id={"emb": other}, device_id_type=MESH)
    pl.semaphore_wait(barrier, owners - 1)

    def ask(step):
        return pltpu.make_async_remote_copy(
            src_ref=codes_ref,
            dst_ref=codes_all.at[step],
            send_sem=ask_send.at[step - 1],
            recv_sem=ask_got.at[step - 1],
            device_id={"emb": lax.rem(emb + step, owners)},
            device_id_type=MESH,
        )

    def give(step):
        return pltpu.make_async_remote_copy(
            src_ref=packed.at[step],
            dst_ref=landed.at[step - 1],
            send_sem=send.at[step - 1],
            recv_sem=got.at[step - 1],
            device_id={"emb": lax.rem(emb - step + owners, owners)},
            device_id_type=MESH,
        )

    for step in range(1, owners):
        ask(step).start()
    codes_all[0] = codes_ref[...]
    block = min(256, length)

    def triangle(number, carry):
        base = pl.multiple_of(number * block, block)
        above = base + lax.broadcasted_iota(jnp.int32, (block, length), 0)
        below = lax.broadcasted_iota(jnp.int32, (block, length), 1)
        earlier[pl.ds(base, block), :] = jnp.where(above < below, 1.0, 0.0).astype(jnp.bfloat16)
        return carry

    lax.fori_loop(0, length // block, triangle, 0)
    codes = codes_ref[...]
    mine = [
        (codes >= owner * table_rows) & (codes < (owner + 1) * table_rows)
        for owner in range(owners)
    ]
    marks = jnp.concatenate([jnp.where(mark, 1.0, 0.0) for mark in mine], 0)
    places = product(marks.astype(jnp.bfloat16), earlier[...])
    slots = jnp.full((1, length), owners * capacity, jnp.int32)
    for owner in range(owners):
        rank = places[owner : owner + 1].astype(jnp.int32)
        slots = jnp.where(mine[owner], owner * capacity + rank, slots)
    slots_ref[...] = slots
    for step in range(1, owners):
        ask(step).wait()
    local = codes_all[...].reshape(owners, length) - emb * table_rows
    inside = (local >= 0) & (local < table_rows)
    places = product(jnp.where(inside, 1.0, 0.0).astype(jnp.bfloat16), earlier[...])
    ranks[...] = jnp.where(inside, places.astype(jnp.int32), -1).reshape(owners, 1, length)
    bring.wait()

    def gather(step):
        rank = ranks[step]
        local = codes_all[step] - emb * table_rows + 1
        slot = lax.broadcasted_iota(jnp.int32, (capacity, length), 0)
        match = slot == rank
        hot = jnp.where(match, 1.0, 0.0).astype(jnp.bfloat16)
        coarse = lax.div(local, 64)
        fine = local - coarse * 64
        inner = rank >= 0
        pair = jnp.concatenate(
            [jnp.where(inner, coarse, 0), jnp.where(inner, fine, 0)]
            + [jnp.zeros((6, length), jnp.int32)],
            0,
        )
        pair = product_right(pair.astype(jnp.float32).astype(jnp.bfloat16), hot)
        source = lax.rem(emb - step + owners, owners)
        ids_ref[source] = (pair[0:1] * 64.0 + pair[1:2]).astype(jnp.int32) - 1
        wanted = jnp.sum(jnp.where(match, local, 0), 1, keepdims=True) - 1
        total = jnp.zeros((capacity, width), jnp.float32)
        for start in range(0, table_rows, 1024):
            size = min(1024, table_rows - start)
            row = start + lax.broadcasted_iota(jnp.int32, (capacity, size), 1)
            hot = jnp.where(row == wanted, 1.0, 0.0).astype(jnp.bfloat16)
            total = total + product(hot, held[start : start + size, :])
        packed[step] = total.astype(jnp.bfloat16)

    def serve(step, carry):
        gather(step)
        give(step).start()
        return carry

    lax.fori_loop(1, owners, serve, 0)
    gather(0)
    slot_column = column_of(slots, length)
    fetched[...] = jnp.zeros_like(fetched)

    def place_rows(step):
        owner = lax.rem(emb + step, owners)
        rows = packed[0] if step == 0 else landed[step - 1]
        for start in range(0, length, block):
            slot = owner * capacity + lax.broadcasted_iota(jnp.int32, (block, capacity), 1)
            hot = jnp.where(slot == slot_column[start : start + block], 1.0, 0.0)
            fetched[start : start + block, :] += product(hot.astype(jnp.bfloat16), rows)


    def patches(number, carry):
        base = pl.multiple_of(number * block, block)
        rows = pl.ds(base, block)
        first = product(pixels_ref[rows, :], w_patch_ref[...])
        low = first.astype(jnp.bfloat16)
        first_ref[rows, :] = low
        act, slope = gelu_pair(product(low, w_a_ref[...]))
        act = act.astype(jnp.bfloat16)
        act_ref[rows, :] = act
        slope_ref[rows, :] = slope.astype(jnp.bfloat16)
        mixed[rows, :] = first + product(act, w_b_ref[...])
        return carry

    lax.fori_loop(0, length // block, patches, 0)

    def positions(number, carry):
        base = pl.multiple_of(number * block, block)
        spot = lax.broadcasted_iota(jnp.int32, (block, pos_ref.shape[0]), 1)
        place = column_of(place_ref[:, pl.ds(base, block)], block)
        hot = jnp.where(spot == place, 1.0, 0.0).astype(jnp.bfloat16)
        embedded_ref[pl.ds(base, block), :] = product(hot, pos_ref[...])
        return carry

    lax.fori_loop(0, length // block, positions, 0)
    place_rows(0)
    for step in range(1, owners):
        give(step).wait()
        place_rows(step)

    def settle(number, carry):
        base = pl.multiple_of(number * block, block)
        rows = pl.ds(base, block)
        token = base + lax.broadcasted_iota(jnp.int32, (block, width), 0)
        image = mixed[rows, :] + embedded_ref[rows, :]
        value = jnp.where(token < counts_ref[0, 0], image, fetched[rows, :])
        embedded_ref[rows, :] = value
        normed = normalize(value) * gain_ref[...] + bias_ref[...]
        normed_ref[rows, :] = normed.astype(jnp.bfloat16)
        return carry

    lax.fori_loop(0, length // block, settle, 0)


def front(counts, codes, place, pixels, table, pos, w_patch, w_a, w_b, gain, bias, capacity):
    owners = lax.axis_size("emb")
    length, width = pixels.shape
    vmem = pl.BlockSpec(memory_space=pltpu.VMEM)
    low = jax.ShapeDtypeStruct((length, width), jnp.bfloat16)
    full = jax.ShapeDtypeStruct((length, width), jnp.float32)
    return pl.pallas_call(
        front_kernel,
        in_specs=[pl.BlockSpec(memory_space=pltpu.SMEM), vmem, vmem, vmem]
        + [pl.BlockSpec(memory_space=pl.ANY)]
        + [vmem] * 6,
        out_specs=[vmem] * 7,
        out_shape=[
            full,
            low,
            low,
            low,
            low,
            jax.ShapeDtypeStruct((owners, 1, capacity), jnp.int32),
            jax.ShapeDtypeStruct((1, length), jnp.int32),
        ],
        scratch_shapes=[
            pltpu.VMEM((owners, 1, length), jnp.int32),
            pltpu.VMEM((owners, 1, length), jnp.int32),
            pltpu.VMEM((length, length), jnp.bfloat16),
            pltpu.VMEM(table.shape, jnp.bfloat16),
            pltpu.VMEM((owners, capacity, width), jnp.bfloat16),
            pltpu.VMEM((owners - 1, capacity, width), jnp.bfloat16),
            pltpu.VMEM((length, width), jnp.float32),
            pltpu.VMEM((length, width), jnp.float32),
            pltpu.SemaphoreType.DMA((1,)),
            pltpu.SemaphoreType.DMA((owners - 1,)),
            pltpu.SemaphoreType.DMA((owners - 1,)),
            pltpu.SemaphoreType.DMA((owners - 1,)),
            pltpu.SemaphoreType.DMA((owners - 1,)),
        ],
        compiler_params=pltpu.CompilerParams(
            collective_id=1, has_side_effects=True, vmem_limit_bytes=56 << 20
        ),
        name="front",
    )(counts, codes, place, pixels, table, pos, w_patch, w_a, w_b, gain, bias)


def on_device(
    pixels,
    counts,
    token_ids,
    action_bins,
    patch_pos,
    token_table,
    pos_table,
    w_patch,
    w_res_a,
    w_res_b,
    gain_one,
    bias_one,
    w_q,
    w_k,
    w_v,
    w_o,
    gain_two,
    bias_two,
    w_up,
    w_down,
    cotangent,
):
    length = pixels.shape[0]
    model_width = w_q.shape[0]
    positions = jnp.arange(length)
    image_rows = positions < counts[0, 0]
    action_rows = positions >= length - counts[0, 1]
    table_rows = jnp.logical_not(image_rows)
    row_ids = jnp.where(action_rows, TEXT_VOCAB + action_bins, token_ids)
    rows_owned = token_table.shape[0]
    owners_total = lax.axis_size("emb")
    capacity = 3 * length // (2 * owners_total)
    groups = lax.axis_size("dp")
    codes = jnp.where(table_rows, row_ids, -1).reshape(1, length)
    gain_row = gain_one.astype(jnp.float32).reshape(1, model_width)
    bias_row = bias_one.astype(jnp.float32).reshape(1, model_width)
    embedded, normed_one, first_low, res_act, res_slope, ids, slots = front(
        counts,
        codes,
        patch_pos.reshape(1, length),
        pixels,
        token_table,
        pos_table,
        w_patch,
        w_res_a,
        w_res_b,
        gain_row,
        bias_row,
        capacity,
    )
    position_hot = patch_pos[:, None] == jnp.arange(pos_table.shape[0])[None, :]
    facts = jnp.concatenate([ids.reshape(-1), slots.reshape(-1)])
    ring = [facts] + [
        lax.ppermute(facts, "dp", [(i, (i + step) % groups) for i in range(groups)])
        for step in range(1, groups)
    ]
    ring = jnp.stack(ring)
    ring_ids = ring[:, : owners_total * capacity].reshape(groups, owners_total, capacity)
    ring_ids = jnp.swapaxes(ring_ids, 0, 1).reshape(owners_total, 1, groups * capacity)
    ring_slots = ring[:, owners_total * capacity :].reshape(groups, 1, length)
    _, norm_back_one = jax.vjp(
        norm_affine, embedded, gain_one.astype(jnp.float32), bias_one.astype(jnp.float32)
    )
    queries = contract(w_q, normed_one, 0, 1).astype(jnp.bfloat16)
    key_heads = contract(w_k, normed_one, 0, 1).astype(jnp.bfloat16)
    value_heads = contract(w_v, normed_one, 0, 1).astype(jnp.bfloat16)
    attended, probs, inverse = attention_forward(queries, key_heads, value_heads)
    middle = embedded + product_left(attended, w_o)
    normed_two_f, norm_back_two = jax.vjp(
        norm_affine, middle, gain_two.astype(jnp.float32), bias_two.astype(jnp.float32)
    )
    normed_two = normed_two_f.astype(jnp.bfloat16)
    up_pre = product(normed_two, w_up)
    up_act, gelu_back_up = jax.vjp(jax.nn.gelu, up_pre)
    up_low = up_act.astype(jnp.bfloat16)
    output = (middle + product(up_low, w_down)).astype(jnp.bfloat16)
    grad_w_down = product_left(up_low, cotangent)
    (grad_up_pre,) = gelu_back_up(product_right(cotangent, w_down))
    grad_up = grad_up_pre.astype(jnp.bfloat16)
    devices = lax.axis_size("dp") * owners_total
    share = model_width // devices
    folds = w_up.shape[1] // model_width
    folded = [
        rows_of(product_left(normed_two, grad_up[:, n * model_width : (n + 1) * model_width]))
        for n in range(folds)
    ]
    grad_normed_two = product_right(grad_up, w_up)
    grad_middle_norm, grad_gain_two, grad_bias_two = norm_back_two(grad_normed_two)
    grad_middle = cotangent.astype(jnp.float32) + grad_middle_norm
    grad_branch = grad_middle.astype(jnp.bfloat16)
    grad_w_o = product(attended, grad_branch)
    grad_attended = product_right(w_o, grad_branch).astype(jnp.bfloat16)
    gains_two = vector_rows([grad_gain_two, grad_bias_two], 8)
    grad_heads, share_down, share_up = attention_backward(
        queries,
        key_heads,
        value_heads,
        attended,
        grad_attended,
        probs,
        inverse,
        [stacked([rows_of(grad_w_down)]), stacked(folded + [rows_of(grad_w_o), gains_two])],
    )
    grad_heads = grad_heads.reshape(3 * model_width, length)
    grad_normed_one = product_left(grad_heads, jnp.concatenate([w_q.T, w_k.T, w_v.T], 0))
    grad_embed_norm, grad_gain_one, grad_bias_one = norm_back_one(grad_normed_one)
    gains_one = vector_rows([grad_gain_one, grad_bias_one], 8)
    grad_w_heads = [
        rows_of(contract(normed_one, grad_heads[n * model_width : (n + 1) * model_width], 0, 1))
        for n in range(3)
    ]
    grad_embedded = grad_middle + grad_embed_norm
    grad_low = grad_embedded.astype(jnp.bfloat16)
    columns = model_width // groups
    grads_turned = grad_low.T.reshape(groups, columns, length)
    grad_image = jnp.where(image_rows[:, None], grad_embedded, 0.0)
    grad_mixed = grad_image.astype(jnp.bfloat16)
    grad_pos_table = product_left(position_hot.astype(jnp.bfloat16), grad_mixed)
    grad_w_res_b = product_left(res_act, grad_mixed)
    grad_inner = product_right(grad_mixed, w_res_b) * res_slope.astype(jnp.float32)
    grad_inner = grad_inner.astype(jnp.bfloat16)
    grad_w_res_a = product_left(first_low, grad_inner)
    grad_first = (grad_image + product_right(grad_inner, w_res_a)).astype(jnp.bfloat16)
    grad_w_patch = product_left(pixels, grad_first)
    grad_pixels = product_right(grad_first, w_patch)
    res_rows = [rows_of(g) for g in (grad_w_patch, grad_w_res_a, grad_w_res_b, grad_pos_table)]
    grad_table, share_heads, share_res = tail(
        grads_turned,
        ring_slots,
        ring_ids,
        [stacked(grad_w_heads + [gains_one]), stacked(res_rows)],
        rows_owned,
        capacity,
    )
    pos_share = pos_table.shape[0] // devices
    wide = folds * share

    def cut(array, place):
        return array[place * share : (place + 1) * share]

    share_w_up = jnp.swapaxes(share_up[:wide].reshape(folds, share, model_width), 0, 1)
    gains_two = share_up[wide + share, : 2 * share]
    gains_one = share_heads[3 * share, : 2 * share]
    return (
        output,
        grad_pixels,
        grad_table,
        share_res[3 * share : 3 * share + pos_share],
        cut(share_res, 0),
        cut(share_res, 1),
        cut(share_res, 2),
        gains_one[:share],
        gains_one[share:],
        cut(share_heads, 0),
        cut(share_heads, 1),
        cut(share_heads, 2),
        share_up[wide : wide + share],
        gains_two[:share],
        gains_two[share:],
        share_w_up.reshape(share, folds * model_width),
        share_down[: grad_w_down.shape[0] // devices],
    )


def solution(mesh):
    in_specs = (
        P(("dp", "emb"), None),
        P(("dp", "emb"), None),
        P(("dp", "emb")),
        P(("dp", "emb")),
        P(("dp", "emb")),
        P("emb", None),
        P(),
        P(),
        P(),
        P(),
        P(),
        P(),
        P(),
        P(),
        P(),
        P(),
        P(),
        P(),
        P(),
        P(),
        P(("dp", "emb"), None),
    )
    out_specs = (
        P(("dp", "emb"), None),
        P(("dp", "emb"), None),
        P("emb", "dp"),
        P(("dp", "emb"), None),
        P(("dp", "emb"), None),
        P(("dp", "emb"), None),
        P(("dp", "emb"), None),
        P(("dp", "emb")),
        P(("dp", "emb")),
        P(("dp", "emb"), None),
        P(("dp", "emb"), None),
        P(("dp", "emb"), None),
        P(("dp", "emb"), None),
        P(("dp", "emb")),
        P(("dp", "emb")),
        P(("dp", "emb"), None),
        P(("dp", "emb"), None),
    )
    return jax.shard_map(
        on_device, mesh=mesh, in_specs=in_specs, out_specs=out_specs, check_vma=False
    )
```

```python
import functools

import jax
import jax.numpy as jnp
from jax import lax
from jax.experimental import pallas as pl
from jax.experimental.pallas import tpu as pltpu
from jax.sharding import PartitionSpec as P

HEAD_DIM = 32
TEXT_VOCAB = 32000
BLOCK = 256
HEADS_STEP = 2
MESH = pl.DeviceIdType.MESH
LOG2_E = 1.4426950408889634


def normalize(values):
    average = jnp.mean(values, -1, keepdims=True)
    centred = values - average
    variance = jnp.mean(centred * centred, -1, keepdims=True)
    return centred * lax.rsqrt(variance + 1e-05)


def norm_affine(values, gain, offset):
    return normalize(values) * gain + offset


def contract(left, right, left_dim, right_dim):
    return lax.dot_general(
        left, right, (((left_dim,), (right_dim,)), ((), ())), preferred_element_type=jnp.float32
    )


def product(left, right):
    return contract(left, right, 1, 0)


def product_left(left, right):
    return contract(left, right, 0, 0)


def product_right(left, right):
    return contract(left, right, 1, 1)


def forward_kernel(heads, q_ref, k_ref, v_ref, o_ref, p_ref, r_ref):
    length = q_ref.shape[1]
    scaling = HEAD_DIM ** (-0.5) * LOG2_E
    key_place = lax.broadcasted_iota(jnp.int32, (BLOCK, BLOCK), 0)
    query_place = lax.broadcasted_iota(jnp.int32, (BLOCK, BLOCK), 1)
    allowed = key_place <= query_place
    for head in range(heads):
        rows = slice(head * HEAD_DIM, (head + 1) * HEAD_DIM)
        keys = k_ref[rows, :]
        values = v_ref[rows, :]
        for step in range(length // BLOCK):
            start, end = step * BLOCK, (step + 1) * BLOCK
            scores = contract(keys[:, :end], q_ref[rows, start:end], 0, 0) * scaling
            corner = jnp.where(allowed, scores[start:], -1e30)
            highest = jnp.max(corner, 0, keepdims=True)
            if step:
                highest = jnp.maximum(highest, jnp.max(scores[:start], 0, keepdims=True))
            weights = jnp.exp2(corner - highest)
            total = jnp.sum(weights, 0, keepdims=True)
            weights = weights.astype(jnp.bfloat16)
            if step:
                above = jnp.exp2(scores[:start] - highest)
                total = total + jnp.sum(above, 0, keepdims=True)
                weights = jnp.concatenate([above.astype(jnp.bfloat16), weights], 0)
            inverse = 1.0 / total
            base = BLOCK * (step * (step + 1) // 2)
            p_ref[head, base : base + end, :] = weights
            r_ref[head, :, start:end] = inverse
            o_ref[rows, start:end] = (
                contract(values[:, :end], weights, 1, 0) * inverse
            ).astype(jnp.bfloat16)


def packed_rows(length):
    steps = length // BLOCK
    return BLOCK * (steps * (steps + 1) // 2)


def attention_forward(queries, key_heads, values):
    width, length = queries.shape
    heads = width // HEAD_DIM
    packed = packed_rows(length)
    rows = pl.BlockSpec((HEADS_STEP * HEAD_DIM, length), lambda g: (g, 0))
    return pl.pallas_call(
        functools.partial(forward_kernel, HEADS_STEP),
        grid=(heads // HEADS_STEP,),
        in_specs=[rows] * 3,
        out_specs=[
            rows,
            pl.BlockSpec((HEADS_STEP, packed, BLOCK), lambda g: (g, 0, 0)),
            pl.BlockSpec((HEADS_STEP, 1, length), lambda g: (g, 0, 0)),
        ],
        out_shape=[
            jax.ShapeDtypeStruct((width, length), jnp.bfloat16),
            jax.ShapeDtypeStruct((heads, packed, BLOCK), jnp.bfloat16),
            jax.ShapeDtypeStruct((heads, 1, length), jnp.float32),
        ],
        compiler_params=pltpu.CompilerParams(vmem_limit_bytes=32 << 20),
        cost_estimate=pl.CostEstimate(
            flops=50_000_000_000, bytes_accessed=heads * packed * BLOCK * 2, transcendentals=0
        ),
        name="attention_forward",
    )(queries, key_heads, values)


def backward_kernel(
    heads,
    q_ref,
    k_ref,
    v_ref,
    o_ref,
    g_ref,
    p_ref,
    r_ref,
    pack_one,
    pack_two,
    part_ref,
    d_ref,
    out_one,
    out_two,
    ring_ref,
    s_ref,
    *refs,
):
    ring = Ring(part_ref, ring_ref, refs[:3])
    first, second = shares_of([pack_one, pack_two], [out_one, out_two], refs[3:])
    bits = first.bits
    number = pl.program_id(0)
    last = pl.num_programs(0) - 1

    @pl.when(number == 0)
    def begin():
        greet(False)
        first.start()
        second.start()
        ring.start()

    @pl.when(number == 1)
    def first_swap():
        first.take(0)

    @pl.when(number == 4)
    def next_swap():
        first.take(1)
        second.take(0)

    @pl.when(number == 7)
    def other_swaps():
        for stage in range(2, bits):
            first.take(stage)

    @pl.when(number == 8)
    def late_swap():
        second.take(1)

    @pl.when(number == 10)
    def last_swaps():
        for stage in range(2, bits):
            second.take(stage)

    length = q_ref.shape[1]
    steps = length // BLOCK
    scaling = HEAD_DIM ** (-0.5)
    for head in range(heads):
        rows = slice(head * HEAD_DIM, (head + 1) * HEAD_DIM)
        grads = (g_ref[rows, :].astype(jnp.float32) * r_ref[head]).astype(jnp.bfloat16)
        inner = jnp.sum(
            grads.astype(jnp.float32) * o_ref[rows, :].astype(jnp.float32), 0, keepdims=True
        )
        queries = q_ref[rows, :]
        keys = k_ref[rows, :]
        values = v_ref[rows, :]
        for step in range(steps):
            start, end = step * BLOCK, (step + 1) * BLOCK
            base = BLOCK * (step * (step + 1) // 2)
            grad_probs = contract(values[:, :end], grads[:, start:end], 0, 0)
            grad_scores = p_ref[head, base : base + end, :] * (
                grad_probs - inner[:, start:end]
            ).astype(jnp.bfloat16)
            s_ref[head, base : base + end, :] = grad_scores
            d_ref[0, rows, start:end] = (
                contract(keys[:, :end], grad_scores, 1, 0) * scaling
            ).astype(jnp.bfloat16)
        for column in range(steps):
            grad_keys = jnp.zeros((HEAD_DIM, BLOCK), jnp.float32)
            grad_values = jnp.zeros((HEAD_DIM, BLOCK), jnp.float32)
            for step in range(column, steps):
                base = BLOCK * (step * (step + 1) // 2 + column)
                span = slice(step * BLOCK, (step + 1) * BLOCK)
                grad_values = grad_values + contract(
                    grads[:, span], p_ref[head, base : base + BLOCK, :], 1, 1
                )
                grad_keys = grad_keys + contract(
                    queries[:, span], s_ref[head, base : base + BLOCK, :], 1, 1
                )
            span = slice(column * BLOCK, (column + 1) * BLOCK)
            d_ref[1, rows, span] = (grad_keys * scaling).astype(jnp.bfloat16)
            d_ref[2, rows, span] = grad_values.astype(jnp.bfloat16)

    @pl.when(number == last)
    def end():
        ring.finish()
        first.finish()
        second.finish()


def attention_backward(
    queries, key_heads, values, attended, grads, probs, inverse, packs, part
):
    width, length = queries.shape
    heads = width // HEAD_DIM
    packed = packed_rows(length)
    rows = pl.BlockSpec((HEADS_STEP * HEAD_DIM, length), lambda g: (g, 0))
    scratch = [pltpu.VMEM((HEADS_STEP, packed, BLOCK), jnp.bfloat16)]
    scratch = scratch + ring_scratch(part.shape)
    for pack in packs:
        scratch = scratch + shares_scratch(pack.shape)
    return pl.pallas_call(
        functools.partial(backward_kernel, HEADS_STEP),
        grid=(heads // HEADS_STEP,),
        in_specs=[rows] * 5
        + [
            pl.BlockSpec((HEADS_STEP, packed, BLOCK), lambda g: (g, 0, 0)),
            pl.BlockSpec((HEADS_STEP, 1, length), lambda g: (g, 0, 0)),
            pl.BlockSpec(memory_space=pl.ANY),
            pl.BlockSpec(memory_space=pl.ANY),
            pl.BlockSpec(part.shape, lambda g: (0, 0, 0)),
        ],
        out_specs=[
            pl.BlockSpec((3, HEADS_STEP * HEAD_DIM, length), lambda g: (0, g, 0)),
            pl.BlockSpec(packs[0].shape[-2:], lambda g: (0, 0)),
            pl.BlockSpec(packs[1].shape[-2:], lambda g: (0, 0)),
            pl.BlockSpec(part.shape[-2:], lambda g: (0, 0)),
        ],
        out_shape=[
            jax.ShapeDtypeStruct((3, width, length), jnp.bfloat16),
            jax.ShapeDtypeStruct(packs[0].shape[-2:], jnp.float32),
            jax.ShapeDtypeStruct(packs[1].shape[-2:], jnp.float32),
            jax.ShapeDtypeStruct(part.shape[-2:], jnp.float32),
        ],
        scratch_shapes=scratch,
        compiler_params=pltpu.CompilerParams(
            collective_id=2, has_side_effects=True, vmem_limit_bytes=56 << 20
        ),
        name="attention_backward",
    )(queries, key_heads, values, attended, grads, probs, inverse, *packs, part)


def bit_of(index, bit):
    return lax.rem(lax.div(index, 1 << bit), 2)


def flipped(index, bit):
    return index + (1 - 2 * bit_of(index, bit)) * (1 << bit)


def spans_of(rows):
    first = (rows + 31) // 32 * 16
    return ((0, first), (first, rows - first))


class Shares:
    def __init__(self, pack, out, refs):
        self.pack, self.out = pack, out
        self.groups = pack.shape[0]
        self.bits = len(pack.shape) - 3
        self.spans = spans_of(pack.shape[-2])
        refs = list(refs)
        self.own, self.zero = refs[:2]
        count = self.bits - 1
        self.later = [refs[2 + half * count : 2 + (half + 1) * count] for half in range(2)]
        refs = refs[2 + 2 * count :]
        self.ring = refs[:2]
        self.local_sem, self.swap_send, self.swap_got, self.ring_send, self.ring_got = refs[2:]
        self.emb = lax.axis_index("emb")
        self.group = lax.axis_index("dp")
        self.every = (slice(None),) * self.bits

    def order(self, half):
        rest = list(range(1, self.bits))
        return [0] + (rest if half == 0 else rest[::-1])

    def span(self, half):
        return pl.ds(*self.spans[half])

    def place(self, half, stage, mine):
        order = self.order(half)
        index = []
        for bit in range(self.bits - 1, 0, -1):
            value = bit_of(self.emb, bit)
            if order.index(bit) < stage:
                index.append(value)
            elif order.index(bit) == stage:
                index.append(value if mine else 1 - value)
            else:
                index.append(slice(None))
        return tuple(index)

    def swap(self, half, stage):
        if stage == 0:
            other = 1 - bit_of(self.emb, 0)
            source = self.pack.at[self.every + (other, self.span(half))]
            target = self.zero.at[self.every + (self.span(half),)]
        else:
            place = self.place(half, stage, False)
            source = self.own.at[(slice(None),) + place + (self.span(half),)]
            target = self.later[half][stage - 1]
        return pltpu.make_async_remote_copy(
            src_ref=source,
            dst_ref=target,
            send_sem=self.swap_send.at[half, stage],
            recv_sem=self.swap_got.at[half, stage],
            device_id={"emb": flipped(self.emb, self.order(half)[stage])},
            device_id_type=MESH,
        )

    def bring(self, half):
        mine = bit_of(self.emb, 0)
        return pltpu.make_async_copy(
            self.pack.at[self.every + (mine, self.span(half))],
            self.own.at[self.every + (self.span(half),)],
            self.local_sem.at[half],
        )

    def hop(self, half, step):
        other = lax.rem(self.group + step, self.groups)
        place = (other,) + self.place(half, self.bits, True) + (self.span(half),)
        return pltpu.make_async_remote_copy(
            src_ref=self.own.at[place],
            dst_ref=self.ring[half].at[step - 1],
            send_sem=self.ring_send.at[half, step - 1],
            recv_sem=self.ring_got.at[half, step - 1],
            device_id={"dp": other},
            device_id_type=MESH,
        )

    def start(self):
        for half in range(2):
            self.swap(half, 0).start()
            self.bring(half).start()

    def take(self, stage):
        for half in range(2):
            self.take_half(half, stage)

    def take_half(self, half, stage):
        if stage == 0:
            self.bring(half).wait()
        self.swap(half, stage).wait()
        place = self.place(half, stage, True)
        free = [n for n, index in enumerate(place) if isinstance(index, slice)]

        def one(number, carry):
            group = lax.rem(number, self.groups)
            rest = lax.div(number, self.groups)
            index = list(place)
            there = []
            for n in free:
                index[n] = lax.rem(rest, 2)
                there.append(index[n])
                rest = lax.div(rest, 2)
            target = (group,) + tuple(index) + (self.span(half), slice(None))
            if stage == 0:
                arrived = self.zero[target]
            else:
                arrived = self.later[half][stage - 1][(group,) + tuple(there)]
            total = self.own[target].astype(jnp.float32) + arrived.astype(jnp.float32)
            self.own[target] = total.astype(jnp.bfloat16)
            return carry

        lax.fori_loop(0, self.groups * 2 ** len(free), one, 0)
        if stage + 1 < self.bits:
            self.swap(half, stage + 1).start()
        elif self.out is not None:
            for step in range(1, self.groups):
                self.hop(half, step).start()

    def export(self, target):
        for half in range(2):
            place = (slice(None),) + self.place(half, self.bits, True)
            target[:, self.span(half), :] = self.own[place + (self.span(half), slice(None))]

    def finish(self):
        for half in range(2):
            place = (self.group,) + self.place(half, self.bits, True)
            total = self.own[place + (self.span(half), slice(None))].astype(jnp.float32)
            for step in range(1, self.groups):
                self.hop(half, step).wait()
                total = total + self.ring[half][step - 1].astype(jnp.float32)
            self.out[self.span(half), :] = total


class Ring:
    def __init__(self, own, out, refs):
        self.own, self.out = own, out
        self.landed, self.send, self.got = refs
        self.groups = own.shape[0]
        self.group = lax.axis_index("dp")

    def hop(self, step):
        other = lax.rem(self.group + step, self.groups)
        return pltpu.make_async_remote_copy(
            src_ref=self.own.at[other],
            dst_ref=self.landed.at[step - 1],
            send_sem=self.send.at[step - 1],
            recv_sem=self.got.at[step - 1],
            device_id={"dp": other},
            device_id_type=MESH,
        )

    def start(self):
        for step in range(1, self.groups):
            self.hop(step).start()

    def finish(self):
        total = self.own[self.group].astype(jnp.float32)
        for step in range(1, self.groups):
            self.hop(step).wait()
            total = total + self.landed[step - 1].astype(jnp.float32)
        self.out[...] = total


def ring_scratch(shape):
    groups = shape[0]
    semaphores = pltpu.SemaphoreType.DMA((groups - 1,))
    return [pltpu.VMEM((groups - 1,) + shape[1:], jnp.bfloat16), semaphores, semaphores]


def shares_scratch(shape):
    groups, bits, columns = shape[0], len(shape) - 3, shape[-1]
    whole = pltpu.VMEM((groups,) + (2,) * (bits - 1) + shape[-2:], jnp.bfloat16)
    later = [
        pltpu.VMEM((groups,) + (2,) * (bits - 1 - stage) + (span[1], columns), jnp.bfloat16)
        for span in spans_of(shape[-2])
        for stage in range(1, bits)
    ]
    ring = [
        pltpu.VMEM((groups - 1, span[1], columns), jnp.bfloat16) for span in spans_of(shape[-2])
    ]
    semaphores = [(2,), (2, bits), (2, bits), (2, groups - 1), (2, groups - 1)]
    return [whole, whole, *later, *ring] + [pltpu.SemaphoreType.DMA(size) for size in semaphores]


def shares_of(packs, outs, refs):
    bits = len(packs[0].shape) - 3
    each = 2 + 2 * (bits - 1) + 2 + 5
    return [
        Shares(pack, out, refs[n * each : (n + 1) * each])
        for n, (pack, out) in enumerate(zip(packs, outs))
    ]


def greet(everyone, ring=True):
    emb, group = lax.axis_index("emb"), lax.axis_index("dp")
    owners, groups = lax.axis_size("emb"), lax.axis_size("dp")
    barrier = pltpu.get_barrier_semaphore()
    if everyone:
        others = [lax.rem(emb + step, owners) for step in range(1, owners)]
    else:
        others = [flipped(emb, bit) for bit in range(owners.bit_length() - 1)]
    for other in others:
        pl.semaphore_signal(barrier, inc=1, device_id={"emb": other}, device_id_type=MESH)
    for step in range(1, groups if ring else 1):
        other = lax.rem(group + step, groups)
        pl.semaphore_signal(barrier, inc=1, device_id={"dp": other}, device_id_type=MESH)
    pl.semaphore_wait(barrier, len(others) + (groups - 1 if ring else 0))


def blocks_of(array):
    owners, groups = lax.axis_size("emb"), lax.axis_size("dp")
    bits = owners.bit_length() - 1
    return array.reshape((groups,) + (2,) * bits + array.shape[1:])


def rows_of(array):
    devices = lax.axis_size("emb") * lax.axis_size("dp")
    return array.astype(jnp.bfloat16).reshape(devices, array.shape[0] // devices, array.shape[1])


def stacked(pieces):
    rows = sum(piece.shape[1] for piece in pieces)
    devices, _, columns = pieces[0].shape
    spare = -rows % 16
    if rows + spare < 32:
        spare = 32 - rows
    if spare:
        pieces = pieces + [jnp.zeros((devices, spare, columns), jnp.bfloat16)]
    return blocks_of(jnp.concatenate(pieces, 1))


def vector_rows(vectors, rows):
    devices = lax.axis_size("emb") * lax.axis_size("dp")
    wide = vectors[0].shape[0]
    piece = jnp.stack(vectors).astype(jnp.bfloat16).reshape(len(vectors), devices, -1)
    piece = jnp.swapaxes(piece, 0, 1).reshape(devices, 1, -1)
    return jnp.pad(piece, ((0, 0), (0, rows - 1), (0, wide - piece.shape[2])))


def table_scratch(groups, owners, columns, length, capacity):
    wide = groups * capacity
    return [
        pltpu.VMEM((groups, columns, length), jnp.bfloat16),
        pltpu.VMEM((owners, columns, wide), jnp.bfloat16),
        pltpu.VMEM((owners - 1, columns, wide), jnp.bfloat16),
        pltpu.SemaphoreType.DMA((1,)),
        pltpu.SemaphoreType.DMA((groups - 1,)),
        pltpu.SemaphoreType.DMA((groups - 1,)),
        pltpu.SemaphoreType.DMA((owners - 1,)),
        pltpu.SemaphoreType.DMA((owners - 1,)),
    ]


class Table:
    def __init__(self, grads, slots, ids, out, refs):
        self.grads, self.slots, self.ids, self.out = grads, slots, ids, out
        self.turned, self.packed, self.landed = refs[:3]
        self.local_sem, self.ring_send, self.ring_got, self.send, self.got = refs[3:]
        self.groups, self.columns, self.length = self.turned.shape
        self.owners, _, self.wide = self.packed.shape
        self.capacity = self.wide // self.groups
        self.emb = lax.axis_index("emb")
        self.group = lax.axis_index("dp")

    def bring(self):
        return pltpu.make_async_copy(
            self.grads.at[self.group], self.turned.at[0], self.local_sem.at[0]
        )

    def hop(self, step):
        other = lax.rem(self.group + step, self.groups)
        return pltpu.make_async_remote_copy(
            src_ref=self.grads.at[other],
            dst_ref=self.turned.at[step],
            send_sem=self.ring_send.at[step - 1],
            recv_sem=self.ring_got.at[step - 1],
            device_id={"dp": other},
            device_id_type=MESH,
        )

    def give(self, step):
        other = lax.rem(self.emb + step, self.owners)
        return pltpu.make_async_remote_copy(
            src_ref=self.packed.at[other],
            dst_ref=self.landed.at[step - 1],
            send_sem=self.send.at[step - 1],
            recv_sem=self.got.at[step - 1],
            device_id={"emb": other},
            device_id_type=MESH,
        )

    def start(self):
        self.bring().start()
        for step in range(1, self.groups):
            self.hop(step).start()

    def arrive(self):
        self.bring().wait()
        for step in range(1, self.groups):
            self.hop(step).wait()

    def sort(self, step):
        owner = lax.rem(self.emb + step, self.owners)
        rows = lax.broadcasted_iota(jnp.int32, (128, self.length), 0)
        tiles = []
        for tile in range(self.wide // 128):
            total = jnp.zeros((self.columns, 128), jnp.float32)
            for group in range(self.groups):
                low, high = group * self.capacity, (group + 1) * self.capacity
                if high <= tile * 128 or low >= (tile + 1) * 128:
                    continue
                slot = rows + (tile * 128 - low)
                inside = (slot >= 0) & (slot < self.capacity)
                wanted = jnp.where(inside, slot + owner * self.capacity, -2)
                hot = jnp.where(wanted == self.slots[group], 1.0, 0.0).astype(jnp.bfloat16)
                total = total + product_right(self.turned[group], hot)
            tiles.append(total.astype(jnp.bfloat16))
        self.packed[owner] = jnp.concatenate(tiles, 1)
        return owner

    def add(self, step, first):
        source = lax.rem(self.emb - step + self.owners, self.owners)
        rows, columns = self.out.shape
        count = 6 if rows % 48 == 0 else 1
        block = rows // count
        chunk = self.packed[self.emb] if step == 0 else self.landed[step - 1]

        def one(number, carry):
            base = pl.multiple_of(number * block, 8)
            places = base + lax.broadcasted_iota(jnp.int32, (block, self.wide), 0)
            hot = jnp.where(places == self.ids[source], 1.0, 0.0).astype(jnp.bfloat16)
            part = product_right(hot, chunk)
            if not first:
                part = part + self.out[pl.ds(base, block), :]
            self.out[pl.ds(base, block), :] = part
            return carry

        lax.fori_loop(0, count, one, 0)


def tail_kernel(count, grads_ref, slots_ref, ids_ref, *refs):
    packs, table_out, outs = refs[:count], refs[count], refs[count + 1 : 2 * count + 1]
    refs = refs[2 * count + 1 :]
    table = Table(grads_ref, slots_ref, ids_ref, table_out, refs[:8])
    shares = shares_of(packs, outs, refs[8:])
    owners = table.owners
    greet(True)
    table.start()
    for share in shares:
        share.start()
    shares[0].take(0)
    shares[1].take(0)
    for stage in range(1, shares[0].bits):
        for share in shares:
            share.take(stage)
    table.arrive()
    for step in range(1, owners):
        table.sort(step)
        table.give(step).start()
    table.sort(0)
    table.add(0, True)
    for share in shares:
        share.finish()
    for step in range(1, owners):
        table.give(step).wait()
        table.add(step, False)


def tail(grads, slots, ids, packs, table_rows, capacity):
    groups, columns, length = grads.shape
    owners = ids.shape[0]
    anywhere = pl.BlockSpec(memory_space=pl.ANY)
    vmem = pl.BlockSpec(memory_space=pltpu.VMEM)
    scratch = table_scratch(groups, owners, columns, length, capacity)
    for pack in packs:
        scratch = scratch + shares_scratch(pack.shape)
    return pl.pallas_call(
        functools.partial(tail_kernel, len(packs)),
        in_specs=[anywhere, vmem, vmem] + [anywhere] * len(packs),
        out_specs=[vmem] * (1 + len(packs)),
        out_shape=[jax.ShapeDtypeStruct((table_rows, columns), jnp.float32)]
        + [jax.ShapeDtypeStruct(pack.shape[-2:], jnp.float32) for pack in packs],
        scratch_shapes=scratch,
        compiler_params=pltpu.CompilerParams(
            collective_id=3, has_side_effects=True, vmem_limit_bytes=56 << 20
        ),
        name="tail",
    )(grads, slots, ids, *packs)


def column_of(row, rows):
    diagonal = lax.broadcasted_iota(jnp.int32, (128, 128), 0) == lax.broadcasted_iota(
        jnp.int32, (128, 128), 1
    )
    pieces = [
        jnp.sum(jnp.where(diagonal, row[:, start : start + 128], 0), 1, keepdims=True)
        for start in range(0, rows, 128)
    ]
    return jnp.concatenate(pieces, 0)


def gelu_pair(value):
    root = 0.7978845608028654
    square = value * value
    bend = jnp.tanh(root * (value + 0.044715 * (value * square)))
    half = 0.5 * (1.0 + bend)
    slope = half + 0.5 * value * (1.0 - bend * bend) * (root * (1.0 + 3 * 0.044715 * square))
    return value * half, slope


def front_kernel(
    counts_ref,
    codes_ref,
    place_ref,
    pixels_ref,
    table_ref,
    pos_ref,
    w_patch_ref,
    w_a_ref,
    w_b_ref,
    gain_ref,
    bias_ref,
    embedded_ref,
    normed_ref,
    first_ref,
    act_ref,
    slope_ref,
    ids_ref,
    slots_ref,
    codes_all,
    ranks,
    earlier,
    held,
    packed,
    landed,
    fetched,
    mixed,
    local_sem,
    ask_send,
    ask_got,
    send,
    got,
):
    owners, capacity, width = packed.shape
    length = codes_ref.shape[1]
    table_rows = held.shape[0]
    emb = lax.axis_index("emb")
    bring = pltpu.make_async_copy(table_ref, held, local_sem.at[0])
    bring.start()
    barrier = pltpu.get_barrier_semaphore()
    for step in range(1, owners):
        other = lax.rem(emb + step, owners)
        pl.semaphore_signal(barrier, inc=1, device_id={"emb": other}, device_id_type=MESH)
    pl.semaphore_wait(barrier, owners - 1)

    def ask(step):
        return pltpu.make_async_remote_copy(
            src_ref=codes_ref,
            dst_ref=codes_all.at[step],
            send_sem=ask_send.at[step - 1],
            recv_sem=ask_got.at[step - 1],
            device_id={"emb": lax.rem(emb + step, owners)},
            device_id_type=MESH,
        )

    def give(step):
        return pltpu.make_async_remote_copy(
            src_ref=packed.at[step],
            dst_ref=landed.at[step - 1],
            send_sem=send.at[step - 1],
            recv_sem=got.at[step - 1],
            device_id={"emb": lax.rem(emb - step + owners, owners)},
            device_id_type=MESH,
        )

    for step in range(1, owners):
        ask(step).start()
    codes_all[0] = codes_ref[...]
    block = min(256, length)

    def triangle(number, carry):
        base = pl.multiple_of(number * block, block)
        above = base + lax.broadcasted_iota(jnp.int32, (block, length), 0)
        below = lax.broadcasted_iota(jnp.int32, (block, length), 1)
        earlier[pl.ds(base, block), :] = jnp.where(above < below, 1.0, 0.0).astype(jnp.bfloat16)
        return carry

    lax.fori_loop(0, length // block, triangle, 0)
    codes = codes_ref[...]
    mine = [
        (codes >= owner * table_rows) & (codes < (owner + 1) * table_rows)
        for owner in range(owners)
    ]
    marks = jnp.concatenate([jnp.where(mark, 1.0, 0.0) for mark in mine], 0)
    places = product(marks.astype(jnp.bfloat16), earlier[...])
    slots = jnp.full((1, length), owners * capacity, jnp.int32)
    for owner in range(owners):
        rank = places[owner : owner + 1].astype(jnp.int32)
        slots = jnp.where(mine[owner], owner * capacity + rank, slots)
    slots_ref[...] = slots
    for step in range(1, owners):
        ask(step).wait()
    local = codes_all[...].reshape(owners, length) - emb * table_rows
    inside = (local >= 0) & (local < table_rows)
    places = product(jnp.where(inside, 1.0, 0.0).astype(jnp.bfloat16), earlier[...])
    ranks[...] = jnp.where(inside, places.astype(jnp.int32), -1).reshape(owners, 1, length)
    bring.wait()

    def gather(step):
        rank = ranks[step]
        local = codes_all[step] - emb * table_rows + 1
        slot = lax.broadcasted_iota(jnp.int32, (capacity, length), 0)
        match = slot == rank
        hot = jnp.where(match, 1.0, 0.0).astype(jnp.bfloat16)
        coarse = lax.div(local, 64)
        fine = local - coarse * 64
        inner = rank >= 0
        pair = jnp.concatenate(
            [jnp.where(inner, coarse, 0), jnp.where(inner, fine, 0)]
            + [jnp.zeros((6, length), jnp.int32)],
            0,
        )
        pair = product_right(pair.astype(jnp.float32).astype(jnp.bfloat16), hot)
        source = lax.rem(emb - step + owners, owners)
        ids_ref[source] = (pair[0:1] * 64.0 + pair[1:2]).astype(jnp.int32) - 1
        wanted = jnp.sum(jnp.where(match, local, 0), 1, keepdims=True) - 1
        total = jnp.zeros((capacity, width), jnp.float32)
        for start in range(0, table_rows, 1024):
            size = min(1024, table_rows - start)
            row = start + lax.broadcasted_iota(jnp.int32, (capacity, size), 1)
            hot = jnp.where(row == wanted, 1.0, 0.0).astype(jnp.bfloat16)
            total = total + product(hot, held[start : start + size, :])
        packed[step] = total.astype(jnp.bfloat16)

    def serve(step, carry):
        gather(step)
        give(step).start()
        return carry

    lax.fori_loop(1, owners, serve, 0)
    gather(0)
    slot_column = column_of(slots, length)
    fetched[...] = jnp.zeros_like(fetched)

    def place_rows(step):
        owner = lax.rem(emb + step, owners)
        rows = packed[0] if step == 0 else landed[step - 1]
        for start in range(0, length, block):
            slot = owner * capacity + lax.broadcasted_iota(jnp.int32, (block, capacity), 1)
            hot = jnp.where(slot == slot_column[start : start + block], 1.0, 0.0)
            fetched[start : start + block, :] += product(hot.astype(jnp.bfloat16), rows)


    def patches(number, carry):
        base = pl.multiple_of(number * block, block)
        rows = pl.ds(base, block)
        first = product(pixels_ref[rows, :], w_patch_ref[...])
        low = first.astype(jnp.bfloat16)
        first_ref[rows, :] = low
        act, slope = gelu_pair(product(low, w_a_ref[...]))
        act = act.astype(jnp.bfloat16)
        act_ref[rows, :] = act
        slope_ref[rows, :] = slope.astype(jnp.bfloat16)
        mixed[rows, :] = first + product(act, w_b_ref[...])
        return carry

    lax.fori_loop(0, length // block, patches, 0)

    def positions(number, carry):
        base = pl.multiple_of(number * block, block)
        spot = lax.broadcasted_iota(jnp.int32, (block, pos_ref.shape[0]), 1)
        place = column_of(place_ref[:, pl.ds(base, block)], block)
        hot = jnp.where(spot == place, 1.0, 0.0).astype(jnp.bfloat16)
        embedded_ref[pl.ds(base, block), :] = product(hot, pos_ref[...])
        return carry

    lax.fori_loop(0, length // block, positions, 0)
    place_rows(0)
    for step in range(1, owners):
        give(step).wait()
        place_rows(step)

    def settle(number, carry):
        base = pl.multiple_of(number * block, block)
        rows = pl.ds(base, block)
        token = base + lax.broadcasted_iota(jnp.int32, (block, width), 0)
        image = mixed[rows, :] + embedded_ref[rows, :]
        value = jnp.where(token < counts_ref[0, 0], image, fetched[rows, :])
        embedded_ref[rows, :] = value
        normed = normalize(value) * gain_ref[...] + bias_ref[...]
        normed_ref[rows, :] = normed.astype(jnp.bfloat16)
        return carry

    lax.fori_loop(0, length // block, settle, 0)


def front(counts, codes, place, pixels, table, pos, w_patch, w_a, w_b, gain, bias, capacity):
    owners = lax.axis_size("emb")
    length, width = pixels.shape
    vmem = pl.BlockSpec(memory_space=pltpu.VMEM)
    low = jax.ShapeDtypeStruct((length, width), jnp.bfloat16)
    full = jax.ShapeDtypeStruct((length, width), jnp.float32)
    return pl.pallas_call(
        front_kernel,
        in_specs=[pl.BlockSpec(memory_space=pltpu.SMEM), vmem, vmem, vmem]
        + [pl.BlockSpec(memory_space=pl.ANY)]
        + [vmem] * 6,
        out_specs=[vmem] * 7,
        out_shape=[
            full,
            low,
            low,
            low,
            low,
            jax.ShapeDtypeStruct((owners, 1, capacity), jnp.int32),
            jax.ShapeDtypeStruct((1, length), jnp.int32),
        ],
        scratch_shapes=[
            pltpu.VMEM((owners, 1, length), jnp.int32),
            pltpu.VMEM((owners, 1, length), jnp.int32),
            pltpu.VMEM((length, length), jnp.bfloat16),
            pltpu.VMEM(table.shape, jnp.bfloat16),
            pltpu.VMEM((owners, capacity, width), jnp.bfloat16),
            pltpu.VMEM((owners - 1, capacity, width), jnp.bfloat16),
            pltpu.VMEM((length, width), jnp.float32),
            pltpu.VMEM((length, width), jnp.float32),
            pltpu.SemaphoreType.DMA((1,)),
            pltpu.SemaphoreType.DMA((owners - 1,)),
            pltpu.SemaphoreType.DMA((owners - 1,)),
            pltpu.SemaphoreType.DMA((owners - 1,)),
            pltpu.SemaphoreType.DMA((owners - 1,)),
        ],
        compiler_params=pltpu.CompilerParams(
            collective_id=1, has_side_effects=True, vmem_limit_bytes=56 << 20
        ),
        name="front",
    )(counts, codes, place, pixels, table, pos, w_patch, w_a, w_b, gain, bias)


def feed_kernel(
    attended_ref,
    embedded_ref,
    cotangent_ref,
    w_o_ref,
    gain_ref,
    bias_ref,
    w_up_ref,
    w_down_ref,
    output_ref,
    grad_middle_ref,
    grad_up_ref,
    grad_attended_ref,
    grad_w_o_ref,
    gains_ref,
    part_ref,
    middle,
    normed,
    back,
    slopes,
    hidden,
    pack,
    *refs,
):
    (share,) = shares_of([pack], [None], refs)
    groups, length, chunk = slopes.shape
    bits = share.bits
    owners = 1 << bits
    width = middle.shape[1]
    step = pl.program_id(0)
    block = min(512, length)
    blocks = length // block

    @pl.when(step == 0)
    def begin():
        greet(False, ring=False)

        def one(number, carry):
            rows = pl.ds(pl.multiple_of(number * block, block), block)
            value = embedded_ref[rows, :] + product_left(attended_ref[:, rows], w_o_ref[...])
            middle[rows, :] = value
            normed[rows, :] = (normalize(value) * gain_ref[...] + bias_ref[...]).astype(
                jnp.bfloat16
            )
            return carry

        lax.fori_loop(0, blocks, one, 0)

    @pl.when(step < groups)
    def go_forward():
        def one(number, carry):
            rows = pl.ds(pl.multiple_of(number * block, block), block)
            act, slope = gelu_pair(product(normed[rows, :], w_up_ref[...]))
            act = act.astype(jnp.bfloat16)
            hidden[rows, :] = act
            slopes[step, rows, :] = slope.astype(jnp.bfloat16)
            grown = product(act, w_down_ref[...])

            @pl.when(step == 0)
            def first():
                grad_middle_ref[rows, :] = middle[rows, :] + grown

            @pl.when(step > 0)
            def other():
                grad_middle_ref[rows, :] = grad_middle_ref[rows, :] + grown

            return carry

        lax.fori_loop(0, blocks, one, 0)
        units = chunk // owners
        spare = pack.shape[-2] - units
        part = 384 if chunk % 384 == 0 and 384 % units == 0 else chunk
        for start in range(0, chunk, part):
            grads = product_left(hidden[:, start : start + part], cotangent_ref[...])
            for place in range(part // units):
                piece = grads[place * units : (place + 1) * units]
                if spare:
                    piece = jnp.concatenate([piece, jnp.zeros((spare, width), jnp.float32)], 0)
                owner = start // units + place
                index = tuple((owner >> bit) & 1 for bit in range(bits - 1, -1, -1))
                pack[(step,) + index] = piece.astype(jnp.bfloat16)

    @pl.when(step == groups - 1)
    def turn():
        output_ref[...] = grad_middle_ref[...].astype(jnp.bfloat16)
        share.start()

    @pl.when(step == groups + 1)
    def swap():
        share.take(0)

    @pl.when(step >= groups)
    def go_back():
        def one(number, carry):
            rows = pl.ds(pl.multiple_of(number * block, block), block)
            slope = slopes[step - groups, rows, :].astype(jnp.float32)
            grads = product_right(cotangent_ref[rows, :], w_down_ref[...]) * slope
            grads = grads.astype(jnp.bfloat16)
            hidden[rows, :] = grads
            lower = product_right(grads, w_up_ref[...])

            @pl.when(step == groups)
            def first():
                back[rows, :] = lower

            @pl.when(step > groups)
            def other():
                back[rows, :] = back[rows, :] + lower

            return carry

        lax.fori_loop(0, blocks, one, 0)
        for start in range(0, width, 768):
            span = slice(start, start + 768)
            grad_up_ref[0, span, :] = product_left(normed[:, span], hidden[...]).astype(
                jnp.bfloat16
            )

    @pl.when(step == 2 * groups - 1)
    def end():
        share.take(1)
        gains_ref[...] = jnp.zeros_like(gains_ref)

        def one(number, carry):
            rows = pl.ds(pl.multiple_of(number * block, block), block)
            value = middle[rows, :]
            centred = value - jnp.mean(value, -1, keepdims=True)
            scale = lax.rsqrt(jnp.mean(centred * centred, -1, keepdims=True) + 1e-05)
            unit = centred * scale
            grads = back[rows, :]
            gains_ref[0:1, :] += jnp.sum(grads * unit, 0, keepdims=True)
            gains_ref[1:2, :] += jnp.sum(grads, 0, keepdims=True)
            grads = grads * gain_ref[...]
            along = jnp.mean(grads * unit, -1, keepdims=True)
            grads = scale * (grads - jnp.mean(grads, -1, keepdims=True) - unit * along)
            grads = cotangent_ref[rows, :].astype(jnp.float32) + grads
            grad_middle_ref[rows, :] = grads
            normed[rows, :] = grads.astype(jnp.bfloat16)
            return carry

        lax.fori_loop(0, blocks, one, 0)
        for start in range(0, width, 256):
            span = slice(start, start + 256)
            grad_w_o_ref[span, :] = product(attended_ref[span, :], normed[...]).astype(
                jnp.bfloat16
            )
            grad_attended_ref[span, :] = product_right(w_o_ref[span, :], normed[...]).astype(
                jnp.bfloat16
            )
        for stage in range(2, bits):
            share.take(stage)
        share.export(part_ref)


def feed(attended, embedded, cotangent, w_o, gain, bias, w_up, w_down):
    groups, owners = lax.axis_size("dp"), lax.axis_size("emb")
    length, width = embedded.shape
    chunk = w_up.shape[1] // groups
    units = chunk // owners
    units = max(32, units + -units % 16)
    shape = (groups,) + (2,) * (owners.bit_length() - 1) + (units, width)
    once = pl.Buffered(1)

    def whole(array):
        return pl.BlockSpec(array.shape, lambda s: (0, 0), pipeline_mode=once)

    outs = [
        jax.ShapeDtypeStruct((length, width), jnp.bfloat16),
        jax.ShapeDtypeStruct((length, width), jnp.float32),
        jax.ShapeDtypeStruct((groups, width, chunk), jnp.bfloat16),
        jax.ShapeDtypeStruct((width, length), jnp.bfloat16),
        jax.ShapeDtypeStruct((width, width), jnp.bfloat16),
        jax.ShapeDtypeStruct((8, width), jnp.float32),
        jax.ShapeDtypeStruct((groups, units, width), jnp.bfloat16),
    ]
    out_specs = [whole(out) if len(out.shape) == 2 else None for out in outs]
    out_specs[2] = pl.BlockSpec((1, width, chunk), lambda s: (jnp.maximum(s - groups, 0), 0, 0))
    out_specs[6] = pl.BlockSpec(outs[6].shape, lambda s: (0, 0, 0), pipeline_mode=once)
    return pl.pallas_call(
        feed_kernel,
        grid=(2 * groups,),
        in_specs=[
            whole(attended),
            whole(embedded),
            whole(cotangent),
            whole(w_o),
            whole(gain),
            whole(bias),
            pl.BlockSpec((width, chunk), lambda s: (0, lax.rem(s, groups))),
            pl.BlockSpec((chunk, width), lambda s: (lax.rem(s, groups), 0)),
        ],
        out_specs=out_specs,
        out_shape=outs,
        scratch_shapes=[
            pltpu.VMEM((length, width), jnp.float32),
            pltpu.VMEM((length, width), jnp.bfloat16),
            pltpu.VMEM((length, width), jnp.float32),
            pltpu.VMEM((groups, length, chunk), jnp.bfloat16),
            pltpu.VMEM((length, chunk), jnp.bfloat16),
            pltpu.VMEM(shape, jnp.bfloat16),
        ]
        + shares_scratch(shape),
        compiler_params=pltpu.CompilerParams(
            collective_id=4, has_side_effects=True, vmem_limit_bytes=58 << 20
        ),
        name="feed",
    )(attended, embedded, cotangent, w_o, gain, bias, w_up, w_down)


def on_device(
    pixels,
    counts,
    token_ids,
    action_bins,
    patch_pos,
    token_table,
    pos_table,
    w_patch,
    w_res_a,
    w_res_b,
    gain_one,
    bias_one,
    w_q,
    w_k,
    w_v,
    w_o,
    gain_two,
    bias_two,
    w_up,
    w_down,
    cotangent,
):
    length = pixels.shape[0]
    model_width = w_q.shape[0]
    positions = jnp.arange(length)
    image_rows = positions < counts[0, 0]
    action_rows = positions >= length - counts[0, 1]
    table_rows = jnp.logical_not(image_rows)
    row_ids = jnp.where(action_rows, TEXT_VOCAB + action_bins, token_ids)
    rows_owned = token_table.shape[0]
    owners_total = lax.axis_size("emb")
    capacity = 3 * length // (2 * owners_total)
    groups = lax.axis_size("dp")
    codes = jnp.where(table_rows, row_ids, -1).reshape(1, length)
    gain_row = gain_one.astype(jnp.float32).reshape(1, model_width)
    bias_row = bias_one.astype(jnp.float32).reshape(1, model_width)
    embedded, normed_one, first_low, res_act, res_slope, ids, slots = front(
        counts,
        codes,
        patch_pos.reshape(1, length),
        pixels,
        token_table,
        pos_table,
        w_patch,
        w_res_a,
        w_res_b,
        gain_row,
        bias_row,
        capacity,
    )
    position_hot = patch_pos[:, None] == jnp.arange(pos_table.shape[0])[None, :]
    facts = jnp.concatenate([ids.reshape(-1), slots.reshape(-1)])
    ring = [facts] + [
        lax.ppermute(facts, "dp", [(i, (i + step) % groups) for i in range(groups)])
        for step in range(1, groups)
    ]
    ring = jnp.stack(ring)
    ring_ids = ring[:, : owners_total * capacity].reshape(groups, owners_total, capacity)
    ring_ids = jnp.swapaxes(ring_ids, 0, 1).reshape(owners_total, 1, groups * capacity)
    ring_slots = ring[:, owners_total * capacity :].reshape(groups, 1, length)
    _, norm_back_one = jax.vjp(
        norm_affine, embedded, gain_one.astype(jnp.float32), bias_one.astype(jnp.float32)
    )
    queries = contract(w_q, normed_one, 0, 1).astype(jnp.bfloat16)
    key_heads = contract(w_k, normed_one, 0, 1).astype(jnp.bfloat16)
    value_heads = contract(w_v, normed_one, 0, 1).astype(jnp.bfloat16)
    attended, probs, inverse = attention_forward(queries, key_heads, value_heads)
    output, grad_middle, grad_w_up, grad_attended, grad_w_o, gains, part_down = feed(
        attended,
        embedded,
        cotangent,
        w_o,
        gain_two.astype(jnp.float32).reshape(1, model_width),
        bias_two.astype(jnp.float32).reshape(1, model_width),
        w_up,
        w_down,
    )
    devices = groups * owners_total
    share = model_width // devices
    folds = w_up.shape[1] // model_width
    per_fold = groups // folds
    folded = []
    for n in range(folds):
        pieces = [grad_w_up[n * per_fold + m] for m in range(per_fold)]
        folded.append(rows_of(jnp.concatenate(pieces, 1) if per_fold > 1 else pieces[0]))
    grad_heads, share_one, share_two, share_down = attention_backward(
        queries,
        key_heads,
        value_heads,
        attended,
        grad_attended,
        probs,
        inverse,
        [
            stacked(folded[:2] + [rows_of(grad_w_o), vector_rows([gains[0], gains[1]], 8)]),
            stacked(folded[2:]),
        ],
        part_down,
    )
    grad_heads = grad_heads.reshape(3 * model_width, length)
    grad_normed_one = product_left(grad_heads, jnp.concatenate([w_q.T, w_k.T, w_v.T], 0))
    grad_embed_norm, grad_gain_one, grad_bias_one = norm_back_one(grad_normed_one)
    gains_one = vector_rows([grad_gain_one, grad_bias_one], 8)
    grad_w_heads = [
        rows_of(contract(normed_one, grad_heads[n * model_width : (n + 1) * model_width], 0, 1))
        for n in range(3)
    ]
    grad_embedded = grad_middle + grad_embed_norm
    grad_low = grad_embedded.astype(jnp.bfloat16)
    columns = model_width // groups
    grads_turned = grad_low.T.reshape(groups, columns, length)
    grad_image = jnp.where(image_rows[:, None], grad_embedded, 0.0)
    grad_mixed = grad_image.astype(jnp.bfloat16)
    grad_pos_table = product_left(position_hot.astype(jnp.bfloat16), grad_mixed)
    grad_w_res_b = product_left(res_act, grad_mixed)
    grad_inner = product_right(grad_mixed, w_res_b) * res_slope.astype(jnp.float32)
    grad_inner = grad_inner.astype(jnp.bfloat16)
    grad_w_res_a = product_left(first_low, grad_inner)
    grad_first = (grad_image + product_right(grad_inner, w_res_a)).astype(jnp.bfloat16)
    grad_w_patch = product_left(pixels, grad_first)
    grad_pixels = product_right(grad_first, w_patch)
    res_rows = [rows_of(g) for g in (grad_w_patch, grad_w_res_a, grad_w_res_b, grad_pos_table)]
    grad_table, share_heads, share_res = tail(
        grads_turned,
        ring_slots,
        ring_ids,
        [stacked(grad_w_heads + [gains_one]), stacked(res_rows)],
        rows_owned,
        capacity,
    )
    pos_share = pos_table.shape[0] // devices
    def cut(array, place):
        return array[place * share : (place + 1) * share]

    rows_up = jnp.concatenate([share_one[: 2 * share], share_two[: (folds - 2) * share]], 0)
    share_w_up = jnp.swapaxes(rows_up.reshape(folds, share, model_width), 0, 1)
    gains_two = share_one[3 * share, : 2 * share]
    gains_one = share_heads[3 * share, : 2 * share]
    return (
        output,
        grad_pixels,
        grad_table,
        share_res[3 * share : 3 * share + pos_share],
        cut(share_res, 0),
        cut(share_res, 1),
        cut(share_res, 2),
        gains_one[:share],
        gains_one[share:],
        cut(share_heads, 0),
        cut(share_heads, 1),
        cut(share_heads, 2),
        cut(share_one, 2),
        gains_two[:share],
        gains_two[share:],
        share_w_up.reshape(share, folds * model_width),
        share_down[: w_down.shape[0] // devices],
    )


def solution(mesh):
    in_specs = (
        P(("dp", "emb"), None),
        P(("dp", "emb"), None),
        P(("dp", "emb")),
        P(("dp", "emb")),
        P(("dp", "emb")),
        P("emb", None),
        P(),
        P(),
        P(),
        P(),
        P(),
        P(),
        P(),
        P(),
        P(),
        P(),
        P(),
        P(),
        P(),
        P(),
        P(("dp", "emb"), None),
    )
    out_specs = (
        P(("dp", "emb"), None),
        P(("dp", "emb"), None),
        P("emb", "dp"),
        P(("dp", "emb"), None),
        P(("dp", "emb"), None),
        P(("dp", "emb"), None),
        P(("dp", "emb"), None),
        P(("dp", "emb")),
        P(("dp", "emb")),
        P(("dp", "emb"), None),
        P(("dp", "emb"), None),
        P(("dp", "emb"), None),
        P(("dp", "emb"), None),
        P(("dp", "emb")),
        P(("dp", "emb")),
        P(("dp", "emb"), None),
        P(("dp", "emb"), None),
    )
    return jax.shard_map(
        on_device, mesh=mesh, in_specs=in_specs, out_specs=out_specs, check_vma=False
    )
```

```python
import functools

import jax
import jax.numpy as jnp
from jax import lax
from jax.experimental import pallas as pl
from jax.experimental.pallas import tpu as pltpu
from jax.sharding import PartitionSpec as P

HEAD_DIM = 32
TEXT_VOCAB = 32000
BLOCK = 256
HEADS_STEP = 2
MESH = pl.DeviceIdType.MESH
LOG2_E = 1.4426950408889634


def normalize(values):
    average = jnp.mean(values, -1, keepdims=True)
    centred = values - average
    variance = jnp.mean(centred * centred, -1, keepdims=True)
    return centred * lax.rsqrt(variance + 1e-05)


def norm_affine(values, gain, offset):
    return normalize(values) * gain + offset


def contract(left, right, left_dim, right_dim):
    return lax.dot_general(
        left, right, (((left_dim,), (right_dim,)), ((), ())), preferred_element_type=jnp.float32
    )


def product(left, right):
    return contract(left, right, 1, 0)


def product_left(left, right):
    return contract(left, right, 0, 0)


def product_right(left, right):
    return contract(left, right, 1, 1)


def forward_kernel(heads, q_ref, k_ref, v_ref, o_ref, p_ref, r_ref):
    length = q_ref.shape[1]
    scaling = HEAD_DIM ** (-0.5) * LOG2_E
    key_place = lax.broadcasted_iota(jnp.int32, (BLOCK, BLOCK), 0)
    query_place = lax.broadcasted_iota(jnp.int32, (BLOCK, BLOCK), 1)
    allowed = key_place <= query_place
    for head in range(heads):
        rows = slice(head * HEAD_DIM, (head + 1) * HEAD_DIM)
        keys = k_ref[rows, :]
        values = v_ref[rows, :]
        for step in range(length // BLOCK):
            start, end = step * BLOCK, (step + 1) * BLOCK
            scores = contract(keys[:, :end], q_ref[rows, start:end], 0, 0) * scaling
            corner = jnp.where(allowed, scores[start:], -1e30)
            highest = jnp.max(corner, 0, keepdims=True)
            if step:
                highest = jnp.maximum(highest, jnp.max(scores[:start], 0, keepdims=True))
            weights = jnp.exp2(corner - highest)
            total = jnp.sum(weights, 0, keepdims=True)
            weights = weights.astype(jnp.bfloat16)
            if step:
                above = jnp.exp2(scores[:start] - highest)
                total = total + jnp.sum(above, 0, keepdims=True)
                weights = jnp.concatenate([above.astype(jnp.bfloat16), weights], 0)
            inverse = 1.0 / total
            base = BLOCK * (step * (step + 1) // 2)
            p_ref[head, base : base + end, :] = weights
            r_ref[head, :, start:end] = inverse
            o_ref[rows, start:end] = (
                contract(values[:, :end], weights, 1, 0) * inverse
            ).astype(jnp.bfloat16)


def packed_rows(length):
    steps = length // BLOCK
    return BLOCK * (steps * (steps + 1) // 2)


def attention_forward(queries, key_heads, values):
    width, length = queries.shape
    heads = width // HEAD_DIM
    packed = packed_rows(length)
    rows = pl.BlockSpec((HEADS_STEP * HEAD_DIM, length), lambda g: (g, 0))
    return pl.pallas_call(
        functools.partial(forward_kernel, HEADS_STEP),
        grid=(heads // HEADS_STEP,),
        in_specs=[rows] * 3,
        out_specs=[
            rows,
            pl.BlockSpec((HEADS_STEP, packed, BLOCK), lambda g: (g, 0, 0)),
            pl.BlockSpec((HEADS_STEP, 1, length), lambda g: (g, 0, 0)),
        ],
        out_shape=[
            jax.ShapeDtypeStruct((width, length), jnp.bfloat16),
            jax.ShapeDtypeStruct((heads, packed, BLOCK), jnp.bfloat16),
            jax.ShapeDtypeStruct((heads, 1, length), jnp.float32),
        ],
        compiler_params=pltpu.CompilerParams(vmem_limit_bytes=32 << 20),
        cost_estimate=pl.CostEstimate(
            flops=50_000_000_000, bytes_accessed=heads * packed * BLOCK * 2, transcendentals=0
        ),
        name="attention_forward",
    )(queries, key_heads, values)


def backward_kernel(
    heads,
    q_ref,
    k_ref,
    v_ref,
    o_ref,
    g_ref,
    p_ref,
    r_ref,
    pack_one,
    pack_two,
    part_ref,
    d_ref,
    out_one,
    out_two,
    ring_ref,
    s_ref,
    *refs,
):
    ring = Ring(part_ref, ring_ref, refs[:3])
    first, second = shares_of([pack_one, pack_two], [out_one, out_two], refs[3:])
    bits = first.bits
    number = pl.program_id(0)
    last = pl.num_programs(0) - 1

    @pl.when(number == 0)
    def begin():
        greet(False)
        first.start()
        second.start()
        ring.start()

    @pl.when(number == 1)
    def first_swap():
        first.take(0)

    @pl.when(number == 4)
    def next_swap():
        first.take(1)
        second.take(0)

    @pl.when(number == 7)
    def other_swaps():
        for stage in range(2, bits):
            first.take(stage)

    @pl.when(number == 8)
    def late_swap():
        second.take(1)

    @pl.when(number == 10)
    def last_swaps():
        for stage in range(2, bits):
            second.take(stage)

    length = q_ref.shape[1]
    steps = length // BLOCK
    scaling = HEAD_DIM ** (-0.5)
    for head in range(heads):
        rows = slice(head * HEAD_DIM, (head + 1) * HEAD_DIM)
        grads = (g_ref[rows, :].astype(jnp.float32) * r_ref[head]).astype(jnp.bfloat16)
        inner = jnp.sum(
            grads.astype(jnp.float32) * o_ref[rows, :].astype(jnp.float32), 0, keepdims=True
        )
        queries = q_ref[rows, :]
        keys = k_ref[rows, :]
        values = v_ref[rows, :]
        for step in range(steps):
            start, end = step * BLOCK, (step + 1) * BLOCK
            base = BLOCK * (step * (step + 1) // 2)
            grad_probs = contract(values[:, :end], grads[:, start:end], 0, 0)
            grad_scores = p_ref[head, base : base + end, :] * (
                grad_probs - inner[:, start:end]
            ).astype(jnp.bfloat16)
            s_ref[head, base : base + end, :] = grad_scores
            d_ref[0, rows, start:end] = (
                contract(keys[:, :end], grad_scores, 1, 0) * scaling
            ).astype(jnp.bfloat16)
        for column in range(steps):
            grad_keys = jnp.zeros((HEAD_DIM, BLOCK), jnp.float32)
            grad_values = jnp.zeros((HEAD_DIM, BLOCK), jnp.float32)
            for step in range(column, steps):
                base = BLOCK * (step * (step + 1) // 2 + column)
                span = slice(step * BLOCK, (step + 1) * BLOCK)
                grad_values = grad_values + contract(
                    grads[:, span], p_ref[head, base : base + BLOCK, :], 1, 1
                )
                grad_keys = grad_keys + contract(
                    queries[:, span], s_ref[head, base : base + BLOCK, :], 1, 1
                )
            span = slice(column * BLOCK, (column + 1) * BLOCK)
            d_ref[1, rows, span] = (grad_keys * scaling).astype(jnp.bfloat16)
            d_ref[2, rows, span] = grad_values.astype(jnp.bfloat16)

    @pl.when(number == last)
    def end():
        ring.finish()
        first.finish()
        second.finish()


def attention_backward(
    queries, key_heads, values, attended, grads, probs, inverse, packs, part
):
    width, length = queries.shape
    heads = width // HEAD_DIM
    packed = packed_rows(length)
    rows = pl.BlockSpec((HEADS_STEP * HEAD_DIM, length), lambda g: (g, 0))
    scratch = [pltpu.VMEM((HEADS_STEP, packed, BLOCK), jnp.bfloat16)]
    scratch = scratch + ring_scratch(part.shape)
    for pack in packs:
        scratch = scratch + shares_scratch(pack.shape)
    return pl.pallas_call(
        functools.partial(backward_kernel, HEADS_STEP),
        grid=(heads // HEADS_STEP,),
        in_specs=[rows] * 5
        + [
            pl.BlockSpec((HEADS_STEP, packed, BLOCK), lambda g: (g, 0, 0)),
            pl.BlockSpec((HEADS_STEP, 1, length), lambda g: (g, 0, 0)),
            pl.BlockSpec(memory_space=pl.ANY),
            pl.BlockSpec(memory_space=pl.ANY),
            pl.BlockSpec(part.shape, lambda g: (0, 0, 0)),
        ],
        out_specs=[
            pl.BlockSpec((3, HEADS_STEP * HEAD_DIM, length), lambda g: (0, g, 0)),
            pl.BlockSpec(packs[0].shape[-2:], lambda g: (0, 0)),
            pl.BlockSpec(packs[1].shape[-2:], lambda g: (0, 0)),
            pl.BlockSpec(part.shape[-2:], lambda g: (0, 0)),
        ],
        out_shape=[
            jax.ShapeDtypeStruct((3, width, length), jnp.bfloat16),
            jax.ShapeDtypeStruct(packs[0].shape[-2:], jnp.float32),
            jax.ShapeDtypeStruct(packs[1].shape[-2:], jnp.float32),
            jax.ShapeDtypeStruct(part.shape[-2:], jnp.float32),
        ],
        scratch_shapes=scratch,
        compiler_params=pltpu.CompilerParams(
            collective_id=2, has_side_effects=True, vmem_limit_bytes=56 << 20
        ),
        name="attention_backward",
    )(queries, key_heads, values, attended, grads, probs, inverse, *packs, part)


def bit_of(index, bit):
    return lax.rem(lax.div(index, 1 << bit), 2)


def flipped(index, bit):
    return index + (1 - 2 * bit_of(index, bit)) * (1 << bit)


def spans_of(rows):
    first = (rows + 31) // 32 * 16
    return ((0, first), (first, rows - first))


class Shares:
    def __init__(self, pack, out, refs):
        self.pack, self.out = pack, out
        self.groups = pack.shape[0]
        self.bits = len(pack.shape) - 3
        self.spans = spans_of(pack.shape[-2])
        refs = list(refs)
        self.own, self.zero = refs[:2]
        count = self.bits - 1
        self.later = [refs[2 + half * count : 2 + (half + 1) * count] for half in range(2)]
        refs = refs[2 + 2 * count :]
        self.ring = refs[:2]
        self.local_sem, self.swap_send, self.swap_got, self.ring_send, self.ring_got = refs[2:]
        self.emb = lax.axis_index("emb")
        self.group = lax.axis_index("dp")
        self.every = (slice(None),) * self.bits

    def order(self, half):
        rest = list(range(1, self.bits))
        return [0] + (rest if half == 0 else rest[::-1])

    def span(self, half):
        return pl.ds(*self.spans[half])

    def place(self, half, stage, mine):
        order = self.order(half)
        index = []
        for bit in range(self.bits - 1, 0, -1):
            value = bit_of(self.emb, bit)
            if order.index(bit) < stage:
                index.append(value)
            elif order.index(bit) == stage:
                index.append(value if mine else 1 - value)
            else:
                index.append(slice(None))
        return tuple(index)

    def swap(self, half, stage):
        if stage == 0:
            other = 1 - bit_of(self.emb, 0)
            source = self.pack.at[self.every + (other, self.span(half))]
            target = self.zero.at[self.every + (self.span(half),)]
        else:
            place = self.place(half, stage, False)
            source = self.own.at[(slice(None),) + place + (self.span(half),)]
            target = self.later[half][stage - 1]
        return pltpu.make_async_remote_copy(
            src_ref=source,
            dst_ref=target,
            send_sem=self.swap_send.at[half, stage],
            recv_sem=self.swap_got.at[half, stage],
            device_id={"emb": flipped(self.emb, self.order(half)[stage])},
            device_id_type=MESH,
        )

    def bring(self, half):
        mine = bit_of(self.emb, 0)
        return pltpu.make_async_copy(
            self.pack.at[self.every + (mine, self.span(half))],
            self.own.at[self.every + (self.span(half),)],
            self.local_sem.at[half],
        )

    def hop(self, half, step):
        other = lax.rem(self.group + step, self.groups)
        place = (other,) + self.place(half, self.bits, True) + (self.span(half),)
        return pltpu.make_async_remote_copy(
            src_ref=self.own.at[place],
            dst_ref=self.ring[half].at[step - 1],
            send_sem=self.ring_send.at[half, step - 1],
            recv_sem=self.ring_got.at[half, step - 1],
            device_id={"dp": other},
            device_id_type=MESH,
        )

    def start(self):
        for half in range(2):
            self.swap(half, 0).start()
            self.bring(half).start()

    def take(self, stage):
        for half in range(2):
            self.take_half(half, stage)

    def take_half(self, half, stage):
        if stage == 0:
            self.bring(half).wait()
        self.swap(half, stage).wait()
        place = self.place(half, stage, True)
        free = [n for n, index in enumerate(place) if isinstance(index, slice)]

        def one(number, carry):
            group = lax.rem(number, self.groups)
            rest = lax.div(number, self.groups)
            index = list(place)
            there = []
            for n in free:
                index[n] = lax.rem(rest, 2)
                there.append(index[n])
                rest = lax.div(rest, 2)
            target = (group,) + tuple(index) + (self.span(half), slice(None))
            if stage == 0:
                arrived = self.zero[target]
            else:
                arrived = self.later[half][stage - 1][(group,) + tuple(there)]
            total = self.own[target].astype(jnp.float32) + arrived.astype(jnp.float32)
            self.own[target] = total.astype(jnp.bfloat16)
            return carry

        lax.fori_loop(0, self.groups * 2 ** len(free), one, 0)
        if stage + 1 < self.bits:
            self.swap(half, stage + 1).start()
        elif self.out is not None:
            for step in range(1, self.groups):
                self.hop(half, step).start()

    def export(self, target):
        for half in range(2):
            place = (slice(None),) + self.place(half, self.bits, True)
            target[:, self.span(half), :] = self.own[place + (self.span(half), slice(None))]

    def finish(self):
        for half in range(2):
            place = (self.group,) + self.place(half, self.bits, True)
            total = self.own[place + (self.span(half), slice(None))].astype(jnp.float32)
            for step in range(1, self.groups):
                self.hop(half, step).wait()
                total = total + self.ring[half][step - 1].astype(jnp.float32)
            self.out[self.span(half), :] = total


class Ring:
    def __init__(self, own, out, refs):
        self.own, self.out = own, out
        self.landed, self.send, self.got = refs
        self.groups = own.shape[0]
        self.group = lax.axis_index("dp")

    def hop(self, step):
        other = lax.rem(self.group + step, self.groups)
        return pltpu.make_async_remote_copy(
            src_ref=self.own.at[other],
            dst_ref=self.landed.at[step - 1],
            send_sem=self.send.at[step - 1],
            recv_sem=self.got.at[step - 1],
            device_id={"dp": other},
            device_id_type=MESH,
        )

    def start(self):
        for step in range(1, self.groups):
            self.hop(step).start()

    def finish(self):
        total = self.own[self.group].astype(jnp.float32)
        for step in range(1, self.groups):
            self.hop(step).wait()
            total = total + self.landed[step - 1].astype(jnp.float32)
        self.out[...] = total


def ring_scratch(shape):
    groups = shape[0]
    semaphores = pltpu.SemaphoreType.DMA((groups - 1,))
    return [pltpu.VMEM((groups - 1,) + shape[1:], jnp.bfloat16), semaphores, semaphores]


def shares_scratch(shape):
    groups, bits, columns = shape[0], len(shape) - 3, shape[-1]
    whole = pltpu.VMEM((groups,) + (2,) * (bits - 1) + shape[-2:], jnp.bfloat16)
    later = [
        pltpu.VMEM((groups,) + (2,) * (bits - 1 - stage) + (span[1], columns), jnp.bfloat16)
        for span in spans_of(shape[-2])
        for stage in range(1, bits)
    ]
    ring = [
        pltpu.VMEM((groups - 1, span[1], columns), jnp.bfloat16) for span in spans_of(shape[-2])
    ]
    semaphores = [(2,), (2, bits), (2, bits), (2, groups - 1), (2, groups - 1)]
    return [whole, whole, *later, *ring] + [pltpu.SemaphoreType.DMA(size) for size in semaphores]


def shares_of(packs, outs, refs):
    bits = len(packs[0].shape) - 3
    each = 2 + 2 * (bits - 1) + 2 + 5
    return [
        Shares(pack, out, refs[n * each : (n + 1) * each])
        for n, (pack, out) in enumerate(zip(packs, outs))
    ]


def greet(everyone, ring=True):
    emb, group = lax.axis_index("emb"), lax.axis_index("dp")
    owners, groups = lax.axis_size("emb"), lax.axis_size("dp")
    barrier = pltpu.get_barrier_semaphore()
    if everyone:
        others = [lax.rem(emb + step, owners) for step in range(1, owners)]
    else:
        others = [flipped(emb, bit) for bit in range(owners.bit_length() - 1)]
    for other in others:
        pl.semaphore_signal(barrier, inc=1, device_id={"emb": other}, device_id_type=MESH)
    for step in range(1, groups if ring else 1):
        other = lax.rem(group + step, groups)
        pl.semaphore_signal(barrier, inc=1, device_id={"dp": other}, device_id_type=MESH)
    pl.semaphore_wait(barrier, len(others) + (groups - 1 if ring else 0))


def blocks_of(array):
    owners, groups = lax.axis_size("emb"), lax.axis_size("dp")
    bits = owners.bit_length() - 1
    return array.reshape((groups,) + (2,) * bits + array.shape[1:])


def rows_of(array):
    devices = lax.axis_size("emb") * lax.axis_size("dp")
    return array.astype(jnp.bfloat16).reshape(devices, array.shape[0] // devices, array.shape[1])


def stacked(pieces):
    rows = sum(piece.shape[1] for piece in pieces)
    devices, _, columns = pieces[0].shape
    spare = -rows % 16
    if rows + spare < 32:
        spare = 32 - rows
    if spare:
        pieces = pieces + [jnp.zeros((devices, spare, columns), jnp.bfloat16)]
    return blocks_of(jnp.concatenate(pieces, 1))


def vector_rows(vectors, rows):
    devices = lax.axis_size("emb") * lax.axis_size("dp")
    wide = vectors[0].shape[0]
    piece = jnp.stack(vectors).astype(jnp.bfloat16).reshape(len(vectors), devices, -1)
    piece = jnp.swapaxes(piece, 0, 1).reshape(devices, 1, -1)
    return jnp.pad(piece, ((0, 0), (0, rows - 1), (0, wide - piece.shape[2])))


def table_scratch(groups, owners, columns, length, capacity):
    wide = groups * capacity
    return [
        pltpu.VMEM((groups, columns, length), jnp.bfloat16),
        pltpu.VMEM((owners, columns, wide), jnp.bfloat16),
        pltpu.VMEM((owners - 1, columns, wide), jnp.bfloat16),
        pltpu.SemaphoreType.DMA((1,)),
        pltpu.SemaphoreType.DMA((groups - 1,)),
        pltpu.SemaphoreType.DMA((groups - 1,)),
        pltpu.SemaphoreType.DMA((owners - 1,)),
        pltpu.SemaphoreType.DMA((owners - 1,)),
    ]


class Table:
    def __init__(self, grads, slots, ids, out, refs):
        self.grads, self.slots, self.ids, self.out = grads, slots, ids, out
        self.turned, self.packed, self.landed = refs[:3]
        self.local_sem, self.ring_send, self.ring_got, self.send, self.got = refs[3:]
        self.groups, self.columns, self.length = self.turned.shape
        self.owners, _, self.wide = self.packed.shape
        self.capacity = self.wide // self.groups
        self.emb = lax.axis_index("emb")
        self.group = lax.axis_index("dp")

    def bring(self):
        return pltpu.make_async_copy(
            self.grads.at[self.group], self.turned.at[0], self.local_sem.at[0]
        )

    def hop(self, step):
        other = lax.rem(self.group + step, self.groups)
        return pltpu.make_async_remote_copy(
            src_ref=self.grads.at[other],
            dst_ref=self.turned.at[step],
            send_sem=self.ring_send.at[step - 1],
            recv_sem=self.ring_got.at[step - 1],
            device_id={"dp": other},
            device_id_type=MESH,
        )

    def give(self, step):
        other = lax.rem(self.emb + step, self.owners)
        return pltpu.make_async_remote_copy(
            src_ref=self.packed.at[other],
            dst_ref=self.landed.at[step - 1],
            send_sem=self.send.at[step - 1],
            recv_sem=self.got.at[step - 1],
            device_id={"emb": other},
            device_id_type=MESH,
        )

    def start(self):
        self.bring().start()
        for step in range(1, self.groups):
            self.hop(step).start()

    def arrive(self):
        self.bring().wait()
        for step in range(1, self.groups):
            self.hop(step).wait()

    def sort(self, step):
        owner = lax.rem(self.emb + step, self.owners)
        rows = lax.broadcasted_iota(jnp.int32, (128, self.length), 0)
        tiles = []
        for tile in range(self.wide // 128):
            total = jnp.zeros((self.columns, 128), jnp.float32)
            for group in range(self.groups):
                low, high = group * self.capacity, (group + 1) * self.capacity
                if high <= tile * 128 or low >= (tile + 1) * 128:
                    continue
                slot = rows + (tile * 128 - low)
                inside = (slot >= 0) & (slot < self.capacity)
                wanted = jnp.where(inside, slot + owner * self.capacity, -2)
                hot = jnp.where(wanted == self.slots[group], 1.0, 0.0).astype(jnp.bfloat16)
                total = total + product_right(self.turned[group], hot)
            tiles.append(total.astype(jnp.bfloat16))
        self.packed[owner] = jnp.concatenate(tiles, 1)
        return owner

    def add(self, step, first):
        source = lax.rem(self.emb - step + self.owners, self.owners)
        rows, columns = self.out.shape
        count = 6 if rows % 48 == 0 else 1
        block = rows // count
        chunk = self.packed[self.emb] if step == 0 else self.landed[step - 1]

        def one(number, carry):
            base = pl.multiple_of(number * block, 8)
            places = base + lax.broadcasted_iota(jnp.int32, (block, self.wide), 0)
            hot = jnp.where(places == self.ids[source], 1.0, 0.0).astype(jnp.bfloat16)
            part = product_right(hot, chunk)
            if not first:
                part = part + self.out[pl.ds(base, block), :]
            self.out[pl.ds(base, block), :] = part
            return carry

        lax.fori_loop(0, count, one, 0)


class Residual:
    def __init__(self, counts, grads, place, sources, weights, out, refs):
        self.counts, self.grads, self.place, self.out = counts, grads, place, out
        self.pixels, self.first, self.act, self.slope = sources
        self.w_a, self.w_b = weights
        self.mixed, self.inner, self.spots, self.pack = refs

    def rows_back(self):
        length, width = self.grads.shape
        block = min(512, length)

        def one(number, carry):
            base = pl.multiple_of(number * block, block)
            rows = pl.ds(base, block)
            token = base + lax.broadcasted_iota(jnp.int32, (block, width), 0)
            image = jnp.where(token < self.counts[0, 0], self.grads[rows, :], 0.0)
            mixed = image.astype(jnp.bfloat16)
            self.mixed[rows, :] = mixed
            inner = product_right(mixed, self.w_b[...]) * self.slope[rows, :].astype(jnp.float32)
            inner = inner.astype(jnp.bfloat16)
            self.inner[rows, :] = inner
            self.out[rows, :] = (image + product_right(inner, self.w_a[...])).astype(jnp.bfloat16)
            return carry

        lax.fori_loop(0, length // block, one, 0)

    def weights(self):
        length, width = self.grads.shape
        groups, bits = self.pack.shape[0], len(self.pack.shape) - 3
        devices = groups << bits
        share = width // devices
        places = self.spots.shape[0]
        spot = lax.broadcasted_iota(jnp.int32, (places, length), 0)
        hot = jnp.where(spot == self.place[...], 1.0, 0.0).astype(jnp.bfloat16)
        self.spots[...] = product(hot, self.mixed[...])
        spare = self.pack.shape[-2] - 3 * share - places // devices
        part = 384
        for start in range(0, width, part):
            span = slice(start, start + part)
            pieces = [
                product_left(self.pixels[:, span], self.out[...]),
                product_left(self.first[:, span], self.inner[...]),
                product_left(self.act[:, span], self.mixed[...]),
            ]
            for place in range(part // share):
                device = start // share + place
                rows = [piece[place * share : (place + 1) * share] for piece in pieces]
                each = places // devices
                rows.append(self.spots[device * each : (device + 1) * each, :])
                if spare:
                    rows.append(jnp.zeros((spare, width), jnp.float32))
                owner = device % (1 << bits)
                index = tuple((owner >> bit) & 1 for bit in range(bits - 1, -1, -1))
                self.pack[(device >> bits,) + index] = jnp.concatenate(rows, 0).astype(
                    jnp.bfloat16
                )


def tail_kernel(inside, grads_ref, slots_ref, ids_ref, *refs):
    if inside:
        inputs, refs = refs[:10], refs[10:]
        table_out, *outs = refs[:3]
        low_ref, refs = refs[3], refs[4:]
        residual = Residual(
            inputs[1], inputs[2], inputs[3], inputs[4:8], inputs[8:10], low_ref, refs[:4]
        )
        packs = [inputs[0], residual.pack]
        refs = refs[4:]
    else:
        packs, (table_out, *outs), refs = refs[:2], refs[2:5], refs[5:]
    table = Table(grads_ref, slots_ref, ids_ref, table_out, refs[:8])
    first, second = shares_of(packs, outs, refs[8:])
    owners = table.owners
    greet(True)
    table.start()
    first.start()
    if inside:
        residual.rows_back()
        first.take(0)
        residual.weights()
        second.start()
    else:
        second.start()
        first.take(0)
    for stage in range(1, first.bits):
        first.take(stage)
        second.take(stage - 1)
    second.take(second.bits - 1)
    table.arrive()
    for step in range(1, owners):
        table.sort(step)
        table.give(step).start()
    table.sort(0)
    table.add(0, True)
    first.finish()
    second.finish()
    for step in range(1, owners):
        table.give(step).wait()
        table.add(step, False)


def tail(grads, slots, ids, pack, extra, table_rows, capacity, inside):
    groups, columns, length = grads.shape
    owners = ids.shape[0]
    anywhere = pl.BlockSpec(memory_space=pl.ANY)
    vmem = pl.BlockSpec(memory_space=pltpu.VMEM)
    smem = pl.BlockSpec(memory_space=pltpu.SMEM)
    width = pack.shape[-1]
    own = []
    outs = [jax.ShapeDtypeStruct((table_rows, columns), jnp.float32)]
    outs.append(jax.ShapeDtypeStruct(pack.shape[-2:], jnp.float32))
    if inside:
        devices = groups * owners
        rows = 3 * (width // devices) + inside // devices
        rows = max(32, rows + -rows % 16)
        shape = pack.shape[:-2] + (rows, width)
        own = [
            pltpu.VMEM((length, width), jnp.bfloat16),
            pltpu.VMEM((length, width), jnp.bfloat16),
            pltpu.VMEM((inside, width), jnp.float32),
            pltpu.VMEM(shape, jnp.bfloat16),
        ]
        specs = [anywhere, smem] + [vmem] * 8
        outs.append(jax.ShapeDtypeStruct(shape[-2:], jnp.float32))
        outs.append(jax.ShapeDtypeStruct((length, width), jnp.bfloat16))
    else:
        shape = extra[0].shape
        specs = [anywhere, anywhere]
        outs.append(jax.ShapeDtypeStruct(shape[-2:], jnp.float32))
    scratch = own + table_scratch(groups, owners, columns, length, capacity)
    scratch = scratch + shares_scratch(pack.shape) + shares_scratch(shape)
    return pl.pallas_call(
        functools.partial(tail_kernel, inside),
        in_specs=[anywhere, vmem, vmem] + specs,
        out_specs=[vmem] * len(outs),
        out_shape=outs,
        scratch_shapes=scratch,
        compiler_params=pltpu.CompilerParams(
            collective_id=3, has_side_effects=True, vmem_limit_bytes=60 << 20
        ),
        name="tail",
    )(grads, slots, ids, pack, *extra)


def column_of(row, rows):
    diagonal = lax.broadcasted_iota(jnp.int32, (128, 128), 0) == lax.broadcasted_iota(
        jnp.int32, (128, 128), 1
    )
    pieces = [
        jnp.sum(jnp.where(diagonal, row[:, start : start + 128], 0), 1, keepdims=True)
        for start in range(0, rows, 128)
    ]
    return jnp.concatenate(pieces, 0)


def gelu_pair(value):
    root = 0.7978845608028654
    square = value * value
    bend = jnp.tanh(root * (value + 0.044715 * (value * square)))
    half = 0.5 * (1.0 + bend)
    slope = half + 0.5 * value * (1.0 - bend * bend) * (root * (1.0 + 3 * 0.044715 * square))
    return value * half, slope


def front_kernel(
    counts_ref,
    codes_ref,
    place_ref,
    pixels_ref,
    table_ref,
    pos_ref,
    w_patch_ref,
    w_a_ref,
    w_b_ref,
    gain_ref,
    bias_ref,
    embedded_ref,
    normed_ref,
    first_ref,
    act_ref,
    slope_ref,
    ids_ref,
    slots_ref,
    codes_all,
    ranks,
    earlier,
    held,
    packed,
    landed,
    fetched,
    mixed,
    local_sem,
    ask_send,
    ask_got,
    send,
    got,
):
    owners, capacity, width = packed.shape
    length = codes_ref.shape[1]
    table_rows = held.shape[0]
    emb = lax.axis_index("emb")
    bring = pltpu.make_async_copy(table_ref, held, local_sem.at[0])
    bring.start()
    barrier = pltpu.get_barrier_semaphore()
    for step in range(1, owners):
        other = lax.rem(emb + step, owners)
        pl.semaphore_signal(barrier, inc=1, device_id={"emb": other}, device_id_type=MESH)
    pl.semaphore_wait(barrier, owners - 1)

    def ask(step):
        return pltpu.make_async_remote_copy(
            src_ref=codes_ref,
            dst_ref=codes_all.at[step],
            send_sem=ask_send.at[step - 1],
            recv_sem=ask_got.at[step - 1],
            device_id={"emb": lax.rem(emb + step, owners)},
            device_id_type=MESH,
        )

    def give(step):
        return pltpu.make_async_remote_copy(
            src_ref=packed.at[step],
            dst_ref=landed.at[step - 1],
            send_sem=send.at[step - 1],
            recv_sem=got.at[step - 1],
            device_id={"emb": lax.rem(emb - step + owners, owners)},
            device_id_type=MESH,
        )

    for step in range(1, owners):
        ask(step).start()
    codes_all[0] = codes_ref[...]
    block = min(256, length)

    def triangle(number, carry):
        base = pl.multiple_of(number * block, block)
        above = base + lax.broadcasted_iota(jnp.int32, (block, length), 0)
        below = lax.broadcasted_iota(jnp.int32, (block, length), 1)
        earlier[pl.ds(base, block), :] = jnp.where(above < below, 1.0, 0.0).astype(jnp.bfloat16)
        return carry

    lax.fori_loop(0, length // block, triangle, 0)
    codes = codes_ref[...]
    mine = [
        (codes >= owner * table_rows) & (codes < (owner + 1) * table_rows)
        for owner in range(owners)
    ]
    marks = jnp.concatenate([jnp.where(mark, 1.0, 0.0) for mark in mine], 0)
    places = product(marks.astype(jnp.bfloat16), earlier[...])
    slots = jnp.full((1, length), owners * capacity, jnp.int32)
    for owner in range(owners):
        rank = places[owner : owner + 1].astype(jnp.int32)
        slots = jnp.where(mine[owner], owner * capacity + rank, slots)
    slots_ref[...] = slots
    for step in range(1, owners):
        ask(step).wait()
    local = codes_all[...].reshape(owners, length) - emb * table_rows
    inside = (local >= 0) & (local < table_rows)
    places = product(jnp.where(inside, 1.0, 0.0).astype(jnp.bfloat16), earlier[...])
    ranks[...] = jnp.where(inside, places.astype(jnp.int32), -1).reshape(owners, 1, length)
    bring.wait()

    def gather(step):
        rank = ranks[step]
        local = codes_all[step] - emb * table_rows + 1
        slot = lax.broadcasted_iota(jnp.int32, (capacity, length), 0)
        match = slot == rank
        hot = jnp.where(match, 1.0, 0.0).astype(jnp.bfloat16)
        coarse = lax.div(local, 64)
        fine = local - coarse * 64
        inner = rank >= 0
        pair = jnp.concatenate(
            [jnp.where(inner, coarse, 0), jnp.where(inner, fine, 0)]
            + [jnp.zeros((6, length), jnp.int32)],
            0,
        )
        pair = product_right(pair.astype(jnp.float32).astype(jnp.bfloat16), hot)
        source = lax.rem(emb - step + owners, owners)
        ids_ref[source] = (pair[0:1] * 64.0 + pair[1:2]).astype(jnp.int32) - 1
        wanted = jnp.sum(jnp.where(match, local, 0), 1, keepdims=True) - 1
        total = jnp.zeros((capacity, width), jnp.float32)
        for start in range(0, table_rows, 1024):
            size = min(1024, table_rows - start)
            row = start + lax.broadcasted_iota(jnp.int32, (capacity, size), 1)
            hot = jnp.where(row == wanted, 1.0, 0.0).astype(jnp.bfloat16)
            total = total + product(hot, held[start : start + size, :])
        packed[step] = total.astype(jnp.bfloat16)

    def serve(step, carry):
        gather(step)
        give(step).start()
        return carry

    lax.fori_loop(1, owners, serve, 0)
    gather(0)
    slot_column = column_of(slots, length)
    fetched[...] = jnp.zeros_like(fetched)

    def place_rows(step):
        owner = lax.rem(emb + step, owners)
        rows = packed[0] if step == 0 else landed[step - 1]
        for start in range(0, length, block):
            slot = owner * capacity + lax.broadcasted_iota(jnp.int32, (block, capacity), 1)
            hot = jnp.where(slot == slot_column[start : start + block], 1.0, 0.0)
            fetched[start : start + block, :] += product(hot.astype(jnp.bfloat16), rows)


    def patches(number, carry):
        base = pl.multiple_of(number * block, block)
        rows = pl.ds(base, block)
        first = product(pixels_ref[rows, :], w_patch_ref[...])
        low = first.astype(jnp.bfloat16)
        first_ref[rows, :] = low
        act, slope = gelu_pair(product(low, w_a_ref[...]))
        act = act.astype(jnp.bfloat16)
        act_ref[rows, :] = act
        slope_ref[rows, :] = slope.astype(jnp.bfloat16)
        mixed[rows, :] = first + product(act, w_b_ref[...])
        return carry

    lax.fori_loop(0, length // block, patches, 0)

    def positions(number, carry):
        base = pl.multiple_of(number * block, block)
        spot = lax.broadcasted_iota(jnp.int32, (block, pos_ref.shape[0]), 1)
        place = column_of(place_ref[:, pl.ds(base, block)], block)
        hot = jnp.where(spot == place, 1.0, 0.0).astype(jnp.bfloat16)
        embedded_ref[pl.ds(base, block), :] = product(hot, pos_ref[...])
        return carry

    lax.fori_loop(0, length // block, positions, 0)
    place_rows(0)
    for step in range(1, owners):
        give(step).wait()
        place_rows(step)

    def settle(number, carry):
        base = pl.multiple_of(number * block, block)
        rows = pl.ds(base, block)
        token = base + lax.broadcasted_iota(jnp.int32, (block, width), 0)
        image = mixed[rows, :] + embedded_ref[rows, :]
        value = jnp.where(token < counts_ref[0, 0], image, fetched[rows, :])
        embedded_ref[rows, :] = value
        normed = normalize(value) * gain_ref[...] + bias_ref[...]
        normed_ref[rows, :] = normed.astype(jnp.bfloat16)
        return carry

    lax.fori_loop(0, length // block, settle, 0)


def front(counts, codes, place, pixels, table, pos, w_patch, w_a, w_b, gain, bias, capacity):
    owners = lax.axis_size("emb")
    length, width = pixels.shape
    vmem = pl.BlockSpec(memory_space=pltpu.VMEM)
    low = jax.ShapeDtypeStruct((length, width), jnp.bfloat16)
    full = jax.ShapeDtypeStruct((length, width), jnp.float32)
    return pl.pallas_call(
        front_kernel,
        in_specs=[pl.BlockSpec(memory_space=pltpu.SMEM), vmem, vmem, vmem]
        + [pl.BlockSpec(memory_space=pl.ANY)]
        + [vmem] * 6,
        out_specs=[vmem] * 7,
        out_shape=[
            full,
            low,
            low,
            low,
            low,
            jax.ShapeDtypeStruct((owners, 1, capacity), jnp.int32),
            jax.ShapeDtypeStruct((1, length), jnp.int32),
        ],
        scratch_shapes=[
            pltpu.VMEM((owners, 1, length), jnp.int32),
            pltpu.VMEM((owners, 1, length), jnp.int32),
            pltpu.VMEM((length, length), jnp.bfloat16),
            pltpu.VMEM(table.shape, jnp.bfloat16),
            pltpu.VMEM((owners, capacity, width), jnp.bfloat16),
            pltpu.VMEM((owners - 1, capacity, width), jnp.bfloat16),
            pltpu.VMEM((length, width), jnp.float32),
            pltpu.VMEM((length, width), jnp.float32),
            pltpu.SemaphoreType.DMA((1,)),
            pltpu.SemaphoreType.DMA((owners - 1,)),
            pltpu.SemaphoreType.DMA((owners - 1,)),
            pltpu.SemaphoreType.DMA((owners - 1,)),
            pltpu.SemaphoreType.DMA((owners - 1,)),
        ],
        compiler_params=pltpu.CompilerParams(
            collective_id=1, has_side_effects=True, vmem_limit_bytes=56 << 20
        ),
        name="front",
    )(counts, codes, place, pixels, table, pos, w_patch, w_a, w_b, gain, bias)


def feed_kernel(
    attended_ref,
    embedded_ref,
    cotangent_ref,
    w_o_ref,
    gain_ref,
    bias_ref,
    w_up_ref,
    w_down_ref,
    output_ref,
    grad_middle_ref,
    grad_up_ref,
    grad_attended_ref,
    grad_w_o_ref,
    gains_ref,
    part_ref,
    middle,
    normed,
    back,
    slopes,
    hidden,
    pack,
    *refs,
):
    (share,) = shares_of([pack], [None], refs)
    groups, length, chunk = slopes.shape
    bits = share.bits
    owners = 1 << bits
    width = middle.shape[1]
    step = pl.program_id(0)
    block = min(512, length)
    blocks = length // block

    @pl.when(step == 0)
    def begin():
        greet(False, ring=False)

        def one(number, carry):
            rows = pl.ds(pl.multiple_of(number * block, block), block)
            value = embedded_ref[rows, :] + product_left(attended_ref[:, rows], w_o_ref[...])
            middle[rows, :] = value
            normed[rows, :] = (normalize(value) * gain_ref[...] + bias_ref[...]).astype(
                jnp.bfloat16
            )
            return carry

        lax.fori_loop(0, blocks, one, 0)

    @pl.when(step < groups)
    def go_forward():
        def one(number, carry):
            rows = pl.ds(pl.multiple_of(number * block, block), block)
            act, slope = gelu_pair(product(normed[rows, :], w_up_ref[...]))
            act = act.astype(jnp.bfloat16)
            hidden[rows, :] = act
            slopes[step, rows, :] = slope.astype(jnp.bfloat16)
            grown = product(act, w_down_ref[...])

            @pl.when(step == 0)
            def first():
                grad_middle_ref[rows, :] = middle[rows, :] + grown

            @pl.when(step > 0)
            def other():
                grad_middle_ref[rows, :] = grad_middle_ref[rows, :] + grown

            return carry

        lax.fori_loop(0, blocks, one, 0)
        units = chunk // owners
        spare = pack.shape[-2] - units
        part = 384 if chunk % 384 == 0 and 384 % units == 0 else chunk
        for start in range(0, chunk, part):
            grads = product_left(hidden[:, start : start + part], cotangent_ref[...])
            for place in range(part // units):
                piece = grads[place * units : (place + 1) * units]
                if spare:
                    piece = jnp.concatenate([piece, jnp.zeros((spare, width), jnp.float32)], 0)
                owner = start // units + place
                index = tuple((owner >> bit) & 1 for bit in range(bits - 1, -1, -1))
                pack[(step,) + index] = piece.astype(jnp.bfloat16)

    @pl.when(step == groups - 1)
    def turn():
        output_ref[...] = grad_middle_ref[...].astype(jnp.bfloat16)
        share.start()

    @pl.when(step == groups + 1)
    def swap():
        share.take(0)

    @pl.when(step >= groups)
    def go_back():
        def one(number, carry):
            rows = pl.ds(pl.multiple_of(number * block, block), block)
            slope = slopes[step - groups, rows, :].astype(jnp.float32)
            grads = product_right(cotangent_ref[rows, :], w_down_ref[...]) * slope
            grads = grads.astype(jnp.bfloat16)
            hidden[rows, :] = grads
            lower = product_right(grads, w_up_ref[...])

            @pl.when(step == groups)
            def first():
                back[rows, :] = lower

            @pl.when(step > groups)
            def other():
                back[rows, :] = back[rows, :] + lower

            return carry

        lax.fori_loop(0, blocks, one, 0)
        for start in range(0, width, 768):
            span = slice(start, start + 768)
            grad_up_ref[0, span, :] = product_left(normed[:, span], hidden[...]).astype(
                jnp.bfloat16
            )

    @pl.when(step == 2 * groups - 1)
    def end():
        share.take(1)
        gains_ref[...] = jnp.zeros_like(gains_ref)

        def one(number, carry):
            rows = pl.ds(pl.multiple_of(number * block, block), block)
            value = middle[rows, :]
            centred = value - jnp.mean(value, -1, keepdims=True)
            scale = lax.rsqrt(jnp.mean(centred * centred, -1, keepdims=True) + 1e-05)
            unit = centred * scale
            grads = back[rows, :]
            gains_ref[0:1, :] += jnp.sum(grads * unit, 0, keepdims=True)
            gains_ref[1:2, :] += jnp.sum(grads, 0, keepdims=True)
            grads = grads * gain_ref[...]
            along = jnp.mean(grads * unit, -1, keepdims=True)
            grads = scale * (grads - jnp.mean(grads, -1, keepdims=True) - unit * along)
            grads = cotangent_ref[rows, :].astype(jnp.float32) + grads
            grad_middle_ref[rows, :] = grads
            normed[rows, :] = grads.astype(jnp.bfloat16)
            return carry

        lax.fori_loop(0, blocks, one, 0)
        for start in range(0, width, 256):
            span = slice(start, start + 256)
            grad_w_o_ref[span, :] = product(attended_ref[span, :], normed[...]).astype(
                jnp.bfloat16
            )
            grad_attended_ref[span, :] = product_right(w_o_ref[span, :], normed[...]).astype(
                jnp.bfloat16
            )
        for stage in range(2, bits):
            share.take(stage)
        share.export(part_ref)


def feed(attended, embedded, cotangent, w_o, gain, bias, w_up, w_down):
    groups, owners = lax.axis_size("dp"), lax.axis_size("emb")
    length, width = embedded.shape
    chunk = w_up.shape[1] // groups
    units = chunk // owners
    units = max(32, units + -units % 16)
    shape = (groups,) + (2,) * (owners.bit_length() - 1) + (units, width)
    once = pl.Buffered(1)

    def whole(array):
        return pl.BlockSpec(array.shape, lambda s: (0, 0), pipeline_mode=once)

    outs = [
        jax.ShapeDtypeStruct((length, width), jnp.bfloat16),
        jax.ShapeDtypeStruct((length, width), jnp.float32),
        jax.ShapeDtypeStruct((groups, width, chunk), jnp.bfloat16),
        jax.ShapeDtypeStruct((width, length), jnp.bfloat16),
        jax.ShapeDtypeStruct((width, width), jnp.bfloat16),
        jax.ShapeDtypeStruct((8, width), jnp.float32),
        jax.ShapeDtypeStruct((groups, units, width), jnp.bfloat16),
    ]
    out_specs = [whole(out) if len(out.shape) == 2 else None for out in outs]
    out_specs[2] = pl.BlockSpec((1, width, chunk), lambda s: (jnp.maximum(s - groups, 0), 0, 0))
    out_specs[6] = pl.BlockSpec(outs[6].shape, lambda s: (0, 0, 0), pipeline_mode=once)
    return pl.pallas_call(
        feed_kernel,
        grid=(2 * groups,),
        in_specs=[
            whole(attended),
            whole(embedded),
            whole(cotangent),
            whole(w_o),
            whole(gain),
            whole(bias),
            pl.BlockSpec((width, chunk), lambda s: (0, lax.rem(s, groups))),
            pl.BlockSpec((chunk, width), lambda s: (lax.rem(s, groups), 0)),
        ],
        out_specs=out_specs,
        out_shape=outs,
        scratch_shapes=[
            pltpu.VMEM((length, width), jnp.float32),
            pltpu.VMEM((length, width), jnp.bfloat16),
            pltpu.VMEM((length, width), jnp.float32),
            pltpu.VMEM((groups, length, chunk), jnp.bfloat16),
            pltpu.VMEM((length, chunk), jnp.bfloat16),
            pltpu.VMEM(shape, jnp.bfloat16),
        ]
        + shares_scratch(shape),
        compiler_params=pltpu.CompilerParams(
            collective_id=4, has_side_effects=True, vmem_limit_bytes=58 << 20
        ),
        name="feed",
    )(attended, embedded, cotangent, w_o, gain, bias, w_up, w_down)


def first_kernel(
    heads_ref,
    w_q_ref,
    w_k_ref,
    w_v_ref,
    embedded_ref,
    middle_ref,
    normed_ref,
    gain_ref,
    grad_ref,
    turned_ref,
    weights_ref,
    gains_ref,
    back,
    normed_turned,
):
    length, width = embedded_ref.shape
    block = min(512, length)
    gains_ref[...] = jnp.zeros_like(gains_ref)

    def rows_back(number, carry):
        base = pl.multiple_of(number * block, block)
        rows = pl.ds(base, block)
        back[...] = product(w_q_ref[...], heads_ref[0:width, rows])
        back[...] += product(w_k_ref[...], heads_ref[width : 2 * width, rows])
        back[...] += product(w_v_ref[...], heads_ref[2 * width :, rows])
        grads = back[...].T
        value = embedded_ref[rows, :]
        centred = value - jnp.mean(value, -1, keepdims=True)
        scale = lax.rsqrt(jnp.mean(centred * centred, -1, keepdims=True) + 1e-05)
        unit = centred * scale
        gains_ref[0:1, :] += jnp.sum(grads * unit, 0, keepdims=True)
        gains_ref[1:2, :] += jnp.sum(grads, 0, keepdims=True)
        grads = grads * gain_ref[...]
        along = jnp.mean(grads * unit, -1, keepdims=True)
        grads = scale * (grads - jnp.mean(grads, -1, keepdims=True) - unit * along)
        grads = middle_ref[rows, :] + grads
        grad_ref[rows, :] = grads
        turned_ref[:, rows] = grads.T.astype(jnp.bfloat16)
        normed_turned[:, rows] = normed_ref[rows, :].astype(jnp.float32).T.astype(jnp.bfloat16)
        return carry

    lax.fori_loop(0, length // block, rows_back, 0)

    def weights(number, carry):
        base = pl.multiple_of(number * width, width)
        weights_ref[number] = product_right(
            normed_turned[...], heads_ref[pl.ds(base, width), :]
        ).astype(jnp.bfloat16)
        return carry

    lax.fori_loop(0, 3, weights, 0)


def first_backward(heads, w_q, w_k, w_v, embedded, middle, normed, gain):
    length, width = embedded.shape
    vmem = pl.BlockSpec(memory_space=pltpu.VMEM)
    return pl.pallas_call(
        first_kernel,
        in_specs=[vmem] * 8,
        out_specs=[vmem] * 4,
        out_shape=[
            jax.ShapeDtypeStruct((length, width), jnp.float32),
            jax.ShapeDtypeStruct((width, length), jnp.bfloat16),
            jax.ShapeDtypeStruct((3, width, width), jnp.bfloat16),
            jax.ShapeDtypeStruct((8, width), jnp.float32),
        ],
        scratch_shapes=[
            pltpu.VMEM((width, min(512, length)), jnp.float32),
            pltpu.VMEM((width, length), jnp.bfloat16),
        ],
        compiler_params=pltpu.CompilerParams(vmem_limit_bytes=56 << 20),
        name="first_backward",
    )(heads, w_q, w_k, w_v, embedded, middle, normed, gain)


def on_device(
    pixels,
    counts,
    token_ids,
    action_bins,
    patch_pos,
    token_table,
    pos_table,
    w_patch,
    w_res_a,
    w_res_b,
    gain_one,
    bias_one,
    w_q,
    w_k,
    w_v,
    w_o,
    gain_two,
    bias_two,
    w_up,
    w_down,
    cotangent,
):
    length = pixels.shape[0]
    model_width = w_q.shape[0]
    positions = jnp.arange(length)
    image_rows = positions < counts[0, 0]
    action_rows = positions >= length - counts[0, 1]
    table_rows = jnp.logical_not(image_rows)
    row_ids = jnp.where(action_rows, TEXT_VOCAB + action_bins, token_ids)
    rows_owned = token_table.shape[0]
    owners_total = lax.axis_size("emb")
    capacity = 3 * length // (2 * owners_total)
    groups = lax.axis_size("dp")
    codes = jnp.where(table_rows, row_ids, -1).reshape(1, length)
    gain_row = gain_one.astype(jnp.float32).reshape(1, model_width)
    bias_row = bias_one.astype(jnp.float32).reshape(1, model_width)
    embedded, normed_one, first_low, res_act, res_slope, ids, slots = front(
        counts,
        codes,
        patch_pos.reshape(1, length),
        pixels,
        token_table,
        pos_table,
        w_patch,
        w_res_a,
        w_res_b,
        gain_row,
        bias_row,
        capacity,
    )
    facts = jnp.concatenate([ids.reshape(-1), slots.reshape(-1)])
    ring = [facts] + [
        lax.ppermute(facts, "dp", [(i, (i + step) % groups) for i in range(groups)])
        for step in range(1, groups)
    ]
    ring = jnp.stack(ring)
    ring_ids = ring[:, : owners_total * capacity].reshape(groups, owners_total, capacity)
    ring_ids = jnp.swapaxes(ring_ids, 0, 1).reshape(owners_total, 1, groups * capacity)
    ring_slots = ring[:, owners_total * capacity :].reshape(groups, 1, length)
    queries = contract(w_q, normed_one, 0, 1).astype(jnp.bfloat16)
    key_heads = contract(w_k, normed_one, 0, 1).astype(jnp.bfloat16)
    value_heads = contract(w_v, normed_one, 0, 1).astype(jnp.bfloat16)
    attended, probs, inverse = attention_forward(queries, key_heads, value_heads)
    output, grad_middle, grad_w_up, grad_attended, grad_w_o, gains, part_down = feed(
        attended,
        embedded,
        cotangent,
        w_o,
        gain_two.astype(jnp.float32).reshape(1, model_width),
        bias_two.astype(jnp.float32).reshape(1, model_width),
        w_up,
        w_down,
    )
    devices = groups * owners_total
    share = model_width // devices
    folds = w_up.shape[1] // model_width
    per_fold = groups // folds
    folded = []
    for n in range(folds):
        pieces = [grad_w_up[n * per_fold + m] for m in range(per_fold)]
        folded.append(rows_of(jnp.concatenate(pieces, 1) if per_fold > 1 else pieces[0]))
    grad_heads, share_one, share_two, share_down = attention_backward(
        queries,
        key_heads,
        value_heads,
        attended,
        grad_attended,
        probs,
        inverse,
        [
            stacked(folded[:2] + [rows_of(grad_w_o), vector_rows([gains[0], gains[1]], 8)]),
            stacked(folded[2:]),
        ],
        part_down,
    )
    grad_heads = grad_heads.reshape(3 * model_width, length)
    grad_embedded, grads_turned, grad_w_heads, gains = first_backward(
        grad_heads, w_q, w_k, w_v, embedded, grad_middle, normed_one, gain_row
    )
    gains_one = vector_rows([gains[0], gains[1]], 8)
    grad_w_heads = [rows_of(grad_w_heads[n]) for n in range(3)]
    columns = model_width // groups
    grads_turned = grads_turned.reshape(groups, columns, length)
    pos_rows = pos_table.shape[0]
    pos_share = pos_rows // devices
    pack_heads = stacked(grad_w_heads + [gains_one])
    if share % 8 == 0 and 384 % share == 0 and pos_share % 8 == 0:
        grad_table, share_heads, share_res, grad_first = tail(
            grads_turned,
            ring_slots,
            ring_ids,
            pack_heads,
            [
                counts,
                grad_embedded,
                patch_pos.reshape(1, length),
                pixels,
                first_low,
                res_act,
                res_slope,
                w_res_a,
                w_res_b,
            ],
            rows_owned,
            capacity,
            pos_rows,
        )
    else:
        grad_image = jnp.where(image_rows[:, None], grad_embedded, 0.0)
        grad_mixed = grad_image.astype(jnp.bfloat16)
        position_hot = patch_pos[:, None] == jnp.arange(pos_rows)[None, :]
        grad_pos_table = product_left(position_hot.astype(jnp.bfloat16), grad_mixed)
        grad_w_res_b = product_left(res_act, grad_mixed)
        grad_inner = product_right(grad_mixed, w_res_b) * res_slope.astype(jnp.float32)
        grad_inner = grad_inner.astype(jnp.bfloat16)
        grad_w_res_a = product_left(first_low, grad_inner)
        grad_first = (grad_image + product_right(grad_inner, w_res_a)).astype(jnp.bfloat16)
        grad_w_patch = product_left(pixels, grad_first)
        res_rows = [rows_of(g) for g in (grad_w_patch, grad_w_res_a, grad_w_res_b, grad_pos_table)]
        grad_table, share_heads, share_res = tail(
            grads_turned,
            ring_slots,
            ring_ids,
            pack_heads,
            [stacked(res_rows)],
            rows_owned,
            capacity,
            0,
        )
    grad_pixels = product_right(grad_first, w_patch)

    def cut(array, place):
        return array[place * share : (place + 1) * share]

    rows_up = jnp.concatenate([share_one[: 2 * share], share_two[: (folds - 2) * share]], 0)
    share_w_up = jnp.swapaxes(rows_up.reshape(folds, share, model_width), 0, 1)
    gains_two = share_one[3 * share, : 2 * share]
    gains_one = share_heads[3 * share, : 2 * share]
    return (
        output,
        grad_pixels,
        grad_table,
        share_res[3 * share : 3 * share + pos_share],
        cut(share_res, 0),
        cut(share_res, 1),
        cut(share_res, 2),
        gains_one[:share],
        gains_one[share:],
        cut(share_heads, 0),
        cut(share_heads, 1),
        cut(share_heads, 2),
        cut(share_one, 2),
        gains_two[:share],
        gains_two[share:],
        share_w_up.reshape(share, folds * model_width),
        share_down[: w_down.shape[0] // devices],
    )


def solution(mesh):
    in_specs = (
        P(("dp", "emb"), None),
        P(("dp", "emb"), None),
        P(("dp", "emb")),
        P(("dp", "emb")),
        P(("dp", "emb")),
        P("emb", None),
        P(),
        P(),
        P(),
        P(),
        P(),
        P(),
        P(),
        P(),
        P(),
        P(),
        P(),
        P(),
        P(),
        P(),
        P(("dp", "emb"), None),
    )
    out_specs = (
        P(("dp", "emb"), None),
        P(("dp", "emb"), None),
        P("emb", "dp"),
        P(("dp", "emb"), None),
        P(("dp", "emb"), None),
        P(("dp", "emb"), None),
        P(("dp", "emb"), None),
        P(("dp", "emb")),
        P(("dp", "emb")),
        P(("dp", "emb"), None),
        P(("dp", "emb"), None),
        P(("dp", "emb"), None),
        P(("dp", "emb"), None),
        P(("dp", "emb")),
        P(("dp", "emb")),
        P(("dp", "emb"), None),
        P(("dp", "emb"), None),
    )
    return jax.shard_map(
        on_device, mesh=mesh, in_specs=in_specs, out_specs=out_specs, check_vma=False
    )
```

```python
import functools

import jax
import jax.numpy as jnp
from jax import lax
from jax.experimental import pallas as pl
from jax.experimental.pallas import tpu as pltpu
from jax.sharding import PartitionSpec as P

HEAD_DIM = 32
TEXT_VOCAB = 32000
BLOCK = 256
HEADS_STEP = 2
MESH = pl.DeviceIdType.MESH
LOG2_E = 1.4426950408889634


def normalize(values):
    average = jnp.mean(values, -1, keepdims=True)
    centred = values - average
    variance = jnp.mean(centred * centred, -1, keepdims=True)
    return centred * lax.rsqrt(variance + 1e-05)


def norm_affine(values, gain, offset):
    return normalize(values) * gain + offset


def contract(left, right, left_dim, right_dim):
    return lax.dot_general(
        left, right, (((left_dim,), (right_dim,)), ((), ())), preferred_element_type=jnp.float32
    )


def product(left, right):
    return contract(left, right, 1, 0)


def product_left(left, right):
    return contract(left, right, 0, 0)


def product_right(left, right):
    return contract(left, right, 1, 1)


def forward_kernel(heads, q_ref, k_ref, v_ref, o_ref, p_ref, r_ref):
    length = q_ref.shape[1]
    scaling = HEAD_DIM ** (-0.5) * LOG2_E
    key_place = lax.broadcasted_iota(jnp.int32, (BLOCK, BLOCK), 0)
    query_place = lax.broadcasted_iota(jnp.int32, (BLOCK, BLOCK), 1)
    allowed = key_place <= query_place
    for head in range(heads):
        rows = slice(head * HEAD_DIM, (head + 1) * HEAD_DIM)
        keys = k_ref[rows, :]
        values = v_ref[rows, :]
        for step in range(length // BLOCK):
            start, end = step * BLOCK, (step + 1) * BLOCK
            scores = contract(keys[:, :end], q_ref[rows, start:end], 0, 0) * scaling
            corner = jnp.where(allowed, scores[start:], -1e30)
            highest = jnp.max(corner, 0, keepdims=True)
            if step:
                highest = jnp.maximum(highest, jnp.max(scores[:start], 0, keepdims=True))
            weights = jnp.exp2(corner - highest)
            total = jnp.sum(weights, 0, keepdims=True)
            weights = weights.astype(jnp.bfloat16)
            if step:
                above = jnp.exp2(scores[:start] - highest)
                total = total + jnp.sum(above, 0, keepdims=True)
                weights = jnp.concatenate([above.astype(jnp.bfloat16), weights], 0)
            inverse = 1.0 / total
            base = BLOCK * (step * (step + 1) // 2)
            p_ref[head, base : base + end, :] = weights
            r_ref[head, :, start:end] = inverse
            o_ref[rows, start:end] = (
                contract(values[:, :end], weights, 1, 0) * inverse
            ).astype(jnp.bfloat16)


def packed_rows(length):
    steps = length // BLOCK
    return BLOCK * (steps * (steps + 1) // 2)


def attention_forward(queries, key_heads, values):
    width, length = queries.shape
    heads = width // HEAD_DIM
    packed = packed_rows(length)
    rows = pl.BlockSpec((HEADS_STEP * HEAD_DIM, length), lambda g: (g, 0))
    return pl.pallas_call(
        functools.partial(forward_kernel, HEADS_STEP),
        grid=(heads // HEADS_STEP,),
        in_specs=[rows] * 3,
        out_specs=[
            rows,
            pl.BlockSpec((HEADS_STEP, packed, BLOCK), lambda g: (g, 0, 0)),
            pl.BlockSpec((HEADS_STEP, 1, length), lambda g: (g, 0, 0)),
        ],
        out_shape=[
            jax.ShapeDtypeStruct((width, length), jnp.bfloat16),
            jax.ShapeDtypeStruct((heads, packed, BLOCK), jnp.bfloat16),
            jax.ShapeDtypeStruct((heads, 1, length), jnp.float32),
        ],
        compiler_params=pltpu.CompilerParams(vmem_limit_bytes=32 << 20),
        cost_estimate=pl.CostEstimate(
            flops=50_000_000_000, bytes_accessed=heads * packed * BLOCK * 2, transcendentals=0
        ),
        name="attention_forward",
    )(queries, key_heads, values)


def backward_kernel(
    heads,
    q_ref,
    k_ref,
    v_ref,
    o_ref,
    g_ref,
    p_ref,
    r_ref,
    pack_one,
    pack_two,
    part_ref,
    d_ref,
    out_one,
    out_two,
    ring_ref,
    s_ref,
    *refs,
):
    ring = Ring(part_ref, ring_ref, refs[:3])
    first, second = shares_of([pack_one, pack_two], [out_one, out_two], refs[3:])
    bits = first.bits
    number = pl.program_id(0)
    last = pl.num_programs(0) - 1

    @pl.when(number == 0)
    def begin():
        greet(False)
        first.start()
        second.start()
        ring.start()

    @pl.when(number == 1)
    def first_swap():
        first.take(0)

    @pl.when(number == 4)
    def next_swap():
        first.take(1)
        second.take(0)

    @pl.when(number == 7)
    def other_swaps():
        for stage in range(2, bits):
            first.take(stage)

    @pl.when(number == 8)
    def late_swap():
        second.take(1)

    @pl.when(number == 10)
    def last_swaps():
        for stage in range(2, bits):
            second.take(stage)

    length = q_ref.shape[1]
    steps = length // BLOCK
    scaling = HEAD_DIM ** (-0.5)
    for head in range(heads):
        rows = slice(head * HEAD_DIM, (head + 1) * HEAD_DIM)
        grads = (g_ref[rows, :].astype(jnp.float32) * r_ref[head]).astype(jnp.bfloat16)
        inner = jnp.sum(
            grads.astype(jnp.float32) * o_ref[rows, :].astype(jnp.float32), 0, keepdims=True
        )
        queries = q_ref[rows, :]
        keys = k_ref[rows, :]
        values = v_ref[rows, :]
        for step in range(steps):
            start, end = step * BLOCK, (step + 1) * BLOCK
            base = BLOCK * (step * (step + 1) // 2)
            grad_probs = contract(values[:, :end], grads[:, start:end], 0, 0)
            grad_scores = p_ref[head, base : base + end, :] * (
                grad_probs - inner[:, start:end]
            ).astype(jnp.bfloat16)
            s_ref[head, base : base + end, :] = grad_scores
            d_ref[0, rows, start:end] = (
                contract(keys[:, :end], grad_scores, 1, 0) * scaling
            ).astype(jnp.bfloat16)
        for column in range(steps):
            grad_keys = jnp.zeros((HEAD_DIM, BLOCK), jnp.float32)
            grad_values = jnp.zeros((HEAD_DIM, BLOCK), jnp.float32)
            for step in range(column, steps):
                base = BLOCK * (step * (step + 1) // 2 + column)
                span = slice(step * BLOCK, (step + 1) * BLOCK)
                grad_values = grad_values + contract(
                    grads[:, span], p_ref[head, base : base + BLOCK, :], 1, 1
                )
                grad_keys = grad_keys + contract(
                    queries[:, span], s_ref[head, base : base + BLOCK, :], 1, 1
                )
            span = slice(column * BLOCK, (column + 1) * BLOCK)
            d_ref[1, rows, span] = (grad_keys * scaling).astype(jnp.bfloat16)
            d_ref[2, rows, span] = grad_values.astype(jnp.bfloat16)

    @pl.when(number == last)
    def end():
        ring.finish()
        first.finish()
        second.finish()


def attention_backward(
    queries, key_heads, values, attended, grads, probs, inverse, packs, part
):
    width, length = queries.shape
    heads = width // HEAD_DIM
    packed = packed_rows(length)
    rows = pl.BlockSpec((HEADS_STEP * HEAD_DIM, length), lambda g: (g, 0))
    scratch = [pltpu.VMEM((HEADS_STEP, packed, BLOCK), jnp.bfloat16)]
    scratch = scratch + ring_scratch(part.shape)
    for pack in packs:
        scratch = scratch + shares_scratch(pack.shape)
    return pl.pallas_call(
        functools.partial(backward_kernel, HEADS_STEP),
        grid=(heads // HEADS_STEP,),
        in_specs=[rows] * 5
        + [
            pl.BlockSpec((HEADS_STEP, packed, BLOCK), lambda g: (g, 0, 0)),
            pl.BlockSpec((HEADS_STEP, 1, length), lambda g: (g, 0, 0)),
            pl.BlockSpec(memory_space=pl.ANY),
            pl.BlockSpec(memory_space=pl.ANY),
            pl.BlockSpec(part.shape, lambda g: (0, 0, 0)),
        ],
        out_specs=[
            pl.BlockSpec((3, HEADS_STEP * HEAD_DIM, length), lambda g: (0, g, 0)),
            pl.BlockSpec(packs[0].shape[-2:], lambda g: (0, 0)),
            pl.BlockSpec(packs[1].shape[-2:], lambda g: (0, 0)),
            pl.BlockSpec(part.shape[-2:], lambda g: (0, 0)),
        ],
        out_shape=[
            jax.ShapeDtypeStruct((3, width, length), jnp.bfloat16),
            jax.ShapeDtypeStruct(packs[0].shape[-2:], jnp.float32),
            jax.ShapeDtypeStruct(packs[1].shape[-2:], jnp.float32),
            jax.ShapeDtypeStruct(part.shape[-2:], jnp.float32),
        ],
        scratch_shapes=scratch,
        compiler_params=pltpu.CompilerParams(
            collective_id=2, has_side_effects=True, vmem_limit_bytes=56 << 20
        ),
        name="attention_backward",
    )(queries, key_heads, values, attended, grads, probs, inverse, *packs, part)


def bit_of(index, bit):
    return lax.rem(lax.div(index, 1 << bit), 2)


def flipped(index, bit):
    return index + (1 - 2 * bit_of(index, bit)) * (1 << bit)


def spans_of(rows):
    first = (rows + 31) // 32 * 16
    return ((0, first), (first, rows - first))


class Shares:
    def __init__(self, pack, out, refs):
        self.pack, self.out = pack, out
        self.groups = pack.shape[0]
        self.bits = len(pack.shape) - 3
        self.spans = spans_of(pack.shape[-2])
        refs = list(refs)
        self.own, self.zero = refs[:2]
        count = self.bits - 1
        self.later = [refs[2 + half * count : 2 + (half + 1) * count] for half in range(2)]
        refs = refs[2 + 2 * count :]
        self.ring = refs[:2]
        self.local_sem, self.swap_send, self.swap_got, self.ring_send, self.ring_got = refs[2:]
        self.emb = lax.axis_index("emb")
        self.group = lax.axis_index("dp")
        self.every = (slice(None),) * self.bits

    def order(self, half):
        rest = list(range(1, self.bits))
        return [0] + (rest if half == 0 else rest[::-1])

    def span(self, half):
        return pl.ds(*self.spans[half])

    def place(self, half, stage, mine):
        order = self.order(half)
        index = []
        for bit in range(self.bits - 1, 0, -1):
            value = bit_of(self.emb, bit)
            if order.index(bit) < stage:
                index.append(value)
            elif order.index(bit) == stage:
                index.append(value if mine else 1 - value)
            else:
                index.append(slice(None))
        return tuple(index)

    def swap(self, half, stage):
        if stage == 0:
            other = 1 - bit_of(self.emb, 0)
            source = self.pack.at[self.every + (other, self.span(half))]
            target = self.zero.at[self.every + (self.span(half),)]
        else:
            place = self.place(half, stage, False)
            source = self.own.at[(slice(None),) + place + (self.span(half),)]
            target = self.later[half][stage - 1]
        return pltpu.make_async_remote_copy(
            src_ref=source,
            dst_ref=target,
            send_sem=self.swap_send.at[half, stage],
            recv_sem=self.swap_got.at[half, stage],
            device_id={"emb": flipped(self.emb, self.order(half)[stage])},
            device_id_type=MESH,
        )

    def bring(self, half):
        mine = bit_of(self.emb, 0)
        return pltpu.make_async_copy(
            self.pack.at[self.every + (mine, self.span(half))],
            self.own.at[self.every + (self.span(half),)],
            self.local_sem.at[half],
        )

    def hop(self, half, step):
        other = lax.rem(self.group + step, self.groups)
        place = (other,) + self.place(half, self.bits, True) + (self.span(half),)
        return pltpu.make_async_remote_copy(
            src_ref=self.own.at[place],
            dst_ref=self.ring[half].at[step - 1],
            send_sem=self.ring_send.at[half, step - 1],
            recv_sem=self.ring_got.at[half, step - 1],
            device_id={"dp": other},
            device_id_type=MESH,
        )

    def start(self):
        for half in range(2):
            self.swap(half, 0).start()
            self.bring(half).start()

    def take(self, stage):
        for half in range(2):
            self.take_half(half, stage)

    def take_half(self, half, stage):
        if stage == 0:
            self.bring(half).wait()
        self.swap(half, stage).wait()
        place = self.place(half, stage, True)
        free = [n for n, index in enumerate(place) if isinstance(index, slice)]

        def one(number, carry):
            group = lax.rem(number, self.groups)
            rest = lax.div(number, self.groups)
            index = list(place)
            there = []
            for n in free:
                index[n] = lax.rem(rest, 2)
                there.append(index[n])
                rest = lax.div(rest, 2)
            target = (group,) + tuple(index) + (self.span(half), slice(None))
            if stage == 0:
                arrived = self.zero[target]
            else:
                arrived = self.later[half][stage - 1][(group,) + tuple(there)]
            total = self.own[target].astype(jnp.float32) + arrived.astype(jnp.float32)
            self.own[target] = total.astype(jnp.bfloat16)
            return carry

        lax.fori_loop(0, self.groups * 2 ** len(free), one, 0)
        if stage + 1 < self.bits:
            self.swap(half, stage + 1).start()
        elif self.out is not None:
            for step in range(1, self.groups):
                self.hop(half, step).start()

    def export(self, target):
        for half in range(2):
            place = (slice(None),) + self.place(half, self.bits, True)
            target[:, self.span(half), :] = self.own[place + (self.span(half), slice(None))]

    def finish(self):
        for half in range(2):
            place = (self.group,) + self.place(half, self.bits, True)
            total = self.own[place + (self.span(half), slice(None))].astype(jnp.float32)
            for step in range(1, self.groups):
                self.hop(half, step).wait()
                total = total + self.ring[half][step - 1].astype(jnp.float32)
            self.out[self.span(half), :] = total


class Ring:
    def __init__(self, own, out, refs):
        self.own, self.out = own, out
        self.landed, self.send, self.got = refs
        self.groups = own.shape[0]
        self.group = lax.axis_index("dp")

    def hop(self, step):
        other = lax.rem(self.group + step, self.groups)
        return pltpu.make_async_remote_copy(
            src_ref=self.own.at[other],
            dst_ref=self.landed.at[step - 1],
            send_sem=self.send.at[step - 1],
            recv_sem=self.got.at[step - 1],
            device_id={"dp": other},
            device_id_type=MESH,
        )

    def start(self):
        for step in range(1, self.groups):
            self.hop(step).start()

    def finish(self):
        total = self.own[self.group].astype(jnp.float32)
        for step in range(1, self.groups):
            self.hop(step).wait()
            total = total + self.landed[step - 1].astype(jnp.float32)
        self.out[...] = total


def ring_scratch(shape):
    groups = shape[0]
    semaphores = pltpu.SemaphoreType.DMA((groups - 1,))
    return [pltpu.VMEM((groups - 1,) + shape[1:], jnp.bfloat16), semaphores, semaphores]


def shares_scratch(shape):
    groups, bits, columns = shape[0], len(shape) - 3, shape[-1]
    whole = pltpu.VMEM((groups,) + (2,) * (bits - 1) + shape[-2:], jnp.bfloat16)
    later = [
        pltpu.VMEM((groups,) + (2,) * (bits - 1 - stage) + (span[1], columns), jnp.bfloat16)
        for span in spans_of(shape[-2])
        for stage in range(1, bits)
    ]
    ring = [
        pltpu.VMEM((groups - 1, span[1], columns), jnp.bfloat16) for span in spans_of(shape[-2])
    ]
    semaphores = [(2,), (2, bits), (2, bits), (2, groups - 1), (2, groups - 1)]
    return [whole, whole, *later, *ring] + [pltpu.SemaphoreType.DMA(size) for size in semaphores]


def shares_of(packs, outs, refs):
    bits = len(packs[0].shape) - 3
    each = 2 + 2 * (bits - 1) + 2 + 5
    return [
        Shares(pack, out, refs[n * each : (n + 1) * each])
        for n, (pack, out) in enumerate(zip(packs, outs))
    ]


def greet(everyone, ring=True):
    emb, group = lax.axis_index("emb"), lax.axis_index("dp")
    owners, groups = lax.axis_size("emb"), lax.axis_size("dp")
    barrier = pltpu.get_barrier_semaphore()
    if everyone:
        others = [lax.rem(emb + step, owners) for step in range(1, owners)]
    else:
        others = [flipped(emb, bit) for bit in range(owners.bit_length() - 1)]
    for other in others:
        pl.semaphore_signal(barrier, inc=1, device_id={"emb": other}, device_id_type=MESH)
    for step in range(1, groups if ring else 1):
        other = lax.rem(group + step, groups)
        pl.semaphore_signal(barrier, inc=1, device_id={"dp": other}, device_id_type=MESH)
    pl.semaphore_wait(barrier, len(others) + (groups - 1 if ring else 0))


def blocks_of(array):
    owners, groups = lax.axis_size("emb"), lax.axis_size("dp")
    bits = owners.bit_length() - 1
    return array.reshape((groups,) + (2,) * bits + array.shape[1:])


def rows_of(array):
    devices = lax.axis_size("emb") * lax.axis_size("dp")
    return array.astype(jnp.bfloat16).reshape(devices, array.shape[0] // devices, array.shape[1])


def stacked(pieces):
    rows = sum(piece.shape[1] for piece in pieces)
    devices, _, columns = pieces[0].shape
    spare = -rows % 16
    if rows + spare < 32:
        spare = 32 - rows
    if spare:
        pieces = pieces + [jnp.zeros((devices, spare, columns), jnp.bfloat16)]
    return blocks_of(jnp.concatenate(pieces, 1))


def vector_rows(vectors):
    devices = lax.axis_size("emb") * lax.axis_size("dp")
    return jnp.broadcast_to(vectors.astype(jnp.bfloat16)[None], (devices,) + vectors.shape)


def table_scratch(groups, owners, columns, length, capacity):
    wide = groups * capacity
    return [
        pltpu.VMEM((groups, columns, length), jnp.bfloat16),
        pltpu.VMEM((owners, columns, wide), jnp.bfloat16),
        pltpu.VMEM((owners - 1, columns, wide), jnp.bfloat16),
        pltpu.SemaphoreType.DMA((1,)),
        pltpu.SemaphoreType.DMA((groups - 1,)),
        pltpu.SemaphoreType.DMA((groups - 1,)),
        pltpu.SemaphoreType.DMA((owners - 1,)),
        pltpu.SemaphoreType.DMA((owners - 1,)),
    ]


class Table:
    def __init__(self, grads, slots, ids, out, refs):
        self.grads, self.slots, self.ids, self.out = grads, slots, ids, out
        self.turned, self.packed, self.landed = refs[:3]
        self.local_sem, self.ring_send, self.ring_got, self.send, self.got = refs[3:]
        self.groups, self.columns, self.length = self.turned.shape
        self.owners, _, self.wide = self.packed.shape
        self.capacity = self.wide // self.groups
        self.emb = lax.axis_index("emb")
        self.group = lax.axis_index("dp")

    def bring(self):
        return pltpu.make_async_copy(
            self.grads.at[self.group], self.turned.at[0], self.local_sem.at[0]
        )

    def hop(self, step):
        other = lax.rem(self.group + step, self.groups)
        return pltpu.make_async_remote_copy(
            src_ref=self.grads.at[other],
            dst_ref=self.turned.at[step],
            send_sem=self.ring_send.at[step - 1],
            recv_sem=self.ring_got.at[step - 1],
            device_id={"dp": other},
            device_id_type=MESH,
        )

    def give(self, step):
        other = lax.rem(self.emb + step, self.owners)
        return pltpu.make_async_remote_copy(
            src_ref=self.packed.at[other],
            dst_ref=self.landed.at[step - 1],
            send_sem=self.send.at[step - 1],
            recv_sem=self.got.at[step - 1],
            device_id={"emb": other},
            device_id_type=MESH,
        )

    def start(self):
        self.bring().start()
        for step in range(1, self.groups):
            self.hop(step).start()

    def arrive(self):
        self.bring().wait()
        for step in range(1, self.groups):
            self.hop(step).wait()

    def sort(self, step):
        owner = lax.rem(self.emb + step, self.owners)
        rows = lax.broadcasted_iota(jnp.int32, (128, self.length), 0)
        tiles = []
        for tile in range(self.wide // 128):
            total = jnp.zeros((self.columns, 128), jnp.float32)
            for group in range(self.groups):
                low, high = group * self.capacity, (group + 1) * self.capacity
                if high <= tile * 128 or low >= (tile + 1) * 128:
                    continue
                slot = rows + (tile * 128 - low)
                inside = (slot >= 0) & (slot < self.capacity)
                wanted = jnp.where(inside, slot + owner * self.capacity, -2)
                hot = jnp.where(wanted == self.slots[group], 1.0, 0.0).astype(jnp.bfloat16)
                total = total + product_right(self.turned[group], hot)
            tiles.append(total.astype(jnp.bfloat16))
        self.packed[owner] = jnp.concatenate(tiles, 1)
        return owner

    def add(self, step, first):
        source = lax.rem(self.emb - step + self.owners, self.owners)
        rows, columns = self.out.shape
        count = 6 if rows % 48 == 0 else 1
        block = rows // count
        chunk = self.packed[self.emb] if step == 0 else self.landed[step - 1]

        def one(number, carry):
            base = pl.multiple_of(number * block, 8)
            places = base + lax.broadcasted_iota(jnp.int32, (block, self.wide), 0)
            hot = jnp.where(places == self.ids[source], 1.0, 0.0).astype(jnp.bfloat16)
            part = product_right(hot, chunk)
            if not first:
                part = part + self.out[pl.ds(base, block), :]
            self.out[pl.ds(base, block), :] = part
            return carry

        lax.fori_loop(0, count, one, 0)


class Residual:
    def __init__(self, counts, grads, place, sources, weights, out, refs):
        self.counts, self.grads, self.place, self.out = counts, grads, place, out
        self.pixels, self.first, self.act, self.slope = sources
        self.w_a, self.w_b = weights
        self.mixed, self.inner, self.spots, self.pack = refs

    def rows_back(self):
        length, width = self.grads.shape
        block = min(512, length)

        def one(number, carry):
            base = pl.multiple_of(number * block, block)
            rows = pl.ds(base, block)
            token = base + lax.broadcasted_iota(jnp.int32, (block, width), 0)
            image = jnp.where(token < self.counts[0, 0], self.grads[rows, :], 0.0)
            mixed = image.astype(jnp.bfloat16)
            self.mixed[rows, :] = mixed
            inner = product_right(mixed, self.w_b[...]) * self.slope[rows, :].astype(jnp.float32)
            inner = inner.astype(jnp.bfloat16)
            self.inner[rows, :] = inner
            self.out[rows, :] = (image + product_right(inner, self.w_a[...])).astype(jnp.bfloat16)
            return carry

        lax.fori_loop(0, length // block, one, 0)

    def weights(self):
        length, width = self.grads.shape
        groups, bits = self.pack.shape[0], len(self.pack.shape) - 3
        devices = groups << bits
        share = width // devices
        places = self.spots.shape[0]
        spot = lax.broadcasted_iota(jnp.int32, (places, length), 0)
        hot = jnp.where(spot == self.place[...], 1.0, 0.0).astype(jnp.bfloat16)
        self.spots[...] = product(hot, self.mixed[...])
        spare = self.pack.shape[-2] - 3 * share - places // devices
        part = 384
        for start in range(0, width, part):
            span = slice(start, start + part)
            pieces = [
                product_left(self.pixels[:, span], self.out[...]),
                product_left(self.first[:, span], self.inner[...]),
                product_left(self.act[:, span], self.mixed[...]),
            ]
            for place in range(part // share):
                device = start // share + place
                rows = [piece[place * share : (place + 1) * share] for piece in pieces]
                each = places // devices
                rows.append(self.spots[device * each : (device + 1) * each, :])
                if spare:
                    rows.append(jnp.zeros((spare, width), jnp.float32))
                owner = device % (1 << bits)
                index = tuple((owner >> bit) & 1 for bit in range(bits - 1, -1, -1))
                self.pack[(device >> bits,) + index] = jnp.concatenate(rows, 0).astype(
                    jnp.bfloat16
                )


def tail_kernel(inside, grads_ref, slots_ref, ids_ref, *refs):
    if inside:
        inputs, refs = refs[:10], refs[10:]
        table_out, *outs = refs[:3]
        low_ref, refs = refs[3], refs[4:]
        residual = Residual(
            inputs[1], inputs[2], inputs[3], inputs[4:8], inputs[8:10], low_ref, refs[:4]
        )
        packs = [inputs[0], residual.pack]
        refs = refs[4:]
    else:
        packs, (table_out, *outs), refs = refs[:2], refs[2:5], refs[5:]
    table = Table(grads_ref, slots_ref, ids_ref, table_out, refs[:8])
    first, second = shares_of(packs, outs, refs[8:])
    owners = table.owners
    greet(True)
    table.start()
    first.start()
    if inside:
        residual.rows_back()
        first.take(0)
        residual.weights()
        second.start()
    else:
        second.start()
        first.take(0)
    for stage in range(1, first.bits):
        first.take(stage)
        second.take(stage - 1)
    second.take(second.bits - 1)
    table.arrive()
    for step in range(1, owners):
        table.sort(step)
        table.give(step).start()
    table.sort(0)
    table.add(0, True)
    first.finish()
    second.finish()
    for step in range(1, owners):
        table.give(step).wait()
        table.add(step, False)


def tail(grads, slots, ids, pack, extra, table_rows, capacity, inside):
    groups, columns, length = grads.shape
    owners = ids.shape[0]
    anywhere = pl.BlockSpec(memory_space=pl.ANY)
    vmem = pl.BlockSpec(memory_space=pltpu.VMEM)
    smem = pl.BlockSpec(memory_space=pltpu.SMEM)
    width = pack.shape[-1]
    own = []
    outs = [jax.ShapeDtypeStruct((table_rows, columns), jnp.float32)]
    outs.append(jax.ShapeDtypeStruct(pack.shape[-2:], jnp.float32))
    if inside:
        devices = groups * owners
        rows = 3 * (width // devices) + inside // devices
        rows = max(32, rows + -rows % 16)
        shape = pack.shape[:-2] + (rows, width)
        own = [
            pltpu.VMEM((length, width), jnp.bfloat16),
            pltpu.VMEM((length, width), jnp.bfloat16),
            pltpu.VMEM((inside, width), jnp.float32),
            pltpu.VMEM(shape, jnp.bfloat16),
        ]
        specs = [anywhere, smem] + [vmem] * 8
        outs.append(jax.ShapeDtypeStruct(shape[-2:], jnp.float32))
        outs.append(jax.ShapeDtypeStruct((length, width), jnp.bfloat16))
    else:
        shape = extra[0].shape
        specs = [anywhere, anywhere]
        outs.append(jax.ShapeDtypeStruct(shape[-2:], jnp.float32))
    scratch = own + table_scratch(groups, owners, columns, length, capacity)
    scratch = scratch + shares_scratch(pack.shape) + shares_scratch(shape)
    return pl.pallas_call(
        functools.partial(tail_kernel, inside),
        in_specs=[anywhere, vmem, vmem] + specs,
        out_specs=[vmem] * len(outs),
        out_shape=outs,
        scratch_shapes=scratch,
        compiler_params=pltpu.CompilerParams(
            collective_id=3, has_side_effects=True, vmem_limit_bytes=60 << 20
        ),
        name="tail",
    )(grads, slots, ids, pack, *extra)


def column_of(row, rows):
    diagonal = lax.broadcasted_iota(jnp.int32, (128, 128), 0) == lax.broadcasted_iota(
        jnp.int32, (128, 128), 1
    )
    pieces = [
        jnp.sum(jnp.where(diagonal, row[:, start : start + 128], 0), 1, keepdims=True)
        for start in range(0, rows, 128)
    ]
    return jnp.concatenate(pieces, 0)


def gelu_pair(value):
    root = 0.7978845608028654
    square = value * value
    bend = jnp.tanh(root * (value + 0.044715 * (value * square)))
    half = 0.5 * (1.0 + bend)
    slope = half + 0.5 * value * (1.0 - bend * bend) * (root * (1.0 + 3 * 0.044715 * square))
    return value * half, slope


def front_kernel(
    counts_ref,
    codes_ref,
    place_ref,
    pixels_ref,
    table_ref,
    pos_ref,
    w_patch_ref,
    w_a_ref,
    w_b_ref,
    gain_ref,
    bias_ref,
    embedded_ref,
    normed_ref,
    first_ref,
    act_ref,
    slope_ref,
    ids_ref,
    slots_ref,
    codes_all,
    ranks,
    earlier,
    held,
    packed,
    landed,
    fetched,
    mixed,
    local_sem,
    ask_send,
    ask_got,
    send,
    got,
):
    owners, capacity, width = packed.shape
    length = codes_ref.shape[1]
    table_rows = held.shape[0]
    emb = lax.axis_index("emb")
    bring = pltpu.make_async_copy(table_ref, held, local_sem.at[0])
    bring.start()
    barrier = pltpu.get_barrier_semaphore()
    for step in range(1, owners):
        other = lax.rem(emb + step, owners)
        pl.semaphore_signal(barrier, inc=1, device_id={"emb": other}, device_id_type=MESH)
    pl.semaphore_wait(barrier, owners - 1)

    def ask(step):
        return pltpu.make_async_remote_copy(
            src_ref=codes_ref,
            dst_ref=codes_all.at[step],
            send_sem=ask_send.at[step - 1],
            recv_sem=ask_got.at[step - 1],
            device_id={"emb": lax.rem(emb + step, owners)},
            device_id_type=MESH,
        )

    def give(step):
        return pltpu.make_async_remote_copy(
            src_ref=packed.at[step],
            dst_ref=landed.at[step - 1],
            send_sem=send.at[step - 1],
            recv_sem=got.at[step - 1],
            device_id={"emb": lax.rem(emb - step + owners, owners)},
            device_id_type=MESH,
        )

    for step in range(1, owners):
        ask(step).start()
    codes_all[0] = codes_ref[...]
    block = min(256, length)

    def triangle(number, carry):
        base = pl.multiple_of(number * block, block)
        above = base + lax.broadcasted_iota(jnp.int32, (block, length), 0)
        below = lax.broadcasted_iota(jnp.int32, (block, length), 1)
        earlier[pl.ds(base, block), :] = jnp.where(above < below, 1.0, 0.0).astype(jnp.bfloat16)
        return carry

    lax.fori_loop(0, length // block, triangle, 0)
    codes = codes_ref[...]
    mine = [
        (codes >= owner * table_rows) & (codes < (owner + 1) * table_rows)
        for owner in range(owners)
    ]
    marks = jnp.concatenate([jnp.where(mark, 1.0, 0.0) for mark in mine], 0)
    places = product(marks.astype(jnp.bfloat16), earlier[...])
    slots = jnp.full((1, length), owners * capacity, jnp.int32)
    for owner in range(owners):
        rank = places[owner : owner + 1].astype(jnp.int32)
        slots = jnp.where(mine[owner], owner * capacity + rank, slots)
    slots_ref[...] = slots
    for step in range(1, owners):
        ask(step).wait()
    local = codes_all[...].reshape(owners, length) - emb * table_rows
    inside = (local >= 0) & (local < table_rows)
    places = product(jnp.where(inside, 1.0, 0.0).astype(jnp.bfloat16), earlier[...])
    ranks[...] = jnp.where(inside, places.astype(jnp.int32), -1).reshape(owners, 1, length)
    bring.wait()

    def gather(step):
        rank = ranks[step]
        local = codes_all[step] - emb * table_rows + 1
        slot = lax.broadcasted_iota(jnp.int32, (capacity, length), 0)
        match = slot == rank
        hot = jnp.where(match, 1.0, 0.0).astype(jnp.bfloat16)
        coarse = lax.div(local, 64)
        fine = local - coarse * 64
        inner = rank >= 0
        pair = jnp.concatenate(
            [jnp.where(inner, coarse, 0), jnp.where(inner, fine, 0)]
            + [jnp.zeros((6, length), jnp.int32)],
            0,
        )
        pair = product_right(pair.astype(jnp.float32).astype(jnp.bfloat16), hot)
        source = lax.rem(emb - step + owners, owners)
        ids_ref[source] = (pair[0:1] * 64.0 + pair[1:2]).astype(jnp.int32) - 1
        wanted = jnp.sum(jnp.where(match, local, 0), 1, keepdims=True) - 1
        total = jnp.zeros((capacity, width), jnp.float32)
        for start in range(0, table_rows, 1024):
            size = min(1024, table_rows - start)
            row = start + lax.broadcasted_iota(jnp.int32, (capacity, size), 1)
            hot = jnp.where(row == wanted, 1.0, 0.0).astype(jnp.bfloat16)
            total = total + product(hot, held[start : start + size, :])
        packed[step] = total.astype(jnp.bfloat16)

    def serve(step, carry):
        gather(step)
        give(step).start()
        return carry

    lax.fori_loop(1, owners, serve, 0)
    gather(0)
    slot_column = column_of(slots, length)
    fetched[...] = jnp.zeros_like(fetched)

    def place_rows(step):
        owner = lax.rem(emb + step, owners)
        rows = packed[0] if step == 0 else landed[step - 1]
        for start in range(0, length, block):
            slot = owner * capacity + lax.broadcasted_iota(jnp.int32, (block, capacity), 1)
            hot = jnp.where(slot == slot_column[start : start + block], 1.0, 0.0)
            fetched[start : start + block, :] += product(hot.astype(jnp.bfloat16), rows)


    def patches(number, carry):
        base = pl.multiple_of(number * block, block)
        rows = pl.ds(base, block)
        first = product(pixels_ref[rows, :], w_patch_ref[...])
        low = first.astype(jnp.bfloat16)
        first_ref[rows, :] = low
        act, slope = gelu_pair(product(low, w_a_ref[...]))
        act = act.astype(jnp.bfloat16)
        act_ref[rows, :] = act
        slope_ref[rows, :] = slope.astype(jnp.bfloat16)
        mixed[rows, :] = first + product(act, w_b_ref[...])
        return carry

    lax.fori_loop(0, length // block, patches, 0)

    def positions(number, carry):
        base = pl.multiple_of(number * block, block)
        spot = lax.broadcasted_iota(jnp.int32, (block, pos_ref.shape[0]), 1)
        place = column_of(place_ref[:, pl.ds(base, block)], block)
        hot = jnp.where(spot == place, 1.0, 0.0).astype(jnp.bfloat16)
        embedded_ref[pl.ds(base, block), :] = product(hot, pos_ref[...])
        return carry

    lax.fori_loop(0, length // block, positions, 0)
    place_rows(0)
    for step in range(1, owners):
        give(step).wait()
        place_rows(step)

    def settle(number, carry):
        base = pl.multiple_of(number * block, block)
        rows = pl.ds(base, block)
        token = base + lax.broadcasted_iota(jnp.int32, (block, width), 0)
        image = mixed[rows, :] + embedded_ref[rows, :]
        value = jnp.where(token < counts_ref[0, 0], image, fetched[rows, :])
        embedded_ref[rows, :] = value
        normed = normalize(value) * gain_ref[...] + bias_ref[...]
        normed_ref[rows, :] = normed.astype(jnp.bfloat16)
        return carry

    lax.fori_loop(0, length // block, settle, 0)


def front(counts, codes, place, pixels, table, pos, w_patch, w_a, w_b, gain, bias, capacity):
    owners = lax.axis_size("emb")
    length, width = pixels.shape
    vmem = pl.BlockSpec(memory_space=pltpu.VMEM)
    low = jax.ShapeDtypeStruct((length, width), jnp.bfloat16)
    full = jax.ShapeDtypeStruct((length, width), jnp.float32)
    return pl.pallas_call(
        front_kernel,
        in_specs=[pl.BlockSpec(memory_space=pltpu.SMEM), vmem, vmem, vmem]
        + [pl.BlockSpec(memory_space=pl.ANY)]
        + [vmem] * 6,
        out_specs=[vmem] * 7,
        out_shape=[
            full,
            low,
            low,
            low,
            low,
            jax.ShapeDtypeStruct((owners, 1, capacity), jnp.int32),
            jax.ShapeDtypeStruct((1, length), jnp.int32),
        ],
        scratch_shapes=[
            pltpu.VMEM((owners, 1, length), jnp.int32),
            pltpu.VMEM((owners, 1, length), jnp.int32),
            pltpu.VMEM((length, length), jnp.bfloat16),
            pltpu.VMEM(table.shape, jnp.bfloat16),
            pltpu.VMEM((owners, capacity, width), jnp.bfloat16),
            pltpu.VMEM((owners - 1, capacity, width), jnp.bfloat16),
            pltpu.VMEM((length, width), jnp.float32),
            pltpu.VMEM((length, width), jnp.float32),
            pltpu.SemaphoreType.DMA((1,)),
            pltpu.SemaphoreType.DMA((owners - 1,)),
            pltpu.SemaphoreType.DMA((owners - 1,)),
            pltpu.SemaphoreType.DMA((owners - 1,)),
            pltpu.SemaphoreType.DMA((owners - 1,)),
        ],
        compiler_params=pltpu.CompilerParams(
            collective_id=1, has_side_effects=True, vmem_limit_bytes=56 << 20
        ),
        name="front",
    )(counts, codes, place, pixels, table, pos, w_patch, w_a, w_b, gain, bias)


def feed_kernel(
    attended_ref,
    embedded_ref,
    cotangent_ref,
    w_o_ref,
    gain_ref,
    bias_ref,
    w_up_ref,
    w_down_ref,
    output_ref,
    grad_middle_ref,
    grad_up_ref,
    grad_attended_ref,
    grad_w_o_ref,
    gains_ref,
    part_ref,
    middle,
    normed,
    back,
    slopes,
    hidden,
    pack,
    *refs,
):
    (share,) = shares_of([pack], [None], refs)
    groups, length, chunk = slopes.shape
    bits = share.bits
    owners = 1 << bits
    width = middle.shape[1]
    step = pl.program_id(0)
    block = min(512, length)
    blocks = length // block

    @pl.when(step == 0)
    def begin():
        greet(False, ring=False)

        def one(number, carry):
            rows = pl.ds(pl.multiple_of(number * block, block), block)
            value = embedded_ref[rows, :] + product_left(attended_ref[:, rows], w_o_ref[...])
            middle[rows, :] = value
            normed[rows, :] = (normalize(value) * gain_ref[...] + bias_ref[...]).astype(
                jnp.bfloat16
            )
            return carry

        lax.fori_loop(0, blocks, one, 0)

    @pl.when(step < groups)
    def go_forward():
        def one(number, carry):
            rows = pl.ds(pl.multiple_of(number * block, block), block)
            act, slope = gelu_pair(product(normed[rows, :], w_up_ref[...]))
            act = act.astype(jnp.bfloat16)
            hidden[rows, :] = act
            slopes[step, rows, :] = slope.astype(jnp.bfloat16)
            grown = product(act, w_down_ref[...])

            @pl.when(step == 0)
            def first():
                grad_middle_ref[rows, :] = middle[rows, :] + grown

            @pl.when(step > 0)
            def other():
                grad_middle_ref[rows, :] = grad_middle_ref[rows, :] + grown

            return carry

        lax.fori_loop(0, blocks, one, 0)
        units = chunk // owners
        spare = pack.shape[-2] - units
        part = 384 if chunk % 384 == 0 and 384 % units == 0 else chunk
        for start in range(0, chunk, part):
            grads = product_left(hidden[:, start : start + part], cotangent_ref[...])
            for place in range(part // units):
                piece = grads[place * units : (place + 1) * units]
                if spare:
                    piece = jnp.concatenate([piece, jnp.zeros((spare, width), jnp.float32)], 0)
                owner = start // units + place
                index = tuple((owner >> bit) & 1 for bit in range(bits - 1, -1, -1))
                pack[(step,) + index] = piece.astype(jnp.bfloat16)

    @pl.when(step == groups - 1)
    def turn():
        output_ref[...] = grad_middle_ref[...].astype(jnp.bfloat16)
        share.start()

    @pl.when(step == groups + 1)
    def swap():
        share.take(0)

    @pl.when(step >= groups)
    def go_back():
        def one(number, carry):
            rows = pl.ds(pl.multiple_of(number * block, block), block)
            slope = slopes[step - groups, rows, :].astype(jnp.float32)
            grads = product_right(cotangent_ref[rows, :], w_down_ref[...]) * slope
            grads = grads.astype(jnp.bfloat16)
            hidden[rows, :] = grads
            lower = product_right(grads, w_up_ref[...])

            @pl.when(step == groups)
            def first():
                back[rows, :] = lower

            @pl.when(step > groups)
            def other():
                back[rows, :] = back[rows, :] + lower

            return carry

        lax.fori_loop(0, blocks, one, 0)
        for start in range(0, width, 768):
            span = slice(start, start + 768)
            grad_up_ref[0, span, :] = product_left(normed[:, span], hidden[...]).astype(
                jnp.bfloat16
            )

    @pl.when(step == 2 * groups - 1)
    def end():
        share.take(1)
        gains_ref[...] = jnp.zeros_like(gains_ref)

        def one(number, carry):
            rows = pl.ds(pl.multiple_of(number * block, block), block)
            value = middle[rows, :]
            centred = value - jnp.mean(value, -1, keepdims=True)
            scale = lax.rsqrt(jnp.mean(centred * centred, -1, keepdims=True) + 1e-05)
            unit = centred * scale
            grads = back[rows, :]
            gains_ref[0:1, :] += jnp.sum(grads * unit, 0, keepdims=True)
            gains_ref[1:2, :] += jnp.sum(grads, 0, keepdims=True)
            grads = grads * gain_ref[...]
            along = jnp.mean(grads * unit, -1, keepdims=True)
            grads = scale * (grads - jnp.mean(grads, -1, keepdims=True) - unit * along)
            grads = cotangent_ref[rows, :].astype(jnp.float32) + grads
            grad_middle_ref[rows, :] = grads
            normed[rows, :] = grads.astype(jnp.bfloat16)
            return carry

        lax.fori_loop(0, blocks, one, 0)
        for start in range(0, width, 256):
            span = slice(start, start + 256)
            grad_w_o_ref[span, :] = product(attended_ref[span, :], normed[...]).astype(
                jnp.bfloat16
            )
            grad_attended_ref[span, :] = product_right(w_o_ref[span, :], normed[...]).astype(
                jnp.bfloat16
            )
        for stage in range(2, bits):
            share.take(stage)
        share.export(part_ref)


def feed(attended, embedded, cotangent, w_o, gain, bias, w_up, w_down):
    groups, owners = lax.axis_size("dp"), lax.axis_size("emb")
    length, width = embedded.shape
    chunk = w_up.shape[1] // groups
    units = chunk // owners
    units = max(32, units + -units % 16)
    shape = (groups,) + (2,) * (owners.bit_length() - 1) + (units, width)
    once = pl.Buffered(1)

    def whole(array):
        return pl.BlockSpec(array.shape, lambda s: (0, 0), pipeline_mode=once)

    outs = [
        jax.ShapeDtypeStruct((length, width), jnp.bfloat16),
        jax.ShapeDtypeStruct((length, width), jnp.float32),
        jax.ShapeDtypeStruct((groups, width, chunk), jnp.bfloat16),
        jax.ShapeDtypeStruct((width, length), jnp.bfloat16),
        jax.ShapeDtypeStruct((width, width), jnp.bfloat16),
        jax.ShapeDtypeStruct((8, width), jnp.float32),
        jax.ShapeDtypeStruct((groups, units, width), jnp.bfloat16),
    ]
    out_specs = [whole(out) if len(out.shape) == 2 else None for out in outs]
    out_specs[2] = pl.BlockSpec((1, width, chunk), lambda s: (jnp.maximum(s - groups, 0), 0, 0))
    out_specs[6] = pl.BlockSpec(outs[6].shape, lambda s: (0, 0, 0), pipeline_mode=once)
    return pl.pallas_call(
        feed_kernel,
        grid=(2 * groups,),
        in_specs=[
            whole(attended),
            whole(embedded),
            whole(cotangent),
            whole(w_o),
            whole(gain),
            whole(bias),
            pl.BlockSpec((width, chunk), lambda s: (0, lax.rem(s, groups))),
            pl.BlockSpec((chunk, width), lambda s: (lax.rem(s, groups), 0)),
        ],
        out_specs=out_specs,
        out_shape=outs,
        scratch_shapes=[
            pltpu.VMEM((length, width), jnp.float32),
            pltpu.VMEM((length, width), jnp.bfloat16),
            pltpu.VMEM((length, width), jnp.float32),
            pltpu.VMEM((groups, length, chunk), jnp.bfloat16),
            pltpu.VMEM((length, chunk), jnp.bfloat16),
            pltpu.VMEM(shape, jnp.bfloat16),
        ]
        + shares_scratch(shape),
        compiler_params=pltpu.CompilerParams(
            collective_id=4, has_side_effects=True, vmem_limit_bytes=58 << 20
        ),
        name="feed",
    )(attended, embedded, cotangent, w_o, gain, bias, w_up, w_down)


def first_kernel(
    heads_ref,
    w_q_ref,
    w_k_ref,
    w_v_ref,
    embedded_ref,
    middle_ref,
    normed_ref,
    gain_ref,
    grad_ref,
    turned_ref,
    weights_ref,
    gains_ref,
    back,
    normed_turned,
):
    length, width = embedded_ref.shape
    block = min(512, length)
    gains_ref[...] = jnp.zeros_like(gains_ref)

    def rows_back(number, carry):
        base = pl.multiple_of(number * block, block)
        rows = pl.ds(base, block)
        back[...] = product(w_q_ref[...], heads_ref[0:width, rows])
        back[...] += product(w_k_ref[...], heads_ref[width : 2 * width, rows])
        back[...] += product(w_v_ref[...], heads_ref[2 * width :, rows])
        grads = back[...].T
        value = embedded_ref[rows, :]
        centred = value - jnp.mean(value, -1, keepdims=True)
        scale = lax.rsqrt(jnp.mean(centred * centred, -1, keepdims=True) + 1e-05)
        unit = centred * scale
        gains_ref[0:1, :] += jnp.sum(grads * unit, 0, keepdims=True)
        gains_ref[1:2, :] += jnp.sum(grads, 0, keepdims=True)
        grads = grads * gain_ref[...]
        along = jnp.mean(grads * unit, -1, keepdims=True)
        grads = scale * (grads - jnp.mean(grads, -1, keepdims=True) - unit * along)
        grads = middle_ref[rows, :] + grads
        grad_ref[rows, :] = grads
        turned_ref[:, rows] = grads.T.astype(jnp.bfloat16)
        normed_turned[:, rows] = normed_ref[rows, :].astype(jnp.float32).T.astype(jnp.bfloat16)
        return carry

    lax.fori_loop(0, length // block, rows_back, 0)

    def weights(number, carry):
        base = pl.multiple_of(number * width, width)
        weights_ref[number] = product_right(
            normed_turned[...], heads_ref[pl.ds(base, width), :]
        ).astype(jnp.bfloat16)
        return carry

    lax.fori_loop(0, 3, weights, 0)


def first_backward(heads, w_q, w_k, w_v, embedded, middle, normed, gain):
    length, width = embedded.shape
    vmem = pl.BlockSpec(memory_space=pltpu.VMEM)
    return pl.pallas_call(
        first_kernel,
        in_specs=[vmem] * 8,
        out_specs=[vmem] * 4,
        out_shape=[
            jax.ShapeDtypeStruct((length, width), jnp.float32),
            jax.ShapeDtypeStruct((width, length), jnp.bfloat16),
            jax.ShapeDtypeStruct((3, width, width), jnp.bfloat16),
            jax.ShapeDtypeStruct((8, width), jnp.float32),
        ],
        scratch_shapes=[
            pltpu.VMEM((width, min(512, length)), jnp.float32),
            pltpu.VMEM((width, length), jnp.bfloat16),
        ],
        compiler_params=pltpu.CompilerParams(vmem_limit_bytes=56 << 20),
        name="first_backward",
    )(heads, w_q, w_k, w_v, embedded, middle, normed, gain)


def on_device(
    pixels,
    counts,
    token_ids,
    action_bins,
    patch_pos,
    token_table,
    pos_table,
    w_patch,
    w_res_a,
    w_res_b,
    gain_one,
    bias_one,
    w_q,
    w_k,
    w_v,
    w_o,
    gain_two,
    bias_two,
    w_up,
    w_down,
    cotangent,
):
    length = pixels.shape[0]
    model_width = w_q.shape[0]
    positions = jnp.arange(length)
    image_rows = positions < counts[0, 0]
    action_rows = positions >= length - counts[0, 1]
    table_rows = jnp.logical_not(image_rows)
    row_ids = jnp.where(action_rows, TEXT_VOCAB + action_bins, token_ids)
    rows_owned = token_table.shape[0]
    owners_total = lax.axis_size("emb")
    capacity = 3 * length // (2 * owners_total)
    groups = lax.axis_size("dp")
    codes = jnp.where(table_rows, row_ids, -1).reshape(1, length)
    gain_row = gain_one.astype(jnp.float32).reshape(1, model_width)
    bias_row = bias_one.astype(jnp.float32).reshape(1, model_width)
    embedded, normed_one, first_low, res_act, res_slope, ids, slots = front(
        counts,
        codes,
        patch_pos.reshape(1, length),
        pixels,
        token_table,
        pos_table,
        w_patch,
        w_res_a,
        w_res_b,
        gain_row,
        bias_row,
        capacity,
    )
    facts = jnp.concatenate([ids.reshape(-1), slots.reshape(-1)])
    ring = [facts] + [
        lax.ppermute(facts, "dp", [(i, (i + step) % groups) for i in range(groups)])
        for step in range(1, groups)
    ]
    ring = jnp.stack(ring)
    ring_ids = ring[:, : owners_total * capacity].reshape(groups, owners_total, capacity)
    ring_ids = jnp.swapaxes(ring_ids, 0, 1).reshape(owners_total, 1, groups * capacity)
    ring_slots = ring[:, owners_total * capacity :].reshape(groups, 1, length)
    queries = contract(w_q, normed_one, 0, 1).astype(jnp.bfloat16)
    key_heads = contract(w_k, normed_one, 0, 1).astype(jnp.bfloat16)
    value_heads = contract(w_v, normed_one, 0, 1).astype(jnp.bfloat16)
    attended, probs, inverse = attention_forward(queries, key_heads, value_heads)
    output, grad_middle, grad_w_up, grad_attended, grad_w_o, gains, part_down = feed(
        attended,
        embedded,
        cotangent,
        w_o,
        gain_two.astype(jnp.float32).reshape(1, model_width),
        bias_two.astype(jnp.float32).reshape(1, model_width),
        w_up,
        w_down,
    )
    devices = groups * owners_total
    share = model_width // devices
    folds = w_up.shape[1] // model_width
    per_fold = groups // folds
    folded = []
    for n in range(folds):
        pieces = [grad_w_up[n * per_fold + m] for m in range(per_fold)]
        folded.append(rows_of(jnp.concatenate(pieces, 1) if per_fold > 1 else pieces[0]))
    grad_heads, share_one, share_two, share_down = attention_backward(
        queries,
        key_heads,
        value_heads,
        attended,
        grad_attended,
        probs,
        inverse,
        [
            stacked(folded[:2] + [rows_of(grad_w_o), vector_rows(gains)]),
            stacked(folded[2:]),
        ],
        part_down,
    )
    grad_heads = grad_heads.reshape(3 * model_width, length)
    grad_embedded, grads_turned, grad_w_heads, gains = first_backward(
        grad_heads, w_q, w_k, w_v, embedded, grad_middle, normed_one, gain_row
    )
    gains_one = vector_rows(gains)
    grad_w_heads = [rows_of(grad_w_heads[n]) for n in range(3)]
    columns = model_width // groups
    grads_turned = grads_turned.reshape(groups, columns, length)
    pos_rows = pos_table.shape[0]
    pos_share = pos_rows // devices
    pack_heads = stacked(grad_w_heads + [gains_one])
    if share % 8 == 0 and 384 % share == 0 and pos_share % 8 == 0:
        grad_table, share_heads, share_res, grad_first = tail(
            grads_turned,
            ring_slots,
            ring_ids,
            pack_heads,
            [
                counts,
                grad_embedded,
                patch_pos.reshape(1, length),
                pixels,
                first_low,
                res_act,
                res_slope,
                w_res_a,
                w_res_b,
            ],
            rows_owned,
            capacity,
            pos_rows,
        )
    else:
        grad_image = jnp.where(image_rows[:, None], grad_embedded, 0.0)
        grad_mixed = grad_image.astype(jnp.bfloat16)
        position_hot = patch_pos[:, None] == jnp.arange(pos_rows)[None, :]
        grad_pos_table = product_left(position_hot.astype(jnp.bfloat16), grad_mixed)
        grad_w_res_b = product_left(res_act, grad_mixed)
        grad_inner = product_right(grad_mixed, w_res_b) * res_slope.astype(jnp.float32)
        grad_inner = grad_inner.astype(jnp.bfloat16)
        grad_w_res_a = product_left(first_low, grad_inner)
        grad_first = (grad_image + product_right(grad_inner, w_res_a)).astype(jnp.bfloat16)
        grad_w_patch = product_left(pixels, grad_first)
        res_rows = [rows_of(g) for g in (grad_w_patch, grad_w_res_a, grad_w_res_b, grad_pos_table)]
        grad_table, share_heads, share_res = tail(
            grads_turned,
            ring_slots,
            ring_ids,
            pack_heads,
            [stacked(res_rows)],
            rows_owned,
            capacity,
            0,
        )
    grad_pixels = product_right(grad_first, w_patch)

    def cut(array, place):
        return array[place * share : (place + 1) * share]

    rows_up = jnp.concatenate([share_one[: 2 * share], share_two[: (folds - 2) * share]], 0)
    share_w_up = jnp.swapaxes(rows_up.reshape(folds, share, model_width), 0, 1)
    place = (lax.axis_index("dp") * owners_total + lax.axis_index("emb")) * share
    gains_two = lax.dynamic_slice(share_one[3 * share : 3 * share + 2], (0, place), (2, share))
    gains_one = lax.dynamic_slice(share_heads[3 * share : 3 * share + 2], (0, place), (2, share))
    return (
        output,
        grad_pixels,
        grad_table,
        share_res[3 * share : 3 * share + pos_share],
        cut(share_res, 0),
        cut(share_res, 1),
        cut(share_res, 2),
        gains_one[0],
        gains_one[1],
        cut(share_heads, 0),
        cut(share_heads, 1),
        cut(share_heads, 2),
        cut(share_one, 2),
        gains_two[0],
        gains_two[1],
        share_w_up.reshape(share, folds * model_width),
        share_down[: w_down.shape[0] // devices],
    )


def solution(mesh):
    in_specs = (
        P(("dp", "emb"), None),
        P(("dp", "emb"), None),
        P(("dp", "emb")),
        P(("dp", "emb")),
        P(("dp", "emb")),
        P("emb", None),
        P(),
        P(),
        P(),
        P(),
        P(),
        P(),
        P(),
        P(),
        P(),
        P(),
        P(),
        P(),
        P(),
        P(),
        P(("dp", "emb"), None),
    )
    out_specs = (
        P(("dp", "emb"), None),
        P(("dp", "emb"), None),
        P("emb", "dp"),
        P(("dp", "emb"), None),
        P(("dp", "emb"), None),
        P(("dp", "emb"), None),
        P(("dp", "emb"), None),
        P(("dp", "emb")),
        P(("dp", "emb")),
        P(("dp", "emb"), None),
        P(("dp", "emb"), None),
        P(("dp", "emb"), None),
        P(("dp", "emb"), None),
        P(("dp", "emb")),
        P(("dp", "emb")),
        P(("dp", "emb"), None),
        P(("dp", "emb"), None),
    )
    return jax.shard_map(
        on_device, mesh=mesh, in_specs=in_specs, out_specs=out_specs, check_vma=False
    )
```

```python
import functools

import jax
import jax.numpy as jnp
from jax import lax
from jax.experimental import pallas as pl
from jax.experimental.pallas import tpu as pltpu
from jax.sharding import PartitionSpec as P

HEAD_DIM = 32
TEXT_VOCAB = 32000
BLOCK = 256
HEADS_STEP = 2
MESH = pl.DeviceIdType.MESH
LOG2_E = 1.4426950408889634


def normalize(values):
    average = jnp.mean(values, -1, keepdims=True)
    centred = values - average
    variance = jnp.mean(centred * centred, -1, keepdims=True)
    return centred * lax.rsqrt(variance + 1e-05)


def norm_affine(values, gain, offset):
    return normalize(values) * gain + offset


def contract(left, right, left_dim, right_dim):
    return lax.dot_general(
        left, right, (((left_dim,), (right_dim,)), ((), ())), preferred_element_type=jnp.float32
    )


def product(left, right):
    return contract(left, right, 1, 0)


def product_left(left, right):
    return contract(left, right, 0, 0)


def product_right(left, right):
    return contract(left, right, 1, 1)


def forward_kernel(heads, q_ref, k_ref, v_ref, o_ref, p_ref, r_ref):
    length = q_ref.shape[1]
    scaling = HEAD_DIM ** (-0.5) * LOG2_E
    key_place = lax.broadcasted_iota(jnp.int32, (BLOCK, BLOCK), 0)
    query_place = lax.broadcasted_iota(jnp.int32, (BLOCK, BLOCK), 1)
    allowed = key_place <= query_place
    for head in range(heads):
        rows = slice(head * HEAD_DIM, (head + 1) * HEAD_DIM)
        keys = k_ref[rows, :]
        values = v_ref[rows, :]
        for step in range(length // BLOCK):
            start, end = step * BLOCK, (step + 1) * BLOCK
            scores = contract(keys[:, :end], q_ref[rows, start:end], 0, 0) * scaling
            corner = jnp.where(allowed, scores[start:], -1e30)
            highest = jnp.max(corner, 0, keepdims=True)
            if step:
                highest = jnp.maximum(highest, jnp.max(scores[:start], 0, keepdims=True))
            weights = jnp.exp2(corner - highest)
            total = jnp.sum(weights, 0, keepdims=True)
            weights = weights.astype(jnp.bfloat16)
            if step:
                above = jnp.exp2(scores[:start] - highest)
                total = total + jnp.sum(above, 0, keepdims=True)
                weights = jnp.concatenate([above.astype(jnp.bfloat16), weights], 0)
            inverse = 1.0 / total
            base = BLOCK * (step * (step + 1) // 2)
            p_ref[head, base : base + end, :] = weights
            r_ref[head, :, start:end] = inverse
            o_ref[rows, start:end] = (
                contract(values[:, :end], weights, 1, 0) * inverse
            ).astype(jnp.bfloat16)


def packed_rows(length):
    steps = length // BLOCK
    return BLOCK * (steps * (steps + 1) // 2)


def attention_forward(queries, key_heads, values):
    width, length = queries.shape
    heads = width // HEAD_DIM
    packed = packed_rows(length)
    rows = pl.BlockSpec((HEADS_STEP * HEAD_DIM, length), lambda g: (g, 0))
    return pl.pallas_call(
        functools.partial(forward_kernel, HEADS_STEP),
        grid=(heads // HEADS_STEP,),
        in_specs=[rows] * 3,
        out_specs=[
            rows,
            pl.BlockSpec((HEADS_STEP, packed, BLOCK), lambda g: (g, 0, 0)),
            pl.BlockSpec((HEADS_STEP, 1, length), lambda g: (g, 0, 0)),
        ],
        out_shape=[
            jax.ShapeDtypeStruct((width, length), jnp.bfloat16),
            jax.ShapeDtypeStruct((heads, packed, BLOCK), jnp.bfloat16),
            jax.ShapeDtypeStruct((heads, 1, length), jnp.float32),
        ],
        compiler_params=pltpu.CompilerParams(vmem_limit_bytes=32 << 20),
        cost_estimate=pl.CostEstimate(
            flops=50_000_000_000, bytes_accessed=heads * packed * BLOCK * 2, transcendentals=0
        ),
        name="attention_forward",
    )(queries, key_heads, values)


def backward_kernel(
    heads,
    q_ref,
    k_ref,
    v_ref,
    o_ref,
    g_ref,
    p_ref,
    r_ref,
    pack_one,
    pack_two,
    part_ref,
    facts_ref,
    d_ref,
    out_one,
    out_two,
    ring_ref,
    facts_out,
    s_ref,
    *refs,
):
    ring = Ring(part_ref, ring_ref, refs[:3])
    facts_landed, facts_send, facts_got = refs[3:6]
    first, second = shares_of([pack_one, pack_two], [out_one, out_two], refs[6:])
    groups = ring.groups

    def tell(step):
        return pltpu.make_async_remote_copy(
            src_ref=facts_ref,
            dst_ref=facts_landed.at[step - 1],
            send_sem=facts_send.at[step - 1],
            recv_sem=facts_got.at[step - 1],
            device_id={"dp": lax.rem(ring.group + step, groups)},
            device_id_type=MESH,
        )

    bits = first.bits
    number = pl.program_id(0)
    last = pl.num_programs(0) - 1

    @pl.when(number == 0)
    def begin():
        greet(False)
        first.start()
        second.start()
        ring.start()
        for step in range(1, groups):
            tell(step).start()

    @pl.when(number == 1)
    def first_swap():
        first.take(0)

    @pl.when(number == 4)
    def next_swap():
        first.take(1)
        second.take(0)

    @pl.when(number == 7)
    def other_swaps():
        for stage in range(2, bits):
            first.take(stage)

    @pl.when(number == 8)
    def late_swap():
        second.take(1)

    @pl.when(number == 10)
    def last_swaps():
        for stage in range(2, bits):
            second.take(stage)

    length = q_ref.shape[1]
    steps = length // BLOCK
    scaling = HEAD_DIM ** (-0.5)
    for head in range(heads):
        rows = slice(head * HEAD_DIM, (head + 1) * HEAD_DIM)
        grads = (g_ref[rows, :].astype(jnp.float32) * r_ref[head]).astype(jnp.bfloat16)
        inner = jnp.sum(
            grads.astype(jnp.float32) * o_ref[rows, :].astype(jnp.float32), 0, keepdims=True
        )
        queries = q_ref[rows, :]
        keys = k_ref[rows, :]
        values = v_ref[rows, :]
        for step in range(steps):
            start, end = step * BLOCK, (step + 1) * BLOCK
            base = BLOCK * (step * (step + 1) // 2)
            grad_probs = contract(values[:, :end], grads[:, start:end], 0, 0)
            grad_scores = p_ref[head, base : base + end, :] * (
                grad_probs - inner[:, start:end]
            ).astype(jnp.bfloat16)
            s_ref[head, base : base + end, :] = grad_scores
            d_ref[0, rows, start:end] = (
                contract(keys[:, :end], grad_scores, 1, 0) * scaling
            ).astype(jnp.bfloat16)
        for column in range(steps):
            grad_keys = jnp.zeros((HEAD_DIM, BLOCK), jnp.float32)
            grad_values = jnp.zeros((HEAD_DIM, BLOCK), jnp.float32)
            for step in range(column, steps):
                base = BLOCK * (step * (step + 1) // 2 + column)
                span = slice(step * BLOCK, (step + 1) * BLOCK)
                grad_values = grad_values + contract(
                    grads[:, span], p_ref[head, base : base + BLOCK, :], 1, 1
                )
                grad_keys = grad_keys + contract(
                    queries[:, span], s_ref[head, base : base + BLOCK, :], 1, 1
                )
            span = slice(column * BLOCK, (column + 1) * BLOCK)
            d_ref[1, rows, span] = (grad_keys * scaling).astype(jnp.bfloat16)
            d_ref[2, rows, span] = grad_values.astype(jnp.bfloat16)

    @pl.when(number == last)
    def end():
        facts_out[0] = facts_ref[...]
        for step in range(1, groups):
            tell(step).wait()
            facts_out[step] = facts_landed[step - 1]
        ring.finish()
        first.finish()
        second.finish()


def attention_backward(
    queries, key_heads, values, attended, grads, probs, inverse, packs, part, facts
):
    width, length = queries.shape
    heads = width // HEAD_DIM
    packed = packed_rows(length)
    rows = pl.BlockSpec((HEADS_STEP * HEAD_DIM, length), lambda g: (g, 0))
    scratch = [pltpu.VMEM((HEADS_STEP, packed, BLOCK), jnp.bfloat16)]
    scratch = scratch + ring_scratch(part.shape)
    groups = part.shape[0]
    semaphores = pltpu.SemaphoreType.DMA((groups - 1,))
    scratch = scratch + [pltpu.VMEM((groups - 1,) + facts.shape, jnp.int32), semaphores, semaphores]
    for pack in packs:
        scratch = scratch + shares_scratch(pack.shape)
    return pl.pallas_call(
        functools.partial(backward_kernel, HEADS_STEP),
        grid=(heads // HEADS_STEP,),
        in_specs=[rows] * 5
        + [
            pl.BlockSpec((HEADS_STEP, packed, BLOCK), lambda g: (g, 0, 0)),
            pl.BlockSpec((HEADS_STEP, 1, length), lambda g: (g, 0, 0)),
            pl.BlockSpec(memory_space=pl.ANY),
            pl.BlockSpec(memory_space=pl.ANY),
            pl.BlockSpec(part.shape, lambda g: (0, 0, 0)),
            pl.BlockSpec(facts.shape, lambda g: (0, 0)),
        ],
        out_specs=[
            pl.BlockSpec((3, HEADS_STEP * HEAD_DIM, length), lambda g: (0, g, 0)),
            pl.BlockSpec(packs[0].shape[-2:], lambda g: (0, 0)),
            pl.BlockSpec(packs[1].shape[-2:], lambda g: (0, 0)),
            pl.BlockSpec(part.shape[-2:], lambda g: (0, 0)),
            pl.BlockSpec((groups,) + facts.shape, lambda g: (0, 0, 0)),
        ],
        out_shape=[
            jax.ShapeDtypeStruct((3, width, length), jnp.bfloat16),
            jax.ShapeDtypeStruct(packs[0].shape[-2:], jnp.float32),
            jax.ShapeDtypeStruct(packs[1].shape[-2:], jnp.float32),
            jax.ShapeDtypeStruct(part.shape[-2:], jnp.float32),
            jax.ShapeDtypeStruct((groups,) + facts.shape, jnp.int32),
        ],
        scratch_shapes=scratch,
        compiler_params=pltpu.CompilerParams(
            collective_id=2, has_side_effects=True, vmem_limit_bytes=56 << 20
        ),
        name="attention_backward",
    )(queries, key_heads, values, attended, grads, probs, inverse, *packs, part, facts)


def bit_of(index, bit):
    return lax.rem(lax.div(index, 1 << bit), 2)


def flipped(index, bit):
    return index + (1 - 2 * bit_of(index, bit)) * (1 << bit)


def spans_of(rows):
    first = (rows + 31) // 32 * 16
    return ((0, first), (first, rows - first))


class Shares:
    def __init__(self, pack, out, refs):
        self.pack, self.out = pack, out
        self.groups = pack.shape[0]
        self.bits = len(pack.shape) - 3
        self.spans = spans_of(pack.shape[-2])
        refs = list(refs)
        self.own, self.zero = refs[:2]
        count = self.bits - 1
        self.later = [refs[2 + half * count : 2 + (half + 1) * count] for half in range(2)]
        refs = refs[2 + 2 * count :]
        self.ring = refs[:2]
        self.local_sem, self.swap_send, self.swap_got, self.ring_send, self.ring_got = refs[2:]
        self.emb = lax.axis_index("emb")
        self.group = lax.axis_index("dp")
        self.every = (slice(None),) * self.bits

    def order(self, half):
        rest = list(range(1, self.bits))
        return [0] + (rest if half == 0 else rest[::-1])

    def span(self, half):
        return pl.ds(*self.spans[half])

    def place(self, half, stage, mine):
        order = self.order(half)
        index = []
        for bit in range(self.bits - 1, 0, -1):
            value = bit_of(self.emb, bit)
            if order.index(bit) < stage:
                index.append(value)
            elif order.index(bit) == stage:
                index.append(value if mine else 1 - value)
            else:
                index.append(slice(None))
        return tuple(index)

    def swap(self, half, stage):
        if stage == 0:
            other = 1 - bit_of(self.emb, 0)
            source = self.pack.at[self.every + (other, self.span(half))]
            target = self.zero.at[self.every + (self.span(half),)]
        else:
            place = self.place(half, stage, False)
            source = self.own.at[(slice(None),) + place + (self.span(half),)]
            target = self.later[half][stage - 1]
        return pltpu.make_async_remote_copy(
            src_ref=source,
            dst_ref=target,
            send_sem=self.swap_send.at[half, stage],
            recv_sem=self.swap_got.at[half, stage],
            device_id={"emb": flipped(self.emb, self.order(half)[stage])},
            device_id_type=MESH,
        )

    def bring(self, half):
        mine = bit_of(self.emb, 0)
        return pltpu.make_async_copy(
            self.pack.at[self.every + (mine, self.span(half))],
            self.own.at[self.every + (self.span(half),)],
            self.local_sem.at[half],
        )

    def hop(self, half, step):
        other = lax.rem(self.group + step, self.groups)
        place = (other,) + self.place(half, self.bits, True) + (self.span(half),)
        return pltpu.make_async_remote_copy(
            src_ref=self.own.at[place],
            dst_ref=self.ring[half].at[step - 1],
            send_sem=self.ring_send.at[half, step - 1],
            recv_sem=self.ring_got.at[half, step - 1],
            device_id={"dp": other},
            device_id_type=MESH,
        )

    def start(self):
        for half in range(2):
            self.swap(half, 0).start()
            self.bring(half).start()

    def take(self, stage):
        for half in range(2):
            self.take_half(half, stage)

    def take_half(self, half, stage):
        if stage == 0:
            self.bring(half).wait()
        self.swap(half, stage).wait()
        place = self.place(half, stage, True)
        free = [n for n, index in enumerate(place) if isinstance(index, slice)]

        def one(number, carry):
            group = lax.rem(number, self.groups)
            rest = lax.div(number, self.groups)
            index = list(place)
            there = []
            for n in free:
                index[n] = lax.rem(rest, 2)
                there.append(index[n])
                rest = lax.div(rest, 2)
            target = (group,) + tuple(index) + (self.span(half), slice(None))
            if stage == 0:
                arrived = self.zero[target]
            else:
                arrived = self.later[half][stage - 1][(group,) + tuple(there)]
            total = self.own[target].astype(jnp.float32) + arrived.astype(jnp.float32)
            self.own[target] = total.astype(jnp.bfloat16)
            return carry

        lax.fori_loop(0, self.groups * 2 ** len(free), one, 0)
        if stage + 1 < self.bits:
            self.swap(half, stage + 1).start()
        elif self.out is not None:
            for step in range(1, self.groups):
                self.hop(half, step).start()

    def export(self, target):
        for half in range(2):
            place = (slice(None),) + self.place(half, self.bits, True)
            target[:, self.span(half), :] = self.own[place + (self.span(half), slice(None))]

    def finish(self):
        for half in range(2):
            place = (self.group,) + self.place(half, self.bits, True)
            total = self.own[place + (self.span(half), slice(None))].astype(jnp.float32)
            for step in range(1, self.groups):
                self.hop(half, step).wait()
                total = total + self.ring[half][step - 1].astype(jnp.float32)
            self.out[self.span(half), :] = total


class Ring:
    def __init__(self, own, out, refs):
        self.own, self.out = own, out
        self.landed, self.send, self.got = refs
        self.groups = own.shape[0]
        self.group = lax.axis_index("dp")

    def hop(self, step):
        other = lax.rem(self.group + step, self.groups)
        return pltpu.make_async_remote_copy(
            src_ref=self.own.at[other],
            dst_ref=self.landed.at[step - 1],
            send_sem=self.send.at[step - 1],
            recv_sem=self.got.at[step - 1],
            device_id={"dp": other},
            device_id_type=MESH,
        )

    def start(self):
        for step in range(1, self.groups):
            self.hop(step).start()

    def finish(self):
        total = self.own[self.group].astype(jnp.float32)
        for step in range(1, self.groups):
            self.hop(step).wait()
            total = total + self.landed[step - 1].astype(jnp.float32)
        self.out[...] = total


def ring_scratch(shape):
    groups = shape[0]
    semaphores = pltpu.SemaphoreType.DMA((groups - 1,))
    return [pltpu.VMEM((groups - 1,) + shape[1:], jnp.bfloat16), semaphores, semaphores]


def shares_scratch(shape):
    groups, bits, columns = shape[0], len(shape) - 3, shape[-1]
    whole = pltpu.VMEM((groups,) + (2,) * (bits - 1) + shape[-2:], jnp.bfloat16)
    later = [
        pltpu.VMEM((groups,) + (2,) * (bits - 1 - stage) + (span[1], columns), jnp.bfloat16)
        for span in spans_of(shape[-2])
        for stage in range(1, bits)
    ]
    ring = [
        pltpu.VMEM((groups - 1, span[1], columns), jnp.bfloat16) for span in spans_of(shape[-2])
    ]
    semaphores = [(2,), (2, bits), (2, bits), (2, groups - 1), (2, groups - 1)]
    return [whole, whole, *later, *ring] + [pltpu.SemaphoreType.DMA(size) for size in semaphores]


def shares_of(packs, outs, refs):
    bits = len(packs[0].shape) - 3
    each = 2 + 2 * (bits - 1) + 2 + 5
    return [
        Shares(pack, out, refs[n * each : (n + 1) * each])
        for n, (pack, out) in enumerate(zip(packs, outs))
    ]


def greet(everyone, ring=True):
    emb, group = lax.axis_index("emb"), lax.axis_index("dp")
    owners, groups = lax.axis_size("emb"), lax.axis_size("dp")
    barrier = pltpu.get_barrier_semaphore()
    if everyone:
        others = [lax.rem(emb + step, owners) for step in range(1, owners)]
    else:
        others = [flipped(emb, bit) for bit in range(owners.bit_length() - 1)]
    for other in others:
        pl.semaphore_signal(barrier, inc=1, device_id={"emb": other}, device_id_type=MESH)
    for step in range(1, groups if ring else 1):
        other = lax.rem(group + step, groups)
        pl.semaphore_signal(barrier, inc=1, device_id={"dp": other}, device_id_type=MESH)
    pl.semaphore_wait(barrier, len(others) + (groups - 1 if ring else 0))


def blocks_of(array):
    owners, groups = lax.axis_size("emb"), lax.axis_size("dp")
    bits = owners.bit_length() - 1
    return array.reshape((groups,) + (2,) * bits + array.shape[1:])


def rows_of(array):
    devices = lax.axis_size("emb") * lax.axis_size("dp")
    return array.astype(jnp.bfloat16).reshape(devices, array.shape[0] // devices, array.shape[1])


def stacked(pieces):
    rows = sum(piece.shape[1] for piece in pieces)
    devices, _, columns = pieces[0].shape
    spare = -rows % 16
    if rows + spare < 32:
        spare = 32 - rows
    if spare:
        pieces = pieces + [jnp.zeros((devices, spare, columns), jnp.bfloat16)]
    return blocks_of(jnp.concatenate(pieces, 1))


def vector_rows(vectors):
    devices = lax.axis_size("emb") * lax.axis_size("dp")
    return jnp.broadcast_to(vectors.astype(jnp.bfloat16)[None], (devices,) + vectors.shape)


def table_scratch(groups, owners, columns, length, capacity):
    wide = groups * capacity
    return [
        pltpu.VMEM((groups, columns, length), jnp.bfloat16),
        pltpu.VMEM((owners, columns, wide), jnp.bfloat16),
        pltpu.VMEM((owners - 1, columns, wide), jnp.bfloat16),
        pltpu.SemaphoreType.DMA((1,)),
        pltpu.SemaphoreType.DMA((groups - 1,)),
        pltpu.SemaphoreType.DMA((groups - 1,)),
        pltpu.SemaphoreType.DMA((owners - 1,)),
        pltpu.SemaphoreType.DMA((owners - 1,)),
    ]


class Table:
    def __init__(self, grads, slots, ids, out, refs):
        self.grads, self.slots, self.ids, self.out = grads, slots, ids, out
        self.turned, self.packed, self.landed = refs[:3]
        self.local_sem, self.ring_send, self.ring_got, self.send, self.got = refs[3:]
        self.groups, self.columns, self.length = self.turned.shape
        self.owners, _, self.wide = self.packed.shape
        self.capacity = self.wide // self.groups
        self.emb = lax.axis_index("emb")
        self.group = lax.axis_index("dp")

    def bring(self):
        return pltpu.make_async_copy(
            self.grads.at[self.group], self.turned.at[0], self.local_sem.at[0]
        )

    def hop(self, step):
        other = lax.rem(self.group + step, self.groups)
        return pltpu.make_async_remote_copy(
            src_ref=self.grads.at[other],
            dst_ref=self.turned.at[step],
            send_sem=self.ring_send.at[step - 1],
            recv_sem=self.ring_got.at[step - 1],
            device_id={"dp": other},
            device_id_type=MESH,
        )

    def give(self, step):
        other = lax.rem(self.emb + step, self.owners)
        return pltpu.make_async_remote_copy(
            src_ref=self.packed.at[other],
            dst_ref=self.landed.at[step - 1],
            send_sem=self.send.at[step - 1],
            recv_sem=self.got.at[step - 1],
            device_id={"emb": other},
            device_id_type=MESH,
        )

    def start(self):
        self.bring().start()
        for step in range(1, self.groups):
            self.hop(step).start()

    def arrive(self):
        self.bring().wait()
        for step in range(1, self.groups):
            self.hop(step).wait()

    def sort(self, step):
        owner = lax.rem(self.emb + step, self.owners)
        rows = lax.broadcasted_iota(jnp.int32, (128, self.length), 0)
        tiles = []
        for tile in range(self.wide // 128):
            total = jnp.zeros((self.columns, 128), jnp.float32)
            for group in range(self.groups):
                low, high = group * self.capacity, (group + 1) * self.capacity
                if high <= tile * 128 or low >= (tile + 1) * 128:
                    continue
                slot = rows + (tile * 128 - low)
                inside = (slot >= 0) & (slot < self.capacity)
                wanted = jnp.where(inside, slot + owner * self.capacity, -2)
                hot = jnp.where(wanted == self.slots[group], 1.0, 0.0).astype(jnp.bfloat16)
                total = total + product_right(self.turned[group], hot)
            tiles.append(total.astype(jnp.bfloat16))
        self.packed[owner] = jnp.concatenate(tiles, 1)
        return owner

    def add(self, step, first):
        source = lax.rem(self.emb - step + self.owners, self.owners)
        rows, columns = self.out.shape
        count = 6 if rows % 48 == 0 else 1
        block = rows // count
        chunk = self.packed[self.emb] if step == 0 else self.landed[step - 1]

        def one(number, carry):
            base = pl.multiple_of(number * block, 8)
            places = base + lax.broadcasted_iota(jnp.int32, (block, self.wide), 0)
            hot = jnp.where(places == self.ids[source], 1.0, 0.0).astype(jnp.bfloat16)
            part = product_right(hot, chunk)
            if not first:
                part = part + self.out[pl.ds(base, block), :]
            self.out[pl.ds(base, block), :] = part
            return carry

        lax.fori_loop(0, count, one, 0)


class Residual:
    def __init__(self, counts, grads, place, sources, weights, out, refs):
        self.counts, self.grads, self.place, self.out = counts, grads, place, out
        self.pixels, self.first, self.act, self.slope = sources
        self.w_a, self.w_b = weights
        self.mixed, self.inner, self.spots, self.pack = refs

    def rows_back(self):
        length, width = self.grads.shape
        block = min(512, length)

        def one(number, carry):
            base = pl.multiple_of(number * block, block)
            rows = pl.ds(base, block)
            token = base + lax.broadcasted_iota(jnp.int32, (block, width), 0)
            image = jnp.where(token < self.counts[0, 0], self.grads[rows, :], 0.0)
            mixed = image.astype(jnp.bfloat16)
            self.mixed[rows, :] = mixed
            inner = product_right(mixed, self.w_b[...]) * self.slope[rows, :].astype(jnp.float32)
            inner = inner.astype(jnp.bfloat16)
            self.inner[rows, :] = inner
            self.out[rows, :] = (image + product_right(inner, self.w_a[...])).astype(jnp.bfloat16)
            return carry

        lax.fori_loop(0, length // block, one, 0)

    def weights(self):
        length, width = self.grads.shape
        groups, bits = self.pack.shape[0], len(self.pack.shape) - 3
        devices = groups << bits
        share = width // devices
        places = self.spots.shape[0]
        spot = lax.broadcasted_iota(jnp.int32, (places, length), 0)
        hot = jnp.where(spot == self.place[...], 1.0, 0.0).astype(jnp.bfloat16)
        self.spots[...] = product(hot, self.mixed[...])
        spare = self.pack.shape[-2] - 3 * share - places // devices
        part = 384
        for start in range(0, width, part):
            span = slice(start, start + part)
            pieces = [
                product_left(self.pixels[:, span], self.out[...]),
                product_left(self.first[:, span], self.inner[...]),
                product_left(self.act[:, span], self.mixed[...]),
            ]
            for place in range(part // share):
                device = start // share + place
                rows = [piece[place * share : (place + 1) * share] for piece in pieces]
                each = places // devices
                rows.append(self.spots[device * each : (device + 1) * each, :])
                if spare:
                    rows.append(jnp.zeros((spare, width), jnp.float32))
                owner = device % (1 << bits)
                index = tuple((owner >> bit) & 1 for bit in range(bits - 1, -1, -1))
                self.pack[(device >> bits,) + index] = jnp.concatenate(rows, 0).astype(
                    jnp.bfloat16
                )


def tail_kernel(inside, grads_ref, slots_ref, ids_ref, *refs):
    if inside:
        inputs, refs = refs[:10], refs[10:]
        table_out, *outs = refs[:3]
        low_ref, refs = refs[3], refs[4:]
        residual = Residual(
            inputs[1], inputs[2], inputs[3], inputs[4:8], inputs[8:10], low_ref, refs[:4]
        )
        packs = [inputs[0], residual.pack]
        refs = refs[4:]
    else:
        packs, (table_out, *outs), refs = refs[:2], refs[2:5], refs[5:]
    table = Table(grads_ref, slots_ref, ids_ref, table_out, refs[:8])
    first, second = shares_of(packs, outs, refs[8:])
    owners = table.owners
    greet(True)
    table.start()
    first.start()
    if inside:
        residual.rows_back()
        first.take(0)
        residual.weights()
        second.start()
    else:
        second.start()
        first.take(0)
    for stage in range(1, first.bits):
        first.take(stage)
        second.take(stage - 1)
    second.take(second.bits - 1)
    table.arrive()
    for step in range(1, owners):
        table.sort(step)
        table.give(step).start()
    table.sort(0)
    table.add(0, True)
    first.finish()
    second.finish()
    for step in range(1, owners):
        table.give(step).wait()
        table.add(step, False)


def tail(grads, slots, ids, pack, extra, table_rows, capacity, inside):
    groups, columns, length = grads.shape
    owners = ids.shape[0]
    anywhere = pl.BlockSpec(memory_space=pl.ANY)
    vmem = pl.BlockSpec(memory_space=pltpu.VMEM)
    smem = pl.BlockSpec(memory_space=pltpu.SMEM)
    width = pack.shape[-1]
    own = []
    outs = [jax.ShapeDtypeStruct((table_rows, columns), jnp.float32)]
    outs.append(jax.ShapeDtypeStruct(pack.shape[-2:], jnp.float32))
    if inside:
        devices = groups * owners
        rows = 3 * (width // devices) + inside // devices
        rows = max(32, rows + -rows % 16)
        shape = pack.shape[:-2] + (rows, width)
        own = [
            pltpu.VMEM((length, width), jnp.bfloat16),
            pltpu.VMEM((length, width), jnp.bfloat16),
            pltpu.VMEM((inside, width), jnp.float32),
            pltpu.VMEM(shape, jnp.bfloat16),
        ]
        specs = [anywhere, smem] + [vmem] * 8
        outs.append(jax.ShapeDtypeStruct(shape[-2:], jnp.float32))
        outs.append(jax.ShapeDtypeStruct((length, width), jnp.bfloat16))
    else:
        shape = extra[0].shape
        specs = [anywhere, anywhere]
        outs.append(jax.ShapeDtypeStruct(shape[-2:], jnp.float32))
    scratch = own + table_scratch(groups, owners, columns, length, capacity)
    scratch = scratch + shares_scratch(pack.shape) + shares_scratch(shape)
    return pl.pallas_call(
        functools.partial(tail_kernel, inside),
        in_specs=[anywhere, vmem, vmem] + specs,
        out_specs=[vmem] * len(outs),
        out_shape=outs,
        scratch_shapes=scratch,
        compiler_params=pltpu.CompilerParams(
            collective_id=3, has_side_effects=True, vmem_limit_bytes=60 << 20
        ),
        name="tail",
    )(grads, slots, ids, pack, *extra)


def column_of(row, rows):
    diagonal = lax.broadcasted_iota(jnp.int32, (128, 128), 0) == lax.broadcasted_iota(
        jnp.int32, (128, 128), 1
    )
    pieces = [
        jnp.sum(jnp.where(diagonal, row[:, start : start + 128], 0), 1, keepdims=True)
        for start in range(0, rows, 128)
    ]
    return jnp.concatenate(pieces, 0)


def gelu_pair(value):
    root = 0.7978845608028654
    square = value * value
    bend = jnp.tanh(root * (value + 0.044715 * (value * square)))
    half = 0.5 * (1.0 + bend)
    slope = half + 0.5 * value * (1.0 - bend * bend) * (root * (1.0 + 3 * 0.044715 * square))
    return value * half, slope


def front_kernel(
    counts_ref,
    codes_ref,
    place_ref,
    pixels_ref,
    table_ref,
    pos_ref,
    w_patch_ref,
    w_a_ref,
    w_b_ref,
    gain_ref,
    bias_ref,
    embedded_ref,
    normed_ref,
    first_ref,
    act_ref,
    slope_ref,
    ids_ref,
    slots_ref,
    codes_all,
    ranks,
    earlier,
    held,
    packed,
    landed,
    fetched,
    mixed,
    local_sem,
    ask_send,
    ask_got,
    send,
    got,
):
    owners, capacity, width = packed.shape
    length = codes_ref.shape[1]
    table_rows = held.shape[0]
    emb = lax.axis_index("emb")
    bring = pltpu.make_async_copy(table_ref, held, local_sem.at[0])
    bring.start()
    barrier = pltpu.get_barrier_semaphore()
    for step in range(1, owners):
        other = lax.rem(emb + step, owners)
        pl.semaphore_signal(barrier, inc=1, device_id={"emb": other}, device_id_type=MESH)
    pl.semaphore_wait(barrier, owners - 1)

    def ask(step):
        return pltpu.make_async_remote_copy(
            src_ref=codes_ref,
            dst_ref=codes_all.at[step],
            send_sem=ask_send.at[step - 1],
            recv_sem=ask_got.at[step - 1],
            device_id={"emb": lax.rem(emb + step, owners)},
            device_id_type=MESH,
        )

    def give(step):
        return pltpu.make_async_remote_copy(
            src_ref=packed.at[step],
            dst_ref=landed.at[step - 1],
            send_sem=send.at[step - 1],
            recv_sem=got.at[step - 1],
            device_id={"emb": lax.rem(emb - step + owners, owners)},
            device_id_type=MESH,
        )

    for step in range(1, owners):
        ask(step).start()
    codes_all[0] = codes_ref[...]
    block = min(256, length)

    def triangle(number, carry):
        base = pl.multiple_of(number * block, block)
        above = base + lax.broadcasted_iota(jnp.int32, (block, length), 0)
        below = lax.broadcasted_iota(jnp.int32, (block, length), 1)
        earlier[pl.ds(base, block), :] = jnp.where(above < below, 1.0, 0.0).astype(jnp.bfloat16)
        return carry

    lax.fori_loop(0, length // block, triangle, 0)
    codes = codes_ref[...]
    mine = [
        (codes >= owner * table_rows) & (codes < (owner + 1) * table_rows)
        for owner in range(owners)
    ]
    marks = jnp.concatenate([jnp.where(mark, 1.0, 0.0) for mark in mine], 0)
    places = product(marks.astype(jnp.bfloat16), earlier[...])
    slots = jnp.full((1, length), owners * capacity, jnp.int32)
    for owner in range(owners):
        rank = places[owner : owner + 1].astype(jnp.int32)
        slots = jnp.where(mine[owner], owner * capacity + rank, slots)
    slots_ref[...] = slots
    for step in range(1, owners):
        ask(step).wait()
    local = codes_all[...].reshape(owners, length) - emb * table_rows
    inside = (local >= 0) & (local < table_rows)
    places = product(jnp.where(inside, 1.0, 0.0).astype(jnp.bfloat16), earlier[...])
    ranks[...] = jnp.where(inside, places.astype(jnp.int32), -1).reshape(owners, 1, length)
    bring.wait()

    def gather(step):
        rank = ranks[step]
        local = codes_all[step] - emb * table_rows + 1
        slot = lax.broadcasted_iota(jnp.int32, (capacity, length), 0)
        match = slot == rank
        hot = jnp.where(match, 1.0, 0.0).astype(jnp.bfloat16)
        coarse = lax.div(local, 64)
        fine = local - coarse * 64
        inner = rank >= 0
        pair = jnp.concatenate(
            [jnp.where(inner, coarse, 0), jnp.where(inner, fine, 0)]
            + [jnp.zeros((6, length), jnp.int32)],
            0,
        )
        pair = product_right(pair.astype(jnp.float32).astype(jnp.bfloat16), hot)
        source = lax.rem(emb - step + owners, owners)
        ids_ref[source] = (pair[0:1] * 64.0 + pair[1:2]).astype(jnp.int32) - 1
        wanted = jnp.sum(jnp.where(match, local, 0), 1, keepdims=True) - 1
        total = jnp.zeros((capacity, width), jnp.float32)
        for start in range(0, table_rows, 1024):
            size = min(1024, table_rows - start)
            row = start + lax.broadcasted_iota(jnp.int32, (capacity, size), 1)
            hot = jnp.where(row == wanted, 1.0, 0.0).astype(jnp.bfloat16)
            total = total + product(hot, held[start : start + size, :])
        packed[step] = total.astype(jnp.bfloat16)

    def serve(step, carry):
        gather(step)
        give(step).start()
        return carry

    lax.fori_loop(1, owners, serve, 0)
    gather(0)
    slot_column = column_of(slots, length)
    fetched[...] = jnp.zeros_like(fetched)

    def place_rows(step):
        owner = lax.rem(emb + step, owners)
        rows = packed[0] if step == 0 else landed[step - 1]
        for start in range(0, length, block):
            slot = owner * capacity + lax.broadcasted_iota(jnp.int32, (block, capacity), 1)
            hot = jnp.where(slot == slot_column[start : start + block], 1.0, 0.0)
            fetched[start : start + block, :] += product(hot.astype(jnp.bfloat16), rows)


    def patches(number, carry):
        base = pl.multiple_of(number * block, block)
        rows = pl.ds(base, block)
        first = product(pixels_ref[rows, :], w_patch_ref[...])
        low = first.astype(jnp.bfloat16)
        first_ref[rows, :] = low
        act, slope = gelu_pair(product(low, w_a_ref[...]))
        act = act.astype(jnp.bfloat16)
        act_ref[rows, :] = act
        slope_ref[rows, :] = slope.astype(jnp.bfloat16)
        mixed[rows, :] = first + product(act, w_b_ref[...])
        return carry

    lax.fori_loop(0, length // block, patches, 0)

    def positions(number, carry):
        base = pl.multiple_of(number * block, block)
        spot = lax.broadcasted_iota(jnp.int32, (block, pos_ref.shape[0]), 1)
        place = column_of(place_ref[:, pl.ds(base, block)], block)
        hot = jnp.where(spot == place, 1.0, 0.0).astype(jnp.bfloat16)
        embedded_ref[pl.ds(base, block), :] = product(hot, pos_ref[...])
        return carry

    lax.fori_loop(0, length // block, positions, 0)
    place_rows(0)
    for step in range(1, owners):
        give(step).wait()
        place_rows(step)

    def settle(number, carry):
        base = pl.multiple_of(number * block, block)
        rows = pl.ds(base, block)
        token = base + lax.broadcasted_iota(jnp.int32, (block, width), 0)
        image = mixed[rows, :] + embedded_ref[rows, :]
        value = jnp.where(token < counts_ref[0, 0], image, fetched[rows, :])
        embedded_ref[rows, :] = value
        normed = normalize(value) * gain_ref[...] + bias_ref[...]
        normed_ref[rows, :] = normed.astype(jnp.bfloat16)
        return carry

    lax.fori_loop(0, length // block, settle, 0)


def front(counts, codes, place, pixels, table, pos, w_patch, w_a, w_b, gain, bias, capacity):
    owners = lax.axis_size("emb")
    length, width = pixels.shape
    vmem = pl.BlockSpec(memory_space=pltpu.VMEM)
    low = jax.ShapeDtypeStruct((length, width), jnp.bfloat16)
    full = jax.ShapeDtypeStruct((length, width), jnp.float32)
    return pl.pallas_call(
        front_kernel,
        in_specs=[pl.BlockSpec(memory_space=pltpu.SMEM), vmem, vmem, vmem]
        + [pl.BlockSpec(memory_space=pl.ANY)]
        + [vmem] * 6,
        out_specs=[vmem] * 7,
        out_shape=[
            full,
            low,
            low,
            low,
            low,
            jax.ShapeDtypeStruct((owners, 1, capacity), jnp.int32),
            jax.ShapeDtypeStruct((1, length), jnp.int32),
        ],
        scratch_shapes=[
            pltpu.VMEM((owners, 1, length), jnp.int32),
            pltpu.VMEM((owners, 1, length), jnp.int32),
            pltpu.VMEM((length, length), jnp.bfloat16),
            pltpu.VMEM(table.shape, jnp.bfloat16),
            pltpu.VMEM((owners, capacity, width), jnp.bfloat16),
            pltpu.VMEM((owners - 1, capacity, width), jnp.bfloat16),
            pltpu.VMEM((length, width), jnp.float32),
            pltpu.VMEM((length, width), jnp.float32),
            pltpu.SemaphoreType.DMA((1,)),
            pltpu.SemaphoreType.DMA((owners - 1,)),
            pltpu.SemaphoreType.DMA((owners - 1,)),
            pltpu.SemaphoreType.DMA((owners - 1,)),
            pltpu.SemaphoreType.DMA((owners - 1,)),
        ],
        compiler_params=pltpu.CompilerParams(
            collective_id=1, has_side_effects=True, vmem_limit_bytes=56 << 20
        ),
        name="front",
    )(counts, codes, place, pixels, table, pos, w_patch, w_a, w_b, gain, bias)


def feed_kernel(
    attended_ref,
    embedded_ref,
    cotangent_ref,
    w_o_ref,
    gain_ref,
    bias_ref,
    w_up_ref,
    w_down_ref,
    output_ref,
    grad_middle_ref,
    grad_up_ref,
    grad_attended_ref,
    grad_w_o_ref,
    gains_ref,
    part_ref,
    middle,
    normed,
    back,
    slopes,
    hidden,
    pack,
    *refs,
):
    (share,) = shares_of([pack], [None], refs)
    groups, length, chunk = slopes.shape
    bits = share.bits
    owners = 1 << bits
    width = middle.shape[1]
    step = pl.program_id(0)
    block = min(512, length)
    blocks = length // block

    @pl.when(step == 0)
    def begin():
        greet(False, ring=False)

        def one(number, carry):
            rows = pl.ds(pl.multiple_of(number * block, block), block)
            value = embedded_ref[rows, :] + product_left(attended_ref[:, rows], w_o_ref[...])
            middle[rows, :] = value
            normed[rows, :] = (normalize(value) * gain_ref[...] + bias_ref[...]).astype(
                jnp.bfloat16
            )
            return carry

        lax.fori_loop(0, blocks, one, 0)

    @pl.when(step < groups)
    def go_forward():
        def one(number, carry):
            rows = pl.ds(pl.multiple_of(number * block, block), block)
            act, slope = gelu_pair(product(normed[rows, :], w_up_ref[...]))
            act = act.astype(jnp.bfloat16)
            hidden[rows, :] = act
            slopes[step, rows, :] = slope.astype(jnp.bfloat16)
            grown = product(act, w_down_ref[...])

            @pl.when(step == 0)
            def first():
                grad_middle_ref[rows, :] = middle[rows, :] + grown

            @pl.when(step > 0)
            def other():
                grad_middle_ref[rows, :] = grad_middle_ref[rows, :] + grown

            return carry

        lax.fori_loop(0, blocks, one, 0)
        units = chunk // owners
        spare = pack.shape[-2] - units
        part = 384 if chunk % 384 == 0 and 384 % units == 0 else chunk
        for start in range(0, chunk, part):
            grads = product_left(hidden[:, start : start + part], cotangent_ref[...])
            for place in range(part // units):
                piece = grads[place * units : (place + 1) * units]
                if spare:
                    piece = jnp.concatenate([piece, jnp.zeros((spare, width), jnp.float32)], 0)
                owner = start // units + place
                index = tuple((owner >> bit) & 1 for bit in range(bits - 1, -1, -1))
                pack[(step,) + index] = piece.astype(jnp.bfloat16)

    @pl.when(step == groups - 1)
    def turn():
        output_ref[...] = grad_middle_ref[...].astype(jnp.bfloat16)
        share.start()

    @pl.when(step == groups + 1)
    def swap():
        share.take(0)

    @pl.when(step >= groups)
    def go_back():
        def one(number, carry):
            rows = pl.ds(pl.multiple_of(number * block, block), block)
            slope = slopes[step - groups, rows, :].astype(jnp.float32)
            grads = product_right(cotangent_ref[rows, :], w_down_ref[...]) * slope
            grads = grads.astype(jnp.bfloat16)
            hidden[rows, :] = grads
            lower = product_right(grads, w_up_ref[...])

            @pl.when(step == groups)
            def first():
                back[rows, :] = lower

            @pl.when(step > groups)
            def other():
                back[rows, :] = back[rows, :] + lower

            return carry

        lax.fori_loop(0, blocks, one, 0)
        for start in range(0, width, 768):
            span = slice(start, start + 768)
            grad_up_ref[0, span, :] = product_left(normed[:, span], hidden[...]).astype(
                jnp.bfloat16
            )

    @pl.when(step == 2 * groups - 1)
    def end():
        share.take(1)
        gains_ref[...] = jnp.zeros_like(gains_ref)

        def one(number, carry):
            rows = pl.ds(pl.multiple_of(number * block, block), block)
            value = middle[rows, :]
            centred = value - jnp.mean(value, -1, keepdims=True)
            scale = lax.rsqrt(jnp.mean(centred * centred, -1, keepdims=True) + 1e-05)
            unit = centred * scale
            grads = back[rows, :]
            gains_ref[0:1, :] += jnp.sum(grads * unit, 0, keepdims=True)
            gains_ref[1:2, :] += jnp.sum(grads, 0, keepdims=True)
            grads = grads * gain_ref[...]
            along = jnp.mean(grads * unit, -1, keepdims=True)
            grads = scale * (grads - jnp.mean(grads, -1, keepdims=True) - unit * along)
            grads = cotangent_ref[rows, :].astype(jnp.float32) + grads
            grad_middle_ref[rows, :] = grads
            normed[rows, :] = grads.astype(jnp.bfloat16)
            return carry

        lax.fori_loop(0, blocks, one, 0)
        for start in range(0, width, 256):
            span = slice(start, start + 256)
            grad_w_o_ref[span, :] = product(attended_ref[span, :], normed[...]).astype(
                jnp.bfloat16
            )
            grad_attended_ref[span, :] = product_right(w_o_ref[span, :], normed[...]).astype(
                jnp.bfloat16
            )
        for stage in range(2, bits):
            share.take(stage)
        share.export(part_ref)


def feed(attended, embedded, cotangent, w_o, gain, bias, w_up, w_down):
    groups, owners = lax.axis_size("dp"), lax.axis_size("emb")
    length, width = embedded.shape
    chunk = w_up.shape[1] // groups
    units = chunk // owners
    units = max(32, units + -units % 16)
    shape = (groups,) + (2,) * (owners.bit_length() - 1) + (units, width)
    once = pl.Buffered(1)

    def whole(array):
        return pl.BlockSpec(array.shape, lambda s: (0, 0), pipeline_mode=once)

    outs = [
        jax.ShapeDtypeStruct((length, width), jnp.bfloat16),
        jax.ShapeDtypeStruct((length, width), jnp.float32),
        jax.ShapeDtypeStruct((groups, width, chunk), jnp.bfloat16),
        jax.ShapeDtypeStruct((width, length), jnp.bfloat16),
        jax.ShapeDtypeStruct((width, width), jnp.bfloat16),
        jax.ShapeDtypeStruct((8, width), jnp.float32),
        jax.ShapeDtypeStruct((groups, units, width), jnp.bfloat16),
    ]
    out_specs = [whole(out) if len(out.shape) == 2 else None for out in outs]
    out_specs[2] = pl.BlockSpec((1, width, chunk), lambda s: (jnp.maximum(s - groups, 0), 0, 0))
    out_specs[6] = pl.BlockSpec(outs[6].shape, lambda s: (0, 0, 0), pipeline_mode=once)
    return pl.pallas_call(
        feed_kernel,
        grid=(2 * groups,),
        in_specs=[
            whole(attended),
            whole(embedded),
            whole(cotangent),
            whole(w_o),
            whole(gain),
            whole(bias),
            pl.BlockSpec((width, chunk), lambda s: (0, lax.rem(s, groups))),
            pl.BlockSpec((chunk, width), lambda s: (lax.rem(s, groups), 0)),
        ],
        out_specs=out_specs,
        out_shape=outs,
        scratch_shapes=[
            pltpu.VMEM((length, width), jnp.float32),
            pltpu.VMEM((length, width), jnp.bfloat16),
            pltpu.VMEM((length, width), jnp.float32),
            pltpu.VMEM((groups, length, chunk), jnp.bfloat16),
            pltpu.VMEM((length, chunk), jnp.bfloat16),
            pltpu.VMEM(shape, jnp.bfloat16),
        ]
        + shares_scratch(shape),
        compiler_params=pltpu.CompilerParams(
            collective_id=4, has_side_effects=True, vmem_limit_bytes=58 << 20
        ),
        name="feed",
    )(attended, embedded, cotangent, w_o, gain, bias, w_up, w_down)


def first_kernel(
    heads_ref,
    w_q_ref,
    w_k_ref,
    w_v_ref,
    embedded_ref,
    middle_ref,
    normed_ref,
    gain_ref,
    grad_ref,
    turned_ref,
    weights_ref,
    gains_ref,
    back,
    normed_turned,
):
    length, width = embedded_ref.shape
    block = min(512, length)
    gains_ref[...] = jnp.zeros_like(gains_ref)

    def rows_back(number, carry):
        base = pl.multiple_of(number * block, block)
        rows = pl.ds(base, block)
        back[...] = product(w_q_ref[...], heads_ref[0:width, rows])
        back[...] += product(w_k_ref[...], heads_ref[width : 2 * width, rows])
        back[...] += product(w_v_ref[...], heads_ref[2 * width :, rows])
        grads = back[...].T
        value = embedded_ref[rows, :]
        centred = value - jnp.mean(value, -1, keepdims=True)
        scale = lax.rsqrt(jnp.mean(centred * centred, -1, keepdims=True) + 1e-05)
        unit = centred * scale
        gains_ref[0:1, :] += jnp.sum(grads * unit, 0, keepdims=True)
        gains_ref[1:2, :] += jnp.sum(grads, 0, keepdims=True)
        grads = grads * gain_ref[...]
        along = jnp.mean(grads * unit, -1, keepdims=True)
        grads = scale * (grads - jnp.mean(grads, -1, keepdims=True) - unit * along)
        grads = middle_ref[rows, :] + grads
        grad_ref[rows, :] = grads
        turned_ref[:, rows] = grads.T.astype(jnp.bfloat16)
        normed_turned[:, rows] = normed_ref[rows, :].astype(jnp.float32).T.astype(jnp.bfloat16)
        return carry

    lax.fori_loop(0, length // block, rows_back, 0)

    def weights(number, carry):
        base = pl.multiple_of(number * width, width)
        weights_ref[number] = product_right(
            normed_turned[...], heads_ref[pl.ds(base, width), :]
        ).astype(jnp.bfloat16)
        return carry

    lax.fori_loop(0, 3, weights, 0)


def first_backward(heads, w_q, w_k, w_v, embedded, middle, normed, gain):
    length, width = embedded.shape
    vmem = pl.BlockSpec(memory_space=pltpu.VMEM)
    return pl.pallas_call(
        first_kernel,
        in_specs=[vmem] * 8,
        out_specs=[vmem] * 4,
        out_shape=[
            jax.ShapeDtypeStruct((length, width), jnp.float32),
            jax.ShapeDtypeStruct((width, length), jnp.bfloat16),
            jax.ShapeDtypeStruct((3, width, width), jnp.bfloat16),
            jax.ShapeDtypeStruct((8, width), jnp.float32),
        ],
        scratch_shapes=[
            pltpu.VMEM((width, min(512, length)), jnp.float32),
            pltpu.VMEM((width, length), jnp.bfloat16),
        ],
        compiler_params=pltpu.CompilerParams(vmem_limit_bytes=56 << 20),
        name="first_backward",
    )(heads, w_q, w_k, w_v, embedded, middle, normed, gain)


def on_device(
    pixels,
    counts,
    token_ids,
    action_bins,
    patch_pos,
    token_table,
    pos_table,
    w_patch,
    w_res_a,
    w_res_b,
    gain_one,
    bias_one,
    w_q,
    w_k,
    w_v,
    w_o,
    gain_two,
    bias_two,
    w_up,
    w_down,
    cotangent,
):
    length = pixels.shape[0]
    model_width = w_q.shape[0]
    positions = jnp.arange(length)
    image_rows = positions < counts[0, 0]
    action_rows = positions >= length - counts[0, 1]
    table_rows = jnp.logical_not(image_rows)
    row_ids = jnp.where(action_rows, TEXT_VOCAB + action_bins, token_ids)
    rows_owned = token_table.shape[0]
    owners_total = lax.axis_size("emb")
    capacity = 3 * length // (2 * owners_total)
    groups = lax.axis_size("dp")
    codes = jnp.where(table_rows, row_ids, -1).reshape(1, length)
    gain_row = gain_one.astype(jnp.float32).reshape(1, model_width)
    bias_row = bias_one.astype(jnp.float32).reshape(1, model_width)
    embedded, normed_one, first_low, res_act, res_slope, ids, slots = front(
        counts,
        codes,
        patch_pos.reshape(1, length),
        pixels,
        token_table,
        pos_table,
        w_patch,
        w_res_a,
        w_res_b,
        gain_row,
        bias_row,
        capacity,
    )
    facts = jnp.concatenate([ids.reshape(1, -1), slots], 1)
    queries = contract(w_q, normed_one, 0, 1).astype(jnp.bfloat16)
    key_heads = contract(w_k, normed_one, 0, 1).astype(jnp.bfloat16)
    value_heads = contract(w_v, normed_one, 0, 1).astype(jnp.bfloat16)
    attended, probs, inverse = attention_forward(queries, key_heads, value_heads)
    output, grad_middle, grad_w_up, grad_attended, grad_w_o, gains, part_down = feed(
        attended,
        embedded,
        cotangent,
        w_o,
        gain_two.astype(jnp.float32).reshape(1, model_width),
        bias_two.astype(jnp.float32).reshape(1, model_width),
        w_up,
        w_down,
    )
    devices = groups * owners_total
    share = model_width // devices
    folds = w_up.shape[1] // model_width
    per_fold = groups // folds
    folded = []
    for n in range(folds):
        pieces = [grad_w_up[n * per_fold + m] for m in range(per_fold)]
        folded.append(rows_of(jnp.concatenate(pieces, 1) if per_fold > 1 else pieces[0]))
    grad_heads, share_one, share_two, share_down, ring = attention_backward(
        queries,
        key_heads,
        value_heads,
        attended,
        grad_attended,
        probs,
        inverse,
        [
            stacked(folded[:2] + [rows_of(grad_w_o), vector_rows(gains)]),
            stacked(folded[2:]),
        ],
        part_down,
        facts,
    )
    ring = ring.reshape(groups, -1)
    ring_ids = ring[:, : owners_total * capacity].reshape(groups, owners_total, capacity)
    ring_ids = jnp.swapaxes(ring_ids, 0, 1).reshape(owners_total, 1, groups * capacity)
    ring_slots = ring[:, owners_total * capacity :].reshape(groups, 1, length)
    grad_heads = grad_heads.reshape(3 * model_width, length)
    grad_embedded, grads_turned, grad_w_heads, gains = first_backward(
        grad_heads, w_q, w_k, w_v, embedded, grad_middle, normed_one, gain_row
    )
    gains_one = vector_rows(gains)
    grad_w_heads = [rows_of(grad_w_heads[n]) for n in range(3)]
    columns = model_width // groups
    grads_turned = grads_turned.reshape(groups, columns, length)
    pos_rows = pos_table.shape[0]
    pos_share = pos_rows // devices
    pack_heads = stacked(grad_w_heads + [gains_one])
    if share % 8 == 0 and 384 % share == 0 and pos_share % 8 == 0:
        grad_table, share_heads, share_res, grad_first = tail(
            grads_turned,
            ring_slots,
            ring_ids,
            pack_heads,
            [
                counts,
                grad_embedded,
                patch_pos.reshape(1, length),
                pixels,
                first_low,
                res_act,
                res_slope,
                w_res_a,
                w_res_b,
            ],
            rows_owned,
            capacity,
            pos_rows,
        )
    else:
        grad_image = jnp.where(image_rows[:, None], grad_embedded, 0.0)
        grad_mixed = grad_image.astype(jnp.bfloat16)
        position_hot = patch_pos[:, None] == jnp.arange(pos_rows)[None, :]
        grad_pos_table = product_left(position_hot.astype(jnp.bfloat16), grad_mixed)
        grad_w_res_b = product_left(res_act, grad_mixed)
        grad_inner = product_right(grad_mixed, w_res_b) * res_slope.astype(jnp.float32)
        grad_inner = grad_inner.astype(jnp.bfloat16)
        grad_w_res_a = product_left(first_low, grad_inner)
        grad_first = (grad_image + product_right(grad_inner, w_res_a)).astype(jnp.bfloat16)
        grad_w_patch = product_left(pixels, grad_first)
        res_rows = [rows_of(g) for g in (grad_w_patch, grad_w_res_a, grad_w_res_b, grad_pos_table)]
        grad_table, share_heads, share_res = tail(
            grads_turned,
            ring_slots,
            ring_ids,
            pack_heads,
            [stacked(res_rows)],
            rows_owned,
            capacity,
            0,
        )
    grad_pixels = product_right(grad_first, w_patch)

    def cut(array, place):
        return array[place * share : (place + 1) * share]

    rows_up = jnp.concatenate([share_one[: 2 * share], share_two[: (folds - 2) * share]], 0)
    share_w_up = jnp.swapaxes(rows_up.reshape(folds, share, model_width), 0, 1)
    place = (lax.axis_index("dp") * owners_total + lax.axis_index("emb")) * share
    gains_two = lax.dynamic_slice(share_one[3 * share : 3 * share + 2], (0, place), (2, share))
    gains_one = lax.dynamic_slice(share_heads[3 * share : 3 * share + 2], (0, place), (2, share))
    return (
        output,
        grad_pixels,
        grad_table,
        share_res[3 * share : 3 * share + pos_share],
        cut(share_res, 0),
        cut(share_res, 1),
        cut(share_res, 2),
        gains_one[0],
        gains_one[1],
        cut(share_heads, 0),
        cut(share_heads, 1),
        cut(share_heads, 2),
        cut(share_one, 2),
        gains_two[0],
        gains_two[1],
        share_w_up.reshape(share, folds * model_width),
        share_down[: w_down.shape[0] // devices],
    )


def solution(mesh):
    in_specs = (
        P(("dp", "emb"), None),
        P(("dp", "emb"), None),
        P(("dp", "emb")),
        P(("dp", "emb")),
        P(("dp", "emb")),
        P("emb", None),
        P(),
        P(),
        P(),
        P(),
        P(),
        P(),
        P(),
        P(),
        P(),
        P(),
        P(),
        P(),
        P(),
        P(),
        P(("dp", "emb"), None),
    )
    out_specs = (
        P(("dp", "emb"), None),
        P(("dp", "emb"), None),
        P("emb", "dp"),
        P(("dp", "emb"), None),
        P(("dp", "emb"), None),
        P(("dp", "emb"), None),
        P(("dp", "emb"), None),
        P(("dp", "emb")),
        P(("dp", "emb")),
        P(("dp", "emb"), None),
        P(("dp", "emb"), None),
        P(("dp", "emb"), None),
        P(("dp", "emb"), None),
        P(("dp", "emb")),
        P(("dp", "emb")),
        P(("dp", "emb"), None),
        P(("dp", "emb"), None),
    )
    return jax.shard_map(
        on_device, mesh=mesh, in_specs=in_specs, out_specs=out_specs, check_vma=False
    )
```
